32 devices in a mesh: dp: 8 (over z, y), expert: 2 (over core), shard: 2 (over x).
Axes of the slice: x: 2, y: 2, z: 4, core: 2. Of those that a mesh axis runs over, the one named last changes fastest.
Arguments:
- tokens: bfloat16 [2, 1024, 2048], P('expert', 'dp'), may hold values from -6 to 6
- cotangent: bfloat16 [2, 1024, 2048], P('expert', 'dp'), may hold values from -6 to 6
- attn_gain: float32 [2048], replicated, may hold values from 0.5 to 1.5
- mlp_gain: float32 [2048], replicated, may hold values from 0.5 to 1.5
- key_weight: bfloat16 [2048, 2048], P(None, 'shard'), may hold values from -0.125 to 0.125
- value_weight: bfloat16 [2048, 2048], P(None, 'shard'), may hold values from -0.125 to 0.125
- query_weight: bfloat16 [2048, 16384], P(None, ('dp', 'expert', 'shard')), may hold values from -0.125 to 0.125
- output_weight: bfloat16 [2048, 16384], P(None, ('dp', 'expert', 'shard')), may hold values from -1.5 to 1.5
- attn_router: bfloat16 [2048, 8], replicated, may hold values from -0.09375 to 0.09375
- gate_weight: bfloat16 [2048, 45056], P(None, ('dp', 'expert', 'shard')), may hold values from -0.125 to 0.125
- up_weight: bfloat16 [2048, 45056], P(None, ('dp', 'expert', 'shard')), may hold values from -0.125 to 0.125
- down_weight: bfloat16 [2048, 45056], P(None, ('dp', 'expert', 'shard')), may hold values from -0.15625 to 0.15625
- mlp_router: bfloat16 [2048, 8], replicated, may hold values from -0.09375 to 0.09375
- segment_ids: int32 [2, 1024], P('expert'), may hold values from 0 to 12, as said below
- parent_ids: int32 [2, 13], P('expert'), may hold values from 0 to 11, as said below
- attn_routes: int32 [2, 1024, 2], P('expert', 'dp'), may hold values from 0 to 7, all different within a row; in each aligned block of 128 rows (0 to 127, 128 to 255, ..., all dimensions but the last counted through in order) at most 40 rows name the same one
- mlp_routes: int32 [2, 1024, 2], P('expert', 'dp'), may hold values from 0 to 7, all different within a row
- slot_order: int32 [2, 8, 256], P('expert', 'dp'), may hold values from 0 to 255, each once within a row
Outputs:
- layer_out: bfloat16 [2, 1024, 2048], P('expert', 'dp')
- tokens_grad: float32 [2, 1024, 2048], P('expert', 'dp')
- attn_gain_grad: float32 [2048], P(('dp', 'expert'))
- mlp_gain_grad: float32 [2048], P(('dp', 'expert'))
- key_grad: float32 [2048, 2048], P(('dp', 'expert'), 'shard')
- value_grad: float32 [2048, 2048], P(('dp', 'expert'), 'shard')
- query_grad: float32 [2048, 16384], P(None, ('dp', 'expert', 'shard'))
- output_grad: float32 [2048, 16384], P(None, ('dp', 'expert', 'shard'))
- attn_router_grad: float32 [2048, 8], P(('dp', 'expert'))
- gate_grad: float32 [2048, 45056], P(None, ('dp', 'expert', 'shard'))
- up_grad: float32 [2048, 45056], P(None, ('dp', 'expert', 'shard'))
- down_grad: float32 [2048, 45056], P(None, ('dp', 'expert', 'shard'))
- mlp_router_grad: float32 [2048, 8], P(('dp', 'expert'))
The draws below stay inside these ranges and needn't reach their ends.
Inputs may be any that keep to these rules, and one draw needn't show every extreme that they name: `segment_ids`: along a tree the segment number never falls, segment 0 comes first, and every segment holds at least one token. parent_ids[t, 0] = 0; for s >= 1, parent_ids[t, s] is 0 or a segment r with 1 <= r < s and parent_ids[t, r] = 0. `attn_routes`: A token's 2 attention experts differ. In each block of 128 tokens of a tree no attention expert is named by more than 40 pairs, and in every draw some expert is named by exactly 40 pairs in some block. `mlp_routes`: A token's 2 feed-forward experts differ. `slot_order`: each row holds every pair number of the block once.
All inputs are finite; a program needn't handle non-finite values.
Results may differ from the reference program's by a relative error of at most 0.019.
Values may be sent and summed in bfloat16 or wider, within the bound.
No kernel may reach another device: no remote copies, remote signals or barrier semaphores. Data moves between devices by JAX's collectives and lax.ppermute only.
A program may use at most 384 MiB of HBM per device.

```python
import math
import jax
import jax.numpy as jnp
import numpy as np
from jax import lax

D = 2048
HEADS = 16
HEAD = 128
FF = 5632
EXPERTS = 8
TOP = 2
SEGS = 13
TOK_DEV = 128
TREES = 2
TREE_LEN = 1024
CAP = 40
N_DP = 8


def draw_segment_ids(key, part):
    key = jax.random.fold_in(key, 11)
    trunk_key, score_key = jax.random.split(key)
    trunk_end = jax.random.randint(trunk_key, (TREES,), TREE_LEN // 4, TREE_LEN // 2 + 1)
    positions = jnp.arange(TREE_LEN)
    noise = jax.random.randint(score_key, (TREES, TREE_LEN), 0, 1 << 16)
    scores = jnp.where(positions[None, :] > trunk_end[:, None], noise * TREE_LEN + positions[None, :], -1)
    bounds = lax.top_k(scores, SEGS - 2)[0] % TREE_LEN
    counted = (positions[None, :] >= trunk_end[:, None]).astype(jnp.int32)
    counted = counted + jnp.sum((positions[None, None, :] >= bounds[:, :, None]).astype(jnp.int32), axis=1)
    return counted.astype(jnp.int32)


def draw_parent_ids(key, part):
    key = jax.random.fold_in(key, 23)
    branch = jax.random.randint(key, (TREES, SEGS), 0, 2)
    indices = jnp.arange(SEGS)
    branch = jnp.where(indices[None, :] <= 1, 1, branch)
    branch = jnp.where(indices[None, :] == SEGS - 2, 1, branch)
    branch = jnp.where(indices[None, :] == SEGS - 1, 0, branch)
    marked = jnp.where(branch == 1, indices[None, :], 0)
    latest = lax.cummax(marked, axis=1)
    earlier = jnp.concatenate([jnp.zeros((TREES, 1), jnp.int32), latest[:, :-1].astype(jnp.int32)], axis=1)
    parents = jnp.where(branch == 1, 0, earlier)
    return parents.astype(jnp.int32)


def steps_of(rng, shape, cuts, low, top_value):
    def one(dim, shards_of):
        steps = jax.random.uniform(jax.random.fold_in(jax.random.fold_in(rng, 6), dim), (shards_of,), jnp.float32, low / len(cuts), top_value / len(cuts))
        return jnp.repeat(jnp.exp(steps), shape[dim] // shards_of).reshape((-1,) + (1,) * (len(shape) - dim - 1))

    loudness = one(*cuts[0])
    for cut in cuts[1:]:
        loudness = loudness * one(*cut)
    return loudness


def different_ones(key, rows, amount, top, lift):
    sequence = jax.random.permutation(jax.random.fold_in(key, 1), amount)
    boost = sequence
    for power in range(3):
        boost = boost * boost // amount
    boost = boost * lift // amount
    chance = jax.random.randint(jax.random.fold_in(key, 2), (rows, amount), 0, 4096) + boost
    fixed_rows = jax.random.permutation(jax.random.fold_in(key, 3), rows)[jnp.arange(amount) % rows]
    chance = jnp.where(jnp.arange(rows)[:, None] == fixed_rows[None, :], 1 << 14, chance)
    merit = chance * amount + jnp.arange(amount)
    return lax.top_k(merit.astype(jnp.int32), top)[1].astype(jnp.int32)


def shared_out(stream_key, own, number, rows, count, top, limit, lean):
    order = jax.random.permutation(stream_key, count)
    heavy_load, ordinary = load_shares(count, rows * top, limit, lean, True), load_shares(count, rows * top, limit, lean, False)
    places = jnp.arange(count)

    def named(tallies, rotation):
        used = int((tallies > 0).sum())
        fixed = max(1, used // 4)
        moved = fixed + (places - fixed + rotation * (used - fixed)) % max(1, count - fixed)
        return jnp.zeros((count,), jnp.int32).at[order[jnp.where(places < fixed, places, moved)]].set(jnp.asarray(tallies, jnp.int32))

    tallies = jnp.where(number % 4 == 0, named(heavy_load, number // 4), named(ordinary, number - number // 4 - 1))
    mixed = jax.random.permutation(jax.random.fold_in(own, 3), count)
    giver, taker = mixed[0:count // 2 * 2:2], mixed[1:count // 2 * 2:2]
    room = jnp.minimum(tallies[giver] - 1, limit - tallies[taker]) // 2
    room = jnp.where((giver == order[0]) | (taker == order[0]) | (tallies[taker] == 0), 0, jnp.maximum(room, 0))
    moved = jax.random.randint(jax.random.fold_in(own, 4), (count // 2,), 0, 1 << 20) % (room + 1)
    tallies = tallies.at[giver].add(-moved).at[taker].add(moved)
    items = jnp.searchsorted(jnp.cumsum(tallies), jnp.arange(rows * top), side="right").astype(jnp.int32)
    listing = items.reshape(top, rows).T
    listing = listing[jax.random.permutation(jax.random.fold_in(own, 1), rows)]
    rotation = jax.random.randint(jax.random.fold_in(own, 2), (rows, 1), 0, top)
    return jnp.take_along_axis(listing, (jnp.arange(top)[None, :] + rotation) % top, axis=1)


def load_shares(number_of, total, reach, skew, full):
    weights = [(1 << 20) // math.isqrt(rank ** skew) + 1 for rank in range(1, number_of + 1)]
    largest = reach if full else min(reach, max(-(-total // number_of), total * weights[0] // sum(weights)))
    least = 1 if total - largest >= number_of - 1 else 0
    given, surplus = [largest] + [least] * (number_of - 1), total - largest - least * (number_of - 1)
    while surplus > 0:
        free = [i for i in range(1, number_of) if given[i] < largest] or [i for i in range(1, number_of) if given[i] < reach]
        mass, remaining = sum([weights[i] for i in free]), surplus
        for i in free:
            addition = min(reach - given[i], max(1, remaining * weights[i] // mass), surplus)
            given[i] = given[i] + addition
            surplus = surplus - addition
    return np.array(given)


def centred(own_key, dims, deviation, limit, shards=(), dtype=jnp.bfloat16):
    gain = steps_of(own_key, dims, shards, -0.22, 0.18) if shards else 1.0
    array = jax.random.normal(own_key, dims, jnp.float32) * deviation * gain
    return jnp.minimum(jnp.maximum(array, -limit), limit).astype(dtype)


def setup_inputs(seed: int = 0) -> dict:
    arg_keys = jax.random.split(jax.random.key(seed), 19)
    tokens = centred(arg_keys[0], (TREES, TREE_LEN, D), 1.0, 6.0, ((0, 2), (1, 8)))
    cotangent = centred(arg_keys[1], (TREES, TREE_LEN, D), 1.0, 6.0, ((0, 2), (1, 8)))
    attn_gain = jnp.clip(1.0 + 0.1 * jax.random.normal(arg_keys[2], (D,), jnp.float32), 0.5, 1.5)
    mlp_gain = jnp.clip(1.0 + 0.1 * jax.random.normal(arg_keys[3], (D,), jnp.float32), 0.5, 1.5)
    key_weight = centred(arg_keys[4], (D, HEADS * HEAD), D ** -0.5, 0.125, ((1, 2),))
    value_weight = centred(arg_keys[5], (D, HEADS * HEAD), D ** -0.5, 0.125, ((1, 2),))
    query_weight = centred(arg_keys[6], (D, EXPERTS * HEADS * HEAD), D ** -0.5, 0.125, ((1, 32),))
    output_weight = centred(arg_keys[7], (D, EXPERTS * HEADS * HEAD), (max(1, HEADS * HEAD // 128)) ** -0.5, 1.5, ((1, 32),))
    attn_router = centred(arg_keys[8], (D, EXPERTS), (2 * D) ** -0.5, 0.09375)
    gate_weight = centred(arg_keys[9], (D, EXPERTS * FF), D ** -0.5, 0.125, ((1, 32),))
    up_weight = centred(arg_keys[10], (D, EXPERTS * FF), D ** -0.5, 0.125, ((1, 32),))
    down_weight = centred(arg_keys[11], (D, EXPERTS * FF), (FF // 4) ** -0.5, 0.15625, ((1, 32),))
    mlp_router = centred(arg_keys[12], (D, EXPERTS), (2 * D) ** -0.5, 0.09375)
    segment_ids = draw_segment_ids(jax.random.fold_in(arg_keys[18], 71), 0)
    parent_ids = draw_parent_ids(jax.random.fold_in(arg_keys[18], 71), 0)
    attn_routes_keys = jax.random.split(jax.random.fold_in(arg_keys[15], 1), TREES * TREE_LEN // TOK_DEV)
    attn_routes_turns = jax.random.permutation(jax.random.fold_in(arg_keys[15], 3), TREES * TREE_LEN // TOK_DEV)
    attn_routes = jax.vmap(lambda own, number: shared_out(jax.random.fold_in(arg_keys[15], 2), own, number, TOK_DEV, EXPERTS, TOP, CAP, 1))(attn_routes_keys, attn_routes_turns).reshape((TREES, TREE_LEN, TOP))
    mlp_routes = different_ones(arg_keys[16], TREES * TREE_LEN, EXPERTS, TOP, 2048).reshape((TREES, TREE_LEN, TOP))
    slot_order = jax.vmap(lambda own: jax.random.permutation(own, TOK_DEV * TOP))(jax.random.split(arg_keys[17], TREES * N_DP)).reshape((TREES, N_DP, TOK_DEV * TOP)).astype(jnp.int32)
    return {"tokens": tokens, "cotangent": cotangent, "attn_gain": attn_gain, "mlp_gain": mlp_gain, "key_weight": key_weight, "value_weight": value_weight, "query_weight": query_weight, "output_weight": output_weight, "attn_router": attn_router, "gate_weight": gate_weight, "up_weight": up_weight, "down_weight": down_weight, "mlp_router": mlp_router, "segment_ids": segment_ids, "parent_ids": parent_ids, "attn_routes": attn_routes, "mlp_routes": mlp_routes, "slot_order": slot_order}


@jax.custom_vjp
def low(v):
    return lax.optimization_barrier(v.astype(jnp.bfloat16)).astype(jnp.float32)

@jax.custom_vjp
def low_back(v):
    return v

def low_keep(v):
    return (low(v), None)

def low_pass(kept, grad):
    return (grad,)

def back_keep(v):
    return (v, None)

def back_low(kept, grad):
    return (low(grad),)
low.defvjp(low_keep, low_pass)
low_back.defvjp(back_keep, back_low)
highest = lax.Precision.HIGHEST
epsilon = 1e-06
negative = -1e+30

def matmul(former, latter):
    return jnp.dot(former, latter, precision=highest, preferred_element_type=jnp.float32)

def rms_scale(values):
    return lax.rsqrt(lax.optimization_barrier(jnp.mean(values * values, axis=-1, keepdims=True)) + epsilon)

def pair_gates(logits, routes):
    onehot = routes[:, :, None] == jnp.arange(EXPERTS)[None, None, :]
    chosen = lax.optimization_barrier(jnp.sum(jnp.where(onehot, logits[:, None, :], 0.0), axis=2))
    return jax.nn.softmax(chosen, axis=1)

def kept_pairs(routes, ranking):
    flat_routes = routes.reshape(N_DP, TOK_DEV * TOP)
    same_expert = flat_routes[:, :, None] == flat_routes[:, None, :]
    earlier = ranking[:, None, :] < ranking[:, :, None]
    slots = lax.optimization_barrier(jnp.sum(jnp.logical_and(same_expert, earlier).astype(jnp.int32), axis=2))
    return (slots < CAP).astype(jnp.float32).reshape(TREE_LEN, TOP)

def tree_attention(queries, keys, values, segments, parents):
    parent_one = parents[segments]
    parent_two = parents[parent_one]
    key_places = jnp.arange(TREE_LEN)
    key_heads = keys.reshape(TREE_LEN, HEADS, HEAD)
    value_heads = values.reshape(TREE_LEN, HEADS, HEAD)

    def attend_block(begin):
        row_block = lax.dynamic_slice_in_dim(queries, begin, TOK_DEV, 0).reshape(TOK_DEV, TOP, HEADS, HEAD)
        positions = begin + jnp.arange(TOK_DEV)
        own_segments = lax.dynamic_slice_in_dim(segments, begin, TOK_DEV)
        own_one = lax.dynamic_slice_in_dim(parent_one, begin, TOK_DEV)
        own_two = lax.dynamic_slice_in_dim(parent_two, begin, TOK_DEV)
        ancestor = (segments[None, :] == own_segments[:, None]) | (segments[None, :] == own_one[:, None]) | (segments[None, :] == own_two[:, None])
        visible = jnp.logical_and(key_places[None, :] <= positions[:, None], ancestor)
        raw_scores = low_back(jnp.einsum('rkhd,jhd->rkhj', row_block, key_heads, precision=highest))
        scores = jnp.where(visible[:, None, None, :], raw_scores * HEAD ** (-0.5), negative)
        probs = jax.nn.softmax(scores, axis=-1)
        mixed = jnp.einsum('rkhj,jhd->rkhd', low(probs), value_heads, precision=highest)
        return low(low_back(mixed)).reshape(TOK_DEV, TOP, HEADS * HEAD)
    starts = (jnp.arange(N_DP) * TOK_DEV).astype(jnp.int32)
    return lax.map(jax.checkpoint(attend_block), starts).reshape(TREE_LEN, TOP, HEADS * HEAD)

def layer(tree_x, attn_gain, mlp_gain, key_weight, value_weight, query_weight, output_weight, attn_router, gate_weight, up_weight, down_weight, mlp_router, segments, parents, attn_routes, mlp_routes, keeping):
    normed = low(tree_x * rms_scale(tree_x) * attn_gain)
    keys = low(low_back(matmul(normed, key_weight)))
    values = low(low_back(matmul(normed, value_weight)))
    attn_gates = pair_gates(low_back(matmul(normed, attn_router)), attn_routes)
    head_width = HEADS * HEAD
    queries = jnp.zeros((TREE_LEN, TOP, head_width), jnp.float32)
    for expert in range(EXPERTS):
        projected = low(low_back(matmul(normed, query_weight[:, expert * head_width:(expert + 1) * head_width])))
        picked = (attn_routes == expert).astype(jnp.float32)
        queries = queries + picked[:, :, None] * projected[:, None, :]
    attended = tree_attention(queries, keys, values, segments, parents)
    attn_mix = jnp.zeros_like(tree_x)
    for expert in range(EXPERTS):
        columns = output_weight[:, expert * head_width:(expert + 1) * head_width]
        terms = low_back(jnp.einsum('lkc,dc->lkd', attended, columns, precision=highest))
        picked = jnp.where(attn_routes == expert, attn_gates, 0.0)
        attn_mix = attn_mix + lax.optimization_barrier(jnp.sum(picked[:, :, None] * terms, axis=1))
    middle = tree_x + attn_mix
    mlp_normed = low(middle * rms_scale(middle) * mlp_gain)
    mlp_gates = pair_gates(low_back(matmul(mlp_normed, mlp_router)), mlp_routes) * keeping
    mlp_mix = jnp.zeros_like(tree_x)
    for expert in range(EXPERTS):
        first = expert * FF
        gate_part = low_back(matmul(mlp_normed, gate_weight[:, first:first + FF]))
        up_part = low_back(matmul(mlp_normed, up_weight[:, first:first + FF]))
        hidden = low(jax.nn.silu(gate_part) * up_part)
        result = low_back(matmul(hidden, down_weight[:, first:first + FF].T))
        picked = jnp.where(mlp_routes == expert, mlp_gates, 0.0)
        mlp_mix = mlp_mix + lax.optimization_barrier(jnp.sum(picked, axis=1))[:, None] * result
    return middle + mlp_mix

def reference(tokens, cotangent, attn_gain, mlp_gain, key_weight, value_weight, query_weight, output_weight, attn_router, gate_weight, up_weight, down_weight, mlp_router, segment_ids, parent_ids, attn_routes, mlp_routes, slot_order):
    params = tuple((element.astype(jnp.float32) for element in (attn_gain, mlp_gain, key_weight, value_weight, query_weight, output_weight, attn_router, gate_weight, up_weight, down_weight, mlp_router)))
    running = tuple((jnp.zeros_like(element) for element in params))
    outputs = []
    input_grads = []
    for tree_index in range(TREES):
        keeping = kept_pairs(mlp_routes[tree_index], slot_order[tree_index])
        segments = segment_ids[tree_index]
        parents = parent_ids[tree_index]
        attn_tree = attn_routes[tree_index]
        mlp_tree = mlp_routes[tree_index]

        def forward(tree_x, *weights):
            return layer(tree_x, *weights, segments, parents, attn_tree, mlp_tree, keeping)
        result, pullback = jax.vjp(forward, tokens[tree_index].astype(jnp.float32), *params)
        gradients = pullback(cotangent[tree_index].astype(jnp.float32))
        outputs.append(result.astype(jnp.bfloat16))
        input_grads.append(gradients[0])
        running = tuple((former + latter for former, latter in zip(running, gradients[1:])))
    return (jnp.stack(outputs), jnp.stack(input_grads), running[0], running[1], running[2], running[3], running[4], running[5], running[6], running[7], running[8], running[9], running[10])
```

```python
import functools

import jax
import jax.numpy as jnp
from jax import lax
from jax.experimental import pallas as pl
from jax.experimental.pallas import tpu as pltpu
from jax.sharding import PartitionSpec as P

HEAD = 128

epsilon = 1e-06
negative = -1e30
scale = HEAD ** (-0.5)
bf16 = jnp.bfloat16
f32 = jnp.float32


def product(former, latter):
    return jnp.dot(former, latter, preferred_element_type=f32)


def product_last(former, latter):
    return lax.dot_general(
        former, latter, (((1,), (1,)), ((), ())), preferred_element_type=f32
    )


def product_first(former, latter):
    return lax.dot_general(
        former, latter, (((0,), (0,)), ((), ())), preferred_element_type=f32
    )


def swap(values, axis):
    return lax.ppermute(values, axis, [(0, 1), (1, 0)])


def pair_all_to_all(parts, axis):
    me = lax.axis_index(axis)
    mine = lax.dynamic_index_in_dim(parts, me, 0, keepdims=False)
    theirs = lax.dynamic_index_in_dim(parts, 1 - me, 0, keepdims=False)
    got = swap(theirs, axis)
    first = me == 0
    return jnp.stack([jnp.where(first, mine, got), jnp.where(first, got, mine)])


def ring_order(count):
    return list(range(0, count, 2)) + list(range(1, count, 2))[::-1]


def ring_gather(block, axis, width):
    count = lax.axis_size(axis)
    order = ring_order(count)
    order_of = jnp.array(order, jnp.int32)
    place = jnp.array([order.index(i) for i in range(count)], jnp.int32)[lax.axis_index(axis)]
    right = [(order[i], order[(i + 1) % count]) for i in range(count)]
    left = [(order[i], order[(i - 1) % count]) for i in range(count)]
    rows, columns = block.shape
    half = rows // 2
    out = jnp.zeros((count, rows, width), block.dtype)
    marks = jnp.zeros((count, 16, columns - width), block.dtype)

    def put(out, marks, piece, source, row):
        out = lax.dynamic_update_slice(out, piece[None, :, :width], (source, row, 0))
        if row == 0:
            marks = lax.dynamic_update_slice(marks, piece[None, :16, width:], (source, 0, 0))
        return out, marks

    out, marks = put(out, marks, block, lax.axis_index(axis), 0)
    forward, backward = block, block
    for step in range(1, count // 2 + 1):
        last = step == count // 2
        if last:
            forward, backward = forward[:half], backward[half:]
        forward = lax.ppermute(forward, axis, right)
        backward = lax.ppermute(backward, axis, left)
        out, marks = put(out, marks, forward, order_of[(place - step) % count], 0)
        out, marks = put(out, marks, backward, order_of[(place + step) % count], half if last else 0)
    return out.reshape(count * rows, width), marks


def after(values, *events):
    return lax.optimization_barrier((values,) + events)[0]


def all_to_all_permutes(parts, axis):
    count = lax.axis_size(axis)
    me = lax.axis_index(axis)
    out = parts
    for step in range(1, count):
        sent = lax.dynamic_index_in_dim(parts, (me + step) % count, 0, keepdims=True)
        got = lax.ppermute(sent, axis, [(i, (i + step) % count) for i in range(count)])
        out = lax.dynamic_update_slice_in_dim(out, got, (me - step) % count, 0)
    return out


def ring_scatter(chunks, count, stride):
    order = ring_order(count)
    order_of = jnp.array(order, jnp.int32)
    member = lax.axis_index("dp") // stride
    place = jnp.array([order.index(i) for i in range(count)], jnp.int32)[member]

    def moves(by):
        return [
            (order[i] * stride + j, order[(i + by) % count] * stride + j)
            for i in range(count)
            for j in range(stride)
        ]

    right, left = moves(1), moves(-1)
    half = chunks.shape[1] // 2
    far = count // 2

    def chunk(offset):
        return lax.dynamic_index_in_dim(chunks, order_of[(place + offset) % count], 0, keepdims=False)

    def added(sent, first, offset):
        own = chunk(offset).astype(f32)
        if first is None:
            return (own + sent.astype(f32)).astype(bf16)
        lower, upper = own[:half], own[half:]
        if first:
            lower = lower + sent.astype(f32)
        else:
            upper = upper + sent.astype(f32)
        return jnp.concatenate([lower, upper]).astype(bf16)

    forward, backward = chunk(far)[:half], chunk(-far)[half:]
    for step in range(far):
        event = forward
        forward = lax.ppermute(forward, "dp", right)
        backward = lax.ppermute(backward, "dp", left)
        offset = far - 1 - step
        if offset:
            forward = added(forward, True if step == 0 else None, offset)
            backward = added(backward, False if step == 0 else None, -offset)
    return chunk(0).astype(f32) + forward.astype(f32) + backward.astype(f32), event


def attend_body(tiles, keys_per_tile, q_ref, k_ref, v_ref, bias_ref, out_ref, total_ref):
    rows = q_ref.shape[0] // tiles
    for tile in range(tiles):
        here = pl.ds(tile * rows, rows)
        keys = (tile + 1) * keys_per_tile
        scores = product_last(q_ref[here, :], k_ref[:keys, :]) * scale
        scores = scores + bias_ref[here, :keys].astype(f32)
        highest = jnp.max(scores, axis=1, keepdims=True)
        expo = jnp.exp(scores - highest)
        summed = jnp.sum(expo, axis=1, keepdims=True)
        probs = (expo * (1.0 / summed)).astype(bf16)
        out_ref[here, :] = product(probs, v_ref[:keys, :]).astype(bf16)
        total_ref[0, here, :] = highest + jnp.log(summed)


def attend(queries, shared, bias, tiles):
    rows, columns = queries.shape
    length = shared.shape[0]
    heads = columns // HEAD
    return pl.pallas_call(
        functools.partial(attend_body, tiles, length // tiles),
        grid=(heads,),
        in_specs=[
            pl.BlockSpec((rows, HEAD), lambda h: (0, h)),
            pl.BlockSpec((length, HEAD), lambda h: (0, h)),
            pl.BlockSpec((length, HEAD), lambda h: (0, heads + h)),
            pl.BlockSpec((rows, length), lambda h: (0, 0)),
        ],
        out_specs=[
            pl.BlockSpec((rows, HEAD), lambda h: (0, h)),
            pl.BlockSpec((1, rows, 1), lambda h: (h, 0, 0)),
        ],
        out_shape=[
            jax.ShapeDtypeStruct((rows, columns), bf16),
            jax.ShapeDtypeStruct((heads, rows, 1), f32),
        ],
        compiler_params=pltpu.CompilerParams(vmem_limit_bytes=48 * 2**20),
        cost_estimate=pl.CostEstimate(
            flops=4 * rows * length * columns,
            bytes_accessed=2 * (rows * length + 2 * length * columns),
            transcendentals=rows * length * heads,
        ),
        name="attend",
    )(queries, shared, shared, bias)


def attend_back_body(
    tiles, keys_per_tile, q_ref, k_ref, v_ref, bias_ref, total_ref, grad_ref, dq_ref, dk_ref, dv_ref, dk_sum, dv_sum
):
    rows = q_ref.shape[0] // tiles
    dk_sum[...] = jnp.zeros_like(dk_sum)
    dv_sum[...] = jnp.zeros_like(dv_sum)
    for tile in range(tiles):
        here = pl.ds(tile * rows, rows)
        keys = (tile + 1) * keys_per_tile
        query, grad = q_ref[here, :], grad_ref[here, :]
        scores = product_last(query, k_ref[:keys, :]) * scale
        scores = scores + bias_ref[here, :keys].astype(f32)
        probs = jnp.exp(scores - total_ref[0, here, :])
        prob_grad = product_last(grad, v_ref[:keys, :])
        inner = jnp.sum(probs * prob_grad, axis=1, keepdims=True)
        score_grad = (probs * (prob_grad - inner) * scale).astype(bf16)
        dq_ref[here, :] = product(score_grad, k_ref[:keys, :]).astype(bf16)
        dk_sum[:keys, :] += product_first(score_grad, query)
        dv_sum[:keys, :] += product_first(probs.astype(bf16), grad)
    dk_ref[...] = dk_sum[...].astype(bf16)
    dv_ref[...] = dv_sum[...].astype(bf16)


def attend_back(queries, shared, bias, total, grads, tiles):
    rows, columns = queries.shape
    length = shared.shape[0]
    heads = columns // HEAD
    row_spec = pl.BlockSpec((rows, HEAD), lambda h: (0, h))
    key_spec = pl.BlockSpec((length, HEAD), lambda h: (0, h))
    return pl.pallas_call(
        functools.partial(attend_back_body, tiles, length // tiles),
        grid=(heads,),
        in_specs=[
            row_spec,
            key_spec,
            pl.BlockSpec((length, HEAD), lambda h: (0, heads + h)),
            pl.BlockSpec((rows, length), lambda h: (0, 0)),
            pl.BlockSpec((1, rows, 1), lambda h: (h, 0, 0)),
            row_spec,
        ],
        out_specs=[row_spec, key_spec, key_spec],
        out_shape=[
            jax.ShapeDtypeStruct((rows, columns), bf16),
            jax.ShapeDtypeStruct((length, columns), bf16),
            jax.ShapeDtypeStruct((length, columns), bf16),
        ],
        scratch_shapes=[pltpu.VMEM((length, HEAD), f32), pltpu.VMEM((length, HEAD), f32)],
        compiler_params=pltpu.CompilerParams(vmem_limit_bytes=48 * 2**20),
        cost_estimate=pl.CostEstimate(
            flops=10 * rows * length * columns,
            bytes_accessed=2 * (rows * length + 4 * length * columns),
            transcendentals=rows * length * heads,
        ),
        name="attend_back",
    )(queries, shared, shared, bias, total, grads)


def pair_slots(routes, ranking, capacity):
    flat_routes, flat_rank = routes.reshape(-1), ranking.reshape(-1)
    same_expert = flat_routes[:, None] == flat_routes[None, :]
    earlier = flat_rank[None, :] < flat_rank[:, None]
    slots = jnp.sum(jnp.logical_and(same_expert, earlier).astype(jnp.int32), axis=1)
    return jnp.minimum(slots, capacity).reshape(routes.shape)


def own_mask(routes, slots, experts, capacity):
    places = jnp.arange(experts * capacity)[:, None]
    hits = [
        (places // capacity == routes[k][None]) & (places % capacity == slots[k][None])
        for k in range(2)
    ]
    return jnp.logical_or(hits[0], hits[1]).astype(bf16)


def expert_mask(marks, expert, capacity):
    slots = jnp.arange(capacity, dtype=jnp.int32)[None, :, None]
    hits = [
        (marks[:, 2 * k][:, None] == expert) & (marks[:, 2 * k + 1][:, None] == slots)
        for k in range(2)
    ]
    other = sum(
        jnp.sum(jnp.where(hits[k], marks[:, 2 - 2 * k][:, None], 0), axis=2) for k in range(2)
    )
    return jnp.logical_or(hits[0], hits[1]), other.reshape(-1)


def gate_of(rows, router, expert, other):
    logits = product(rows, router)
    range_of = jnp.arange(router.shape[1])[None, :]
    own_hot = (range_of == expert).astype(f32)
    other_hot = (range_of == other[:, None]).astype(f32)
    difference = own_hot - other_hot
    gate = jax.nn.sigmoid(jnp.sum(logits * difference, axis=1, keepdims=True))
    return gate, difference


def row_bias(chosen, segments, parents):
    blocks, capacity, count = chosen.shape
    length = segments.shape[0]
    seg_blocks = segments.reshape(blocks, 1, count)
    here = jnp.arange(count)[None, None, :]
    own = jnp.sum(jnp.where(chosen, seg_blocks, 0), axis=2).reshape(-1, 1)
    place = jnp.sum(jnp.where(chosen, here, 0), axis=2) + jnp.arange(blocks)[:, None] * count
    place = place.reshape(-1, 1)
    range_of = jnp.arange(parents.shape[0])[None, :]
    one = jnp.sum(jnp.where(own == range_of, parents[None, :], 0), axis=1, keepdims=True)
    two = jnp.sum(jnp.where(one == range_of, parents[None, :], 0), axis=1, keepdims=True)
    keys = segments[None, :]
    visible = ((keys == own) | (keys == one) | (keys == two)) & (jnp.arange(length)[None, :] <= place)
    return jnp.where(visible, 0.0, negative).astype(bf16)


def per_device(
    tokens,
    cotangent,
    attn_gain,
    mlp_gain,
    key_weight,
    value_weight,
    query_weight,
    output_weight,
    attn_router,
    gate_weight,
    up_weight,
    down_weight,
    mlp_router,
    segment_ids,
    parent_ids,
    attn_routes,
    mlp_routes,
    slot_order,
):
    count, width = tokens.shape[1:]
    half = width // 2
    piece = query_weight.shape[1]
    experts = attn_router.shape[1]
    blocks = lax.axis_size("dp")
    members = blocks // experts
    capacity = min(count, 5 * count * attn_routes.shape[2] // (4 * experts))
    length, parents = segment_ids.shape[1], parent_ids.shape[1]
    tiles = blocks // 2
    dp, core, shard = lax.axis_index("dp"), lax.axis_index("expert"), lax.axis_index("shard")
    expert, member = dp // members, dp % members

    def my_half(values):
        return lax.dynamic_slice_in_dim(values, shard * half, half, values.ndim - 1)

    def their_half(values):
        return lax.dynamic_slice_in_dim(values, (1 - shard) * half, half, values.ndim - 1)

    def whole(mine):
        got = swap(mine, "shard")
        first = shard == 0
        return jnp.concatenate(
            [jnp.where(first, mine, got), jnp.where(first, got, mine)], axis=mine.ndim - 1
        )

    ranking = slot_order[0, 0].reshape(count, -1).T
    own_attn, own_mlp = attn_routes[0].T, mlp_routes[0].T
    attn_slots = pair_slots(own_attn, ranking, capacity)
    mlp_slots = pair_slots(own_mlp, ranking, capacity)
    attn_pack = own_mask(own_attn, attn_slots, experts, capacity)
    mlp_pack = own_mask(own_mlp, mlp_slots, experts, capacity)
    own_segments = lax.dynamic_slice_in_dim(segment_ids, dp * count, count, 1)
    marks = [own_attn[:1], attn_slots[:1], own_attn[1:], attn_slots[1:]]
    marks += [own_mlp[:1], mlp_slots[:1], own_mlp[1:], mlp_slots[1:]]
    marks += [own_segments, jnp.pad(parent_ids, ((0, 0), (0, count - parent_ids.shape[1])))]
    marks = jnp.pad(jnp.concatenate(marks), ((0, count - 10), (0, 0))).astype(bf16)

    def dispatch(values, pack, permutes=False):
        packed = product(pack, values).astype(bf16).reshape(experts, 1, capacity, half)
        packed = jnp.broadcast_to(packed, (experts, members, capacity, half))
        packed = packed.reshape(blocks, capacity, half)
        if permutes:
            arrived = all_to_all_permutes(packed, "dp")
        else:
            arrived = lax.all_to_all(packed, "dp", 0, 0, tiled=True)
        own = whole(arrived.reshape(blocks * capacity, half))
        return jnp.concatenate([own, swap(own, "expert")])

    def combine(rows, pack):
        own, other = jnp.split(rows, 2)
        got = swap(other, "expert")
        theirs = (their_half(own).astype(f32) + their_half(got).astype(f32)).astype(bf16)
        back = swap(theirs, "shard")
        mine = my_half(own).astype(f32) + my_half(got).astype(f32) + back.astype(f32)
        mine = mine.astype(bf16).reshape(blocks, capacity, half)
        back = lax.all_to_all(mine, "dp", 0, 0, tiled=True)
        if members > 1:
            back = back.reshape(experts, members, capacity, half).astype(f32)
            back = jnp.sum(back, axis=1).astype(bf16)
        return product_first(pack, back.reshape(experts * capacity, half))

    heads_at = (member * 2 + core) * 2 + shard
    holder = (member * 2 + core) // members
    offset = holder * 2 * members
    names = ("dp", "expert", "shard")
    sends = []
    for d in range(blocks):
        for c in range(2):
            at = (d * 2 + c) * 2
            source = ((d % members) * 2 + c) // members
            sends.append((at + source, at + 1 - source))
    partner_at = (member * 2 + core) * 2 + 1 - shard

    def head_columns(at):
        return jnp.concatenate(
            [
                lax.dynamic_slice_in_dim(weight, (at - offset) * piece, piece, 1)
                for weight in (key_weight, value_weight)
            ],
            axis=1,
        )

    inputs = tokens[0].astype(f32)
    attn_scale = lax.rsqrt(jnp.mean(inputs * inputs, axis=1, keepdims=True) + epsilon)
    normed = (inputs * attn_scale * attn_gain).astype(bf16)
    own_normed, own_marks = ring_gather(jnp.concatenate([normed, marks], axis=1), "dp", width)
    tree_normed = [own_normed, swap(own_normed, "expert")]
    tree_marks = [m.astype(jnp.int32) for m in (own_marks, swap(own_marks, "expert"))]
    got = lax.ppermute(after(head_columns(partner_at), normed), names, sends)
    shared_weight = jnp.where(shard == holder, head_columns(heads_at), got)
    grad_half = my_half(cotangent[0])
    grad_rows = dispatch(after(grad_half, own_normed), mlp_pack, permutes=True)

    attn_marks = [expert_mask(m[:, :4], expert, capacity) for m in tree_marks]
    mlp_marks = [expert_mask(m[:, 4:8], expert, capacity) for m in tree_marks]
    biases = [
        row_bias(attn_marks[t][0], tree_marks[t][:, 8].reshape(-1), tree_marks[t][0, 9, :parents])
        for t in range(2)
    ]
    attn_other = jnp.concatenate([attn_marks[0][1], attn_marks[1][1]])
    mlp_other = jnp.concatenate([mlp_marks[0][1], mlp_marks[1][1]])

    tree_rows, tree_shared = [], []
    for t in range(2):
        tree_shared.append(product(tree_normed[t], shared_weight).astype(bf16))
        picked = lax.dot_general(
            attn_marks[t][0].astype(bf16),
            tree_normed[t].reshape(blocks, count, width),
            (((2,), (1,)), ((0,), (0,))),
            preferred_element_type=f32,
        )
        tree_rows.append(picked.astype(bf16).reshape(blocks * capacity, width))
    rows = jnp.concatenate(tree_rows)
    queries = product(rows, query_weight).astype(bf16)
    tree_queries = jnp.split(queries, 2)
    forward = [
        attend(tree_queries[t], tree_shared[t], biases[t], tiles) for t in range(2)
    ]
    attended = jnp.concatenate([forward[0][0], forward[1][0]])
    attn_gate, attn_difference = gate_of(rows, attn_router, expert, attn_other)
    attn_terms = product_last(attended, output_weight)
    attn_terms = (attn_gate * attn_terms).astype(bf16)
    attn_mix = combine(attn_terms, attn_pack)
    middle = my_half(inputs) + attn_mix

    def feature_mean(values):
        part = jnp.sum(values, axis=1, keepdims=True)
        return (part + swap(part, "shard")) / width

    mlp_scale = lax.rsqrt(feature_mean(middle * middle) + epsilon)
    half_gain = my_half(mlp_gain)
    mlp_normed = (middle * mlp_scale * half_gain).astype(bf16)
    mlp_rows = dispatch(mlp_normed, mlp_pack)
    mlp_gate, mlp_difference = gate_of(mlp_rows, mlp_router, expert, mlp_other)
    gate_pre = product(mlp_rows, gate_weight)
    up_pre = product(mlp_rows, up_weight)
    gate_sigmoid = jax.nn.sigmoid(gate_pre)
    silu_values = gate_pre * gate_sigmoid
    hidden = (silu_values * up_pre).astype(bf16)
    plain_grad = product(after(grad_rows, attn_terms), down_weight)
    mlp_gate_grad = jnp.sum(hidden.astype(f32) * plain_grad, axis=1, keepdims=True)
    hidden_grad = mlp_gate * plain_grad
    gate_pre_grad = (
        hidden_grad * up_pre * gate_sigmoid * (1.0 + gate_pre * (1.0 - gate_sigmoid))
    ).astype(bf16)
    up_pre_grad = (hidden_grad * silu_values).astype(bf16)
    mlp_coefs = mlp_gate * (1.0 - mlp_gate) * mlp_gate_grad * mlp_difference
    row_grad = (
        product_last(gate_pre_grad, gate_weight)
        + product_last(up_pre_grad, up_weight)
        + product_last(mlp_coefs, mlp_router.astype(f32))
    ).astype(bf16)
    mlp_normed_grad = combine(row_grad, mlp_pack)
    late_hidden = after(hidden, row_grad)
    mlp_terms = (mlp_gate * product_last(late_hidden, down_weight)).astype(bf16)
    down_grad = product_first((mlp_gate * grad_rows.astype(f32)).astype(bf16), late_hidden)
    mlp_router_part = product_first(mlp_coefs, mlp_rows.astype(f32))

    mlp_n = middle * mlp_scale
    weighted = mlp_normed_grad * half_gain
    mlp_gain_part = jnp.sum(mlp_normed_grad * mlp_n, axis=0)
    middle_grad = grad_half.astype(f32) + mlp_scale * (
        weighted - mlp_n * feature_mean(weighted * mlp_n)
    )
    low_grad = middle_grad.astype(bf16)
    term_rows = dispatch(low_grad, attn_pack)
    late_rows = after(mlp_rows, low_grad)
    gate_grad = product_first(late_rows, gate_pre_grad)
    up_grad = product_first(late_rows, up_pre_grad)
    mlp_mix = combine(after(mlp_terms, term_rows), mlp_pack)
    layer_out = whole((middle + mlp_mix).astype(bf16))[None]
    plain_attended_grad = product(term_rows, output_weight)
    attn_gate_grad = jnp.sum(attended.astype(f32) * plain_attended_grad, axis=1, keepdims=True)
    attended_grad = jnp.split((attn_gate * plain_attended_grad).astype(bf16), 2)
    backward = [
        attend_back(
            tree_queries[t],
            tree_shared[t],
            biases[t],
            forward[t][1],
            attended_grad[t],
            tiles,
        )
        for t in range(2)
    ]
    query_rows_grad = jnp.concatenate([backward[0][0], backward[1][0]])
    part = length // experts
    key_chunks = jnp.concatenate(
        [backward[t][i].reshape(experts, part, piece) for i in (1, 2) for t in range(2)], axis=1
    )
    key_sums, event = ring_scatter(key_chunks, experts, members)
    key_sums = key_sums.astype(bf16)
    attn_coefs = attn_gate * (1.0 - attn_gate) * attn_gate_grad * attn_difference
    input_rows_grad = product_last(query_rows_grad, query_weight) + product_last(
        attn_coefs, attn_router.astype(f32)
    )
    input_rows_grad = input_rows_grad.astype(bf16)
    normed_grad = combine(input_rows_grad, attn_pack)
    weight_chunks = jnp.concatenate(
        [
            sum(product_first(tree_normed[t], backward[t][i]) for t in range(2))
            .astype(bf16)
            .reshape(experts, width // experts, piece)
            for i in (1, 2)
        ],
        axis=1,
    )
    weight_sums = ring_scatter(after(weight_chunks, event), experts, members)[0]
    query_grad = product_first(after(rows, input_rows_grad), query_rows_grad)
    late_terms = after(term_rows, input_rows_grad)
    output_grad = product_first((attn_gate * late_terms.astype(f32)).astype(bf16), attended)
    attn_router_part = product_first(attn_coefs, rows.astype(f32))

    def shared_part(t):
        keys_part = key_sums[t * part : (t + 1) * part]
        values_part = key_sums[(2 + t) * part : (3 + t) * part]
        return product_last(jnp.concatenate([keys_part, values_part], axis=1), shared_weight)

    shared = shared_part(0) + swap(shared_part(1).astype(bf16), "expert").astype(f32)
    if members > 1:
        groups = [[e * members + m for m in range(members)] for e in range(experts)]
        shared = lax.psum_scatter(
            shared, "dp", scatter_dimension=0, axis_index_groups=groups, tiled=True
        )
    shared = my_half(shared) + swap(their_half(shared).astype(bf16), "shard").astype(f32)
    normed_grad = normed_grad + shared

    attn_n = my_half(inputs) * attn_scale
    weighted = normed_grad * my_half(attn_gain)
    attn_gain_part = jnp.sum(normed_grad * attn_n, axis=0)
    tokens_grad = middle_grad + attn_scale * (weighted - attn_n * feature_mean(weighted * attn_n))
    got = swap(tokens_grad.astype(bf16), "shard").astype(f32)
    tokens_grad = jnp.concatenate(
        [jnp.where(shard == 0, tokens_grad, got), jnp.where(shard == 0, got, tokens_grad)], axis=1
    )[None]

    features = width // (2 * blocks)
    pieces = weight_sums.astype(bf16).reshape(2, members, 2, features, piece).transpose(1, 2, 0, 3, 4)
    if members > 1:
        groups = [[e * members + m for m in range(members)] for e in range(experts)]
        pieces = lax.all_to_all(pieces, "dp", 0, 0, axis_index_groups=groups, tiled=True)
    pieces = pair_all_to_all(pieces.transpose(1, 0, 2, 3, 4), "expert")
    pieces = pieces.transpose(1, 0, 2, 3, 4).reshape(2, members, 2, features, piece)
    pieces = pair_all_to_all(pieces, "shard")
    pieces = pieces.transpose(2, 3, 1, 0, 4).reshape(2, features, -1).astype(f32)

    def spread(values):
        return lax.dynamic_update_slice(jnp.zeros((1, width), f32), values[None], (0, shard * half))

    def small_sum(values):
        values = values + swap(values, "shard")
        values = values.reshape(-1, blocks, 2, features).transpose(2, 1, 0, 3)
        mine = lax.dynamic_index_in_dim(values, core, 0, keepdims=False)
        theirs = lax.dynamic_index_in_dim(values, 1 - core, 0, keepdims=False)
        mine = mine + swap(theirs, "expert")
        return jnp.sum(lax.all_to_all(mine, "dp", 0, 0, tiled=True), axis=0)

    routers = small_sum(jnp.concatenate([attn_router_part, mlp_router_part]))
    gains = jnp.concatenate([spread(attn_gain_part), spread(mlp_gain_part)])
    gains = small_sum(jnp.pad(gains, ((0, 6), (0, 0))))
    return (
        layer_out,
        tokens_grad,
        gains[0],
        gains[1],
        pieces[0],
        pieces[1],
        query_grad,
        output_grad,
        routers[:experts].T,
        gate_grad,
        up_grad,
        down_grad,
        routers[experts:].T,
    )


def solution(mesh):
    tree = P("expert", "dp", None)
    columns = P(None, ("dp", "expert", "shard"))
    spread = P(("dp", "expert"), None)
    in_specs = (
        tree,
        tree,
        P(),
        P(),
        P(None, "shard"),
        P(None, "shard"),
        columns,
        columns,
        P(),
        columns,
        columns,
        columns,
        P(),
        P("expert", None),
        P("expert", None),
        tree,
        tree,
        tree,
    )
    out_specs = (
        tree,
        tree,
        P(("dp", "expert")),
        P(("dp", "expert")),
        P(("dp", "expert"), "shard"),
        P(("dp", "expert"), "shard"),
        columns,
        columns,
        spread,
        columns,
        columns,
        columns,
        spread,
    )
    return jax.shard_map(
        per_device, mesh=mesh, in_specs=in_specs, out_specs=out_specs, check_vma=False
    )
```

```python
import functools

import jax
import jax.numpy as jnp
from jax import lax
from jax.experimental import pallas as pl
from jax.experimental.pallas import tpu as pltpu
from jax.sharding import PartitionSpec as P

HEAD = 128

epsilon = 1e-06
negative = -1e30
scale = HEAD ** (-0.5)
bf16 = jnp.bfloat16
f32 = jnp.float32


def product(former, latter):
    return jnp.dot(former, latter, preferred_element_type=f32)


def product_last(former, latter):
    return lax.dot_general(
        former, latter, (((1,), (1,)), ((), ())), preferred_element_type=f32
    )


def product_first(former, latter):
    return lax.dot_general(
        former, latter, (((0,), (0,)), ((), ())), preferred_element_type=f32
    )


def limit_of(rows):
    return min(56, max(40, rows * 24 // 640)) * 2**20


def swap(values, axis):
    return lax.ppermute(values, axis, [(0, 1), (1, 0)])


def pair_all_to_all(parts, axis):
    me = lax.axis_index(axis)
    mine = lax.dynamic_index_in_dim(parts, me, 0, keepdims=False)
    theirs = lax.dynamic_index_in_dim(parts, 1 - me, 0, keepdims=False)
    got = swap(theirs, axis)
    first = me == 0
    return jnp.stack([jnp.where(first, mine, got), jnp.where(first, got, mine)])


def ring_order(count):
    return list(range(0, count, 2)) + list(range(1, count, 2))[::-1]


def ring_member(place, count):
    place = lax.rem(place + 2 * count, count)
    return jnp.where(place < count // 2, 2 * place, 2 * (count - place) - 1)


def ring_place(member, count):
    return jnp.where(member % 2 == 0, member // 2, count - (member + 1) // 2)


def empty(shape, dtype):
    return pl.pallas_call(
        lambda ref: None,
        out_shape=jax.ShapeDtypeStruct(shape, dtype),
        out_specs=pl.BlockSpec(memory_space=pl.ANY),
        name="empty",
    )()


def ring_gather(block, axis, count, stride):
    order = ring_order(count)
    member = lax.axis_index(axis) // stride
    place = ring_place(member, count)
    right, left = ring_moves(order, 1, stride), ring_moves(order, -1, stride)
    rows, columns = block.shape
    half = rows // 2
    out = empty((count, rows, columns), block.dtype)

    def put(out, piece, source, row):
        return lax.dynamic_update_slice(out, piece[None], (source, row, 0))

    out = put(out, block, member, 0)
    forward, backward = block, block
    arrivals = []
    for step in range(1, count // 2 + 1):
        last = step == count // 2
        if last:
            forward, backward = forward[:half], backward[half:]
        forward = lax.ppermute(forward, axis, right)
        backward = lax.ppermute(backward, axis, left)
        arrivals.append(forward)
        out = put(out, forward, ring_member(place - step, count), 0)
        out = put(out, backward, ring_member(place + step, count), half if last else 0)
    return out, arrivals


def ring_moves(order, by, stride):
    count = len(order)
    return [
        (order[i] * stride + j, order[(i + by) % count] * stride + j)
        for i in range(count)
        for j in range(stride)
    ]


def after(values, *events):
    if events[0] is None:
        return values
    return lax.optimization_barrier((values,) + events)[0]


def ring_scatter(parts, count, stride):
    order = ring_order(count)
    place = ring_place(lax.axis_index("dp") // stride, count)
    right, left = ring_moves(order, 1, stride), ring_moves(order, -1, stride)
    far = count // 2

    def part(tree, offset):
        return lax.dynamic_index_in_dim(parts[tree], ring_member(place + offset, count), 0, keepdims=False)

    def added(sent, tree, offset):
        return (part(tree, offset).astype(f32) + sent.astype(f32)).astype(bf16)

    forward, backward = [part(0, far)], [part(1, -far)]
    first = None
    for step in range(far):
        forward = [lax.ppermute(v, "dp", right) for v in forward]
        backward = [lax.ppermute(v, "dp", left) for v in backward]
        first = forward[0] if first is None else first
        offset = far - 1 - step
        if step == 0:
            forward.append(part(1, offset))
            backward.insert(0, part(0, -offset))
            if offset:
                forward[0] = added(forward[0], 0, offset)
                backward[1] = added(backward[1], 1, -offset)
        elif offset:
            forward = [added(forward[t], t, offset) for t in range(2)]
            backward = [added(backward[t], t, -offset) for t in range(2)]
    total = [part(t, 0).astype(f32) + forward[t].astype(f32) + backward[t].astype(f32) for t in range(2)]
    return jnp.stack(total), first


def attend_body(tiles, keys_per_tile, q_ref, k_ref, v_ref, bias_ref, gate_ref, out_ref, total_ref):
    rows = q_ref.shape[0] // tiles
    for tile in range(tiles):
        here = pl.ds(tile * rows, rows)
        keys = (tile + 1) * keys_per_tile
        scores = product_last(q_ref[here, :], k_ref[:keys, :]) * scale
        scores = scores + bias_ref[here, :keys].astype(f32)
        highest = jnp.max(scores, axis=1, keepdims=True)
        expo = jnp.exp(scores - highest)
        summed = jnp.sum(expo, axis=1, keepdims=True)
        probs = (expo * (1.0 / summed)).astype(bf16)
        mixed = product(probs, v_ref[:keys, :]).astype(bf16).astype(f32)
        out_ref[here, :] = (mixed * gate_ref[here, :]).astype(bf16)
        total_ref[0, here, :] = highest + jnp.log(summed)


def attend(queries, shared, bias, gate, tiles):
    rows, columns = queries.shape[0] // 2, queries.shape[1]
    length = shared.shape[0] // 2
    heads = columns // HEAD
    return pl.pallas_call(
        functools.partial(attend_body, tiles, length // tiles),
        grid=(2, heads),
        in_specs=[
            pl.BlockSpec((rows, HEAD), lambda t, h: (t, h)),
            pl.BlockSpec((length, HEAD), lambda t, h: (t, 2 * h)),
            pl.BlockSpec((length, HEAD), lambda t, h: (t, 2 * h + 1)),
            pl.BlockSpec((rows, length), lambda t, h: (t, 0)),
            pl.BlockSpec((rows, 1), lambda t, h: (t, 0)),
        ],
        out_specs=[
            pl.BlockSpec((rows, HEAD), lambda t, h: (t, h)),
            pl.BlockSpec((1, rows, 1), lambda t, h: (t * heads + h, 0, 0)),
        ],
        out_shape=[
            jax.ShapeDtypeStruct((2 * rows, columns), bf16),
            jax.ShapeDtypeStruct((2 * heads, rows, 1), f32),
        ],
        compiler_params=pltpu.CompilerParams(vmem_limit_bytes=limit_of(2 * rows)),
        cost_estimate=pl.CostEstimate(
            flops=8 * rows * length * columns,
            bytes_accessed=4 * (rows * length + 2 * length * columns),
            transcendentals=2 * rows * length * heads,
        ),
        name="attend",
    )(queries, shared, shared, bias, gate)


def attend_back_body(
    tiles, keys_per_tile, q_ref, k_ref, v_ref, bias_ref, total_ref, grad_ref, dq_ref, both_ref, dk_sum, dv_sum
):
    rows = q_ref.shape[0] // tiles
    dk_sum[...] = jnp.zeros_like(dk_sum)
    dv_sum[...] = jnp.zeros_like(dv_sum)
    for tile in range(tiles):
        here = pl.ds(tile * rows, rows)
        keys = (tile + 1) * keys_per_tile
        query, grad = q_ref[here, :], grad_ref[here, :]
        scores = product_last(query, k_ref[:keys, :]) * scale
        scores = scores + bias_ref[here, :keys].astype(f32)
        probs = jnp.exp(scores - total_ref[0, here, :])
        prob_grad = product_last(grad, v_ref[:keys, :])
        inner = jnp.sum(probs * prob_grad, axis=1, keepdims=True)
        score_grad = (probs * (prob_grad - inner) * scale).astype(bf16)
        dq_ref[here, :] = product(score_grad, k_ref[:keys, :]).astype(bf16)
        dk_sum[:keys, :] += product_first(score_grad, query)
        dv_sum[:keys, :] += product_first(probs.astype(bf16), grad)
    both_ref[0, :, :HEAD] = dk_sum[...].astype(bf16)
    both_ref[0, :, HEAD:] = dv_sum[...].astype(bf16)


def attend_back(queries, shared, bias, total, grads, tiles):
    rows, columns = queries.shape[0] // 2, queries.shape[1]
    length = shared.shape[0] // 2
    heads = columns // HEAD
    row_spec = pl.BlockSpec((rows, HEAD), lambda t, h: (t, h))
    return pl.pallas_call(
        functools.partial(attend_back_body, tiles, length // tiles),
        grid=(2, heads),
        in_specs=[
            row_spec,
            pl.BlockSpec((length, HEAD), lambda t, h: (t, 2 * h)),
            pl.BlockSpec((length, HEAD), lambda t, h: (t, 2 * h + 1)),
            pl.BlockSpec((rows, length), lambda t, h: (t, 0)),
            pl.BlockSpec((1, rows, 1), lambda t, h: (t * heads + h, 0, 0)),
            row_spec,
        ],
        out_specs=[row_spec, pl.BlockSpec((1, length, 2 * HEAD), lambda t, h: (t, 0, h))],
        out_shape=[
            jax.ShapeDtypeStruct((2 * rows, columns), bf16),
            jax.ShapeDtypeStruct((2, length, 2 * columns), bf16),
        ],
        scratch_shapes=[pltpu.VMEM((length, HEAD), f32), pltpu.VMEM((length, HEAD), f32)],
        compiler_params=pltpu.CompilerParams(vmem_limit_bytes=limit_of(2 * rows)),
        cost_estimate=pl.CostEstimate(
            flops=20 * rows * length * columns,
            bytes_accessed=4 * (rows * length + 4 * length * columns),
            transcendentals=2 * rows * length * heads,
        ),
        name="attend_back",
    )(queries, shared, shared, bias, total, grads)


def chunk_of(rows):
    return 640 if rows % 640 == 0 else rows


def assemble(shard, pieces, out_ref, sems):
    rows, half = pieces[0].shape
    copies = []
    for i, piece in enumerate(pieces):
        at = pl.multiple_of((shard if i % 2 == 0 else 1 - shard) * half, 128)
        place = out_ref.at[pl.ds(i // 2 * rows, rows), pl.ds(at, half)]
        copies.append(pltpu.make_async_copy(piece, place, sems.at[i]))
    for copy in copies:
        copy.start()
    for copy in copies:
        copy.wait()


def plain_in_body(shard_ref, p0, p1, p2, p3, w_ref, x_ref, y_ref, sems):
    @pl.when(pl.program_id(0) == 0)
    def _():
        assemble(shard_ref[0], (p0, p1, p2, p3), x_ref, sems)

    chunk = chunk_of(x_ref.shape[0])

    @pl.loop(0, x_ref.shape[0] // chunk)
    def _(i):
        here = pl.ds(pl.multiple_of(i * chunk, 16), chunk)
        y_ref[here, :] = product(x_ref[here, :], w_ref[...])


def plain_in(shard, pieces, weight, tile=512):
    rows, half = pieces[0].shape
    columns = weight.shape[1]
    return pl.pallas_call(
        plain_in_body,
        grid_spec=pltpu.PrefetchScalarGridSpec(
            num_scalar_prefetch=1,
            grid=(pl.cdiv(columns, tile),),
            in_specs=[pl.BlockSpec(memory_space=pl.ANY)] * 4
            + [pl.BlockSpec((2 * half, tile), lambda j, s: (0, j))],
            out_specs=[
                pl.BlockSpec((2 * rows, 2 * half), lambda j, s: (0, 0)),
                pl.BlockSpec((2 * rows, tile), lambda j, s: (0, j)),
            ],
            scratch_shapes=[pltpu.SemaphoreType.DMA((4,))],
        ),
        out_shape=[
            jax.ShapeDtypeStruct((2 * rows, 2 * half), bf16),
            jax.ShapeDtypeStruct((2 * rows, columns), f32),
        ],
        compiler_params=pltpu.CompilerParams(vmem_limit_bytes=limit_of(2 * rows)),
        cost_estimate=pl.CostEstimate(
            flops=8 * rows * half * columns,
            bytes_accessed=16 * rows * half + 4 * half * columns + 8 * rows * columns,
            transcendentals=0,
        ),
        name="plain_in",
    )(shard, *pieces, weight)


def expert_begin_body(shard_ref, p0, p2, gw_ref, uw_ref, gate_ref, up_ref, x_ref, sems):
    rows = p0.shape[0]

    @pl.when(pl.program_id(0) == 0)
    def _():
        copies = [
            pltpu.make_async_copy(p, x_ref.at[pl.ds(i * rows, rows), :], sems.at[i])
            for i, p in enumerate((p0, p2))
        ]
        for copy in copies:
            copy.start()
        for copy in copies:
            copy.wait()

    chunk = chunk_of(x_ref.shape[0])

    @pl.loop(0, x_ref.shape[0] // chunk)
    def _(i):
        here = pl.ds(pl.multiple_of(i * chunk, 16), chunk)
        gate_ref[here, :] = product(x_ref[here, :], gw_ref[...])
        up_ref[here, :] = product(x_ref[here, :], uw_ref[...])


def expert_begin(shard, own, other, gate_weight, up_weight, tile=512):
    rows, half = own.shape
    columns = gate_weight.shape[1]
    weight_spec = pl.BlockSpec((half, tile), lambda j, s: (s[0], j))
    tile_spec = pl.BlockSpec((2 * rows, tile), lambda j, s: (0, j))
    return pl.pallas_call(
        expert_begin_body,
        grid_spec=pltpu.PrefetchScalarGridSpec(
            num_scalar_prefetch=1,
            grid=(pl.cdiv(columns, tile),),
            in_specs=[pl.BlockSpec(memory_space=pl.ANY)] * 2 + [weight_spec, weight_spec],
            out_specs=[tile_spec, tile_spec],
            scratch_shapes=[
                pltpu.VMEM((2 * rows, half), bf16),
                pltpu.SemaphoreType.DMA((2,)),
            ],
        ),
        out_shape=[jax.ShapeDtypeStruct((2 * rows, columns), f32)] * 2,
        compiler_params=pltpu.CompilerParams(vmem_limit_bytes=limit_of(2 * rows)),
        cost_estimate=pl.CostEstimate(
            flops=8 * rows * half * columns,
            bytes_accessed=8 * rows * half + 4 * half * columns + 16 * rows * columns,
            transcendentals=0,
        ),
        name="expert_begin",
    )(shard, own, other, gate_weight, up_weight)


def expert_in_body(
    columns, shard_ref, p0, p1, p2, p3, router_ref, diff_ref, plain_ref, gp_ref, up_ref, gw_ref, uw_ref,
    x_ref, gate_ref, total_ref, hidden_ref, dgate_ref, dup_ref, their_ref, sems,
):
    tile = gw_ref.shape[1]
    rows = p0.shape[0]
    step = pl.program_id(0)

    @pl.when(step == 0)
    def _():
        copies = [
            pltpu.make_async_copy(p, their_ref.at[pl.ds(i * rows, rows), :], sems.at[4 + i])
            for i, p in enumerate((p1, p3))
        ]
        for copy in copies:
            copy.start()
        assemble(shard_ref[0], (p0, p1, p2, p3), x_ref, sems)
        for copy in copies:
            copy.wait()
        logits = product(x_ref[...], router_ref[...])
        gate_ref[...] = jax.nn.sigmoid(jnp.sum(logits * diff_ref[...], axis=1, keepdims=True))
        total_ref[...] = jnp.zeros_like(total_ref)

    chunk = chunk_of(x_ref.shape[0])

    @pl.loop(0, x_ref.shape[0] // chunk)
    def _(i):
        here = pl.ds(pl.multiple_of(i * chunk, 16), chunk)
        their = their_ref[here, :]
        gate_pre = gp_ref[here, :] + product(their, gw_ref[...])
        up_pre = up_ref[here, :] + product(their, uw_ref[...])
        plain, gate = plain_ref[here, :], gate_ref[here, :]
        inside = lax.broadcasted_iota(jnp.int32, (1, tile), 1) + step * tile < columns
        sigmoid = jax.nn.sigmoid(gate_pre)
        silu = gate_pre * sigmoid
        hidden = (silu * up_pre).astype(bf16).astype(f32)
        gated = (gate * hidden).astype(bf16)
        hidden_ref[here, :] = gated
        total_ref[here, :] += jnp.sum(
            jnp.where(inside, gated.astype(f32) * plain, 0.0), axis=1, keepdims=True
        )
        hidden_grad = gate * plain
        up_grad = hidden_grad * silu
        dup_ref[here, :] = up_grad.astype(bf16)
        gate_grad = hidden_grad * up_pre * (sigmoid + silu * (1.0 - sigmoid))
        dgate_ref[here, :] = gate_grad.astype(bf16)


def expert_in(shard, pieces, router, difference, plain, begun, gate_weight, up_weight, tile=256):
    rows, half = pieces[0].shape
    columns = gate_weight.shape[1]
    weight_spec = pl.BlockSpec((half, tile), lambda j, s: (1 - s[0], j))
    tile_spec = pl.BlockSpec((2 * rows, tile), lambda j, s: (0, j))
    held_spec = pl.BlockSpec((2 * rows, 1), lambda j, s: (0, 0))
    hidden_shape = jax.ShapeDtypeStruct((2 * rows, columns), bf16)
    return pl.pallas_call(
        functools.partial(expert_in_body, columns),
        grid_spec=pltpu.PrefetchScalarGridSpec(
            num_scalar_prefetch=1,
            grid=(pl.cdiv(columns, tile),),
            in_specs=[pl.BlockSpec(memory_space=pl.ANY)] * 4
            + [
                pl.BlockSpec(router.shape, lambda j, s: (0, 0)),
                pl.BlockSpec(difference.shape, lambda j, s: (0, 0)),
                tile_spec,
                tile_spec,
                tile_spec,
                weight_spec,
                weight_spec,
            ],
            out_specs=[
                pl.BlockSpec((2 * rows, 2 * half), lambda j, s: (0, 0)),
                held_spec,
                held_spec,
                tile_spec,
                tile_spec,
                tile_spec,
            ],
            scratch_shapes=[
                pltpu.VMEM((2 * rows, half), bf16),
                pltpu.SemaphoreType.DMA((6,)),
            ],
        ),
        out_shape=[
            jax.ShapeDtypeStruct((2 * rows, 2 * half), bf16),
            jax.ShapeDtypeStruct((2 * rows, 1), f32),
            jax.ShapeDtypeStruct((2 * rows, 1), f32),
            hidden_shape,
            hidden_shape,
            hidden_shape,
        ],
        compiler_params=pltpu.CompilerParams(vmem_limit_bytes=limit_of(2 * rows)),
        cost_estimate=pl.CostEstimate(
            flops=8 * rows * half * columns,
            bytes_accessed=16 * rows * half + 4 * half * columns + 36 * rows * columns,
            transcendentals=2 * rows * columns,
        ),
        name="expert_in",
    )(shard, *pieces, router, difference, plain, *begun, gate_weight, up_weight)


def attended_in_body(
    shard_ref, p0, p1, p2, p3, gate_ref, mixed_ref, w_ref, x_ref, total_ref, y_ref, sems
):
    @pl.when(pl.program_id(0) == 0)
    def _():
        assemble(shard_ref[0], (p0, p1, p2, p3), x_ref, sems)
        total_ref[...] = jnp.zeros_like(total_ref)

    chunk = chunk_of(x_ref.shape[0])

    @pl.loop(0, x_ref.shape[0] // chunk)
    def _(i):
        here = pl.ds(pl.multiple_of(i * chunk, 16), chunk)
        plain = product(x_ref[here, :], w_ref[...])
        total_ref[here, :] += jnp.sum(mixed_ref[here, :].astype(f32) * plain, axis=1, keepdims=True)
        y_ref[here, :] = (gate_ref[here, :] * plain).astype(bf16)


def attended_in(shard, pieces, gate, mixed, weight):
    rows, half = pieces[0].shape
    columns = weight.shape[1]
    tile = min(256, columns)
    return pl.pallas_call(
        attended_in_body,
        grid_spec=pltpu.PrefetchScalarGridSpec(
            num_scalar_prefetch=1,
            grid=(columns // tile,),
            in_specs=[pl.BlockSpec(memory_space=pl.ANY)] * 4
            + [
                pl.BlockSpec((2 * rows, 1), lambda j, s: (0, 0)),
                pl.BlockSpec((2 * rows, tile), lambda j, s: (0, j)),
                pl.BlockSpec((2 * half, tile), lambda j, s: (0, j)),
            ],
            out_specs=[
                pl.BlockSpec((2 * rows, 2 * half), lambda j, s: (0, 0)),
                pl.BlockSpec((2 * rows, 1), lambda j, s: (0, 0)),
                pl.BlockSpec((2 * rows, tile), lambda j, s: (0, j)),
            ],
            scratch_shapes=[pltpu.SemaphoreType.DMA((4,))],
        ),
        out_shape=[
            jax.ShapeDtypeStruct((2 * rows, 2 * half), bf16),
            jax.ShapeDtypeStruct((2 * rows, 1), f32),
            jax.ShapeDtypeStruct((2 * rows, columns), bf16),
        ],
        compiler_params=pltpu.CompilerParams(vmem_limit_bytes=limit_of(2 * rows)),
        cost_estimate=pl.CostEstimate(
            flops=8 * rows * half * columns,
            bytes_accessed=16 * rows * half + 4 * half * columns + 8 * rows * columns,
            transcendentals=0,
        ),
        name="attended_in",
    )(shard, *pieces, gate, mixed, weight)


def rows_half_body(count, extra, shard_ref, *refs):
    lefts, weights = refs[:count], refs[count : 2 * count]
    rest = refs[2 * count :]
    if extra:
        total_ref, gate_ref, diff_ref, router_ref = rest[:4]
        rest = rest[4:]
        coef_ref = rest[2]

        @pl.when(pl.program_id(0) == 0)
        def _():
            coef_ref[...] = (1.0 - gate_ref[...]) * total_ref[...] * diff_ref[...]

    rows = rest[0].shape[0]
    chunk = chunk_of(rows)
    for t in range(2):

        @pl.loop(0, rows // chunk)
        def _(i):
            here = pl.ds(pl.multiple_of(t * rows + i * chunk, 16), chunk)
            there = pl.ds(pl.multiple_of(i * chunk, 16), chunk)
            value = sum(product_last(a[here, :], w[...]) for a, w in zip(lefts, weights))
            if extra:
                value = value + product_last(coef_ref[here, :].astype(bf16), router_ref[...])
            rest[t][there, :] = value.astype(bf16)


def rows_half(shard, mine, lefts, weights, extra=None, tile=512):
    rows, width = lefts[0].shape[0] // 2, weights[0].shape[0]
    half = width // 2
    steps = half // tile

    def at(j, s):
        return j + steps * (s[0] if mine else 1 - s[0])

    def whole_spec(array):
        return pl.BlockSpec(array.shape, lambda j, s: (0, 0))

    in_specs = [whole_spec(a) for a in lefts]
    in_specs += [pl.BlockSpec((tile, w.shape[1]), lambda j, s: (at(j, s), 0)) for w in weights]
    operands = list(lefts) + list(weights)
    out_specs = [pl.BlockSpec((rows, tile), lambda j, s: (0, j))] * 2
    out_shape = [jax.ShapeDtypeStruct((rows, half), bf16)] * 2
    if extra:
        total, gate, difference, router = extra
        in_specs += [whole_spec(total), whole_spec(gate), whole_spec(difference)]
        in_specs += [pl.BlockSpec((tile, router.shape[1]), lambda j, s: (at(j, s), 0))]
        operands += [total, gate, difference, router]
        out_specs.append(whole_spec(difference))
        out_shape.append(jax.ShapeDtypeStruct(difference.shape, f32))
    depth = sum(w.shape[1] for w in weights)
    return pl.pallas_call(
        functools.partial(rows_half_body, len(lefts), extra is not None),
        grid_spec=pltpu.PrefetchScalarGridSpec(
            num_scalar_prefetch=1, grid=(steps,), in_specs=in_specs, out_specs=out_specs
        ),
        out_shape=out_shape,
        compiler_params=pltpu.CompilerParams(vmem_limit_bytes=limit_of(2 * rows)),
        cost_estimate=pl.CostEstimate(
            flops=4 * rows * half * depth,
            bytes_accessed=4 * rows * depth + 2 * half * depth + 4 * rows * half,
            transcendentals=0,
        ),
        name="rows_mine" if mine else "rows_theirs",
    )(shard, *operands)


def prepare_body(
    capacity, scalars, tokens_ref, gain_ref, order_ref, attn_ref, mlp_ref, segment_ref, parent_ref,
    block_ref, attn_pack_ref, mlp_pack_ref, tile_ref,
):
    width = tokens_ref.shape[2]
    count = tokens_ref.shape[1]
    values = tokens_ref[0].astype(f32)
    scales = lax.rsqrt(jnp.mean(values * values, axis=1, keepdims=True) + epsilon)
    block_ref[:, :width] = (values * scales * gain_ref[...]).astype(bf16)

    ranks = order_ref[0].astype(f32)
    pairs = lax.broadcasted_iota(jnp.int32, (2 * count, count), 0)
    owners = lax.broadcasted_iota(jnp.int32, (2 * count, count), 1)
    turns = [(pairs == 2 * owners + k).astype(f32) for k in range(2)]
    rank_rows = [product(ranks, turn) for turn in turns]
    rank_columns = [
        lax.dot_general(turn, ranks, (((0,), (1,)), ((), ())), preferred_element_type=f32)
        for turn in turns
    ]
    same = (
        lax.broadcasted_iota(jnp.int32, (count, count), 0)
        == lax.broadcasted_iota(jnp.int32, (count, count), 1)
    ).astype(f32)
    places = lax.broadcasted_iota(jnp.int32, attn_pack_ref.shape, 0).astype(f32)
    tile_ref[...] = jnp.zeros_like(tile_ref)
    for at, (route_ref, pack_ref) in enumerate(((attn_ref, attn_pack_ref), (mlp_ref, mlp_pack_ref))):
        routes = route_ref[0].astype(f32)
        rows = product_first(routes, same)
        hit = None
        for k in range(2):
            route = rows[k : k + 1]
            slot = jnp.zeros((1, count), f32)
            for other in range(2):
                earlier = (routes[:, other : other + 1] == route) & (
                    rank_columns[other] < rank_rows[k]
                )
                slot = slot + jnp.sum(earlier.astype(f32), axis=0, keepdims=True)
            slot = jnp.minimum(slot, float(capacity))
            tile_ref[4 * at + 2 * k : 4 * at + 2 * k + 1, :] = route
            tile_ref[4 * at + 2 * k + 1 : 4 * at + 2 * k + 2, :] = slot
            code = jnp.where(slot < capacity, route * capacity + slot, -1.0)
            here = places == code
            hit = here if hit is None else hit | here
        pack_ref[...] = hit.astype(bf16)
    tile_ref[8:9, :] = segment_ref[...].astype(f32)
    tile_ref[9:10, : parent_ref.shape[1]] = parent_ref[...].astype(f32)
    block_ref[:, width:] = jnp.zeros((count, block_ref.shape[1] - width), bf16)
    block_ref[:16, width : width + count] = tile_ref[...].astype(bf16)


def prepare(place, tokens, gain, order, attn_routes, mlp_routes, segments, parents, experts, capacity):
    _, count, width = tokens.shape

    def whole_spec(array):
        return pl.BlockSpec(array.shape, lambda i, s: (0,) * array.ndim)

    pack = jax.ShapeDtypeStruct((experts * capacity, count), bf16)
    return pl.pallas_call(
        functools.partial(prepare_body, capacity),
        grid_spec=pltpu.PrefetchScalarGridSpec(
            num_scalar_prefetch=1,
            grid=(1,),
            in_specs=[whole_spec(a) for a in (tokens, gain, order, attn_routes, mlp_routes)]
            + [pl.BlockSpec((1, count), lambda i, s: (0, s[0])), whole_spec(parents)],
            out_specs=[
                pl.BlockSpec((count, width + 128), lambda i, s: (0, 0)),
                pl.BlockSpec(pack.shape, lambda i, s: (0, 0)),
                pl.BlockSpec(pack.shape, lambda i, s: (0, 0)),
            ],
            scratch_shapes=[pltpu.VMEM((16, count), f32)],
        ),
        out_shape=[jax.ShapeDtypeStruct((count, width + 128), bf16), pack, pack],
        compiler_params=pltpu.CompilerParams(vmem_limit_bytes=24 * 2**20),
        name="prepare",
    )(place, tokens, gain, order, attn_routes, mlp_routes, segments, parents)


def difference_of(expert, other, experts):
    range_of = lax.broadcasted_iota(jnp.int32, (other.shape[0], experts), 1).astype(f32)
    return (range_of == expert).astype(f32) - (range_of == other).astype(f32)


def front_body(
    capacity, scalars, rows_ref, marks_ref, router_ref, key_hbm, value_hbm, got_key_hbm, got_value_hbm, *refs
):
    shared_ref, picked_ref, gate_ref, bias_ref, attn_diff_ref, mlp_diff_ref, weight, sems = refs[-8:]
    piece = weight.shape[1] // 2
    heads = piece // HEAD

    step = pl.program_id(0)

    def fetch(sources, at):
        for h in range(heads):
            for i, source in enumerate(sources):
                from_here = source.at[:, pl.ds(pl.multiple_of(at + h * HEAD, HEAD), HEAD)]
                place = weight.at[:, pl.ds((2 * h + i) * HEAD, HEAD)]
                pltpu.make_async_copy(from_here, place, sems.at[h]).start()

    @pl.when((step == 0) & (scalars[0] == 1))
    def _():
        fetch((key_hbm, value_hbm), scalars[1] * piece)

    @pl.when((step == 0) & (scalars[0] == 0))
    def _():
        fetch((got_key_hbm, got_value_hbm), 0)

    count = rows_ref.shape[1]
    width = weight.shape[0]
    blocks = marks_ref.shape[0]
    rows = jnp.concatenate([rows_ref[0, :, :width], rows_ref[1, :, :width]])
    expert = scalars[2].astype(f32)
    index = lax.broadcasted_iota(jnp.int32, (2 * capacity, count), 0)
    lanes = lax.broadcasted_iota(jnp.int32, (2 * capacity, count), 1).astype(f32)
    first = index < capacity
    slots = jnp.where(first, index, index - capacity).astype(f32)
    upper = marks_ref[2 * step].astype(f32)
    lower = marks_ref[2 * step + 1].astype(f32)

    def mark(i):
        return jnp.where(first, upper[i : i + 1, :count], lower[i : i + 1, :count])

    def total(values):
        return jnp.sum(values, axis=1, keepdims=True)

    def hits_of(at):
        hits = [(mark(at + 2 * k) == expert) & (mark(at + 2 * k + 1) == slots) for k in range(2)]
        other = total(jnp.where(hits[0], mark(at + 2), 0.0) + jnp.where(hits[1], mark(at), 0.0))
        return hits[0] | hits[1], other

    experts = attn_diff_ref.shape[1]
    mlp_diff_ref[...] = difference_of(expert, hits_of(4)[1], experts)
    hit, other = hits_of(0)
    difference = difference_of(expert, other, experts)
    attn_diff_ref[...] = difference

    own = total(jnp.where(hit, mark(8), 0.0))
    parents = mark(9)
    one = total(jnp.where(lanes == own, parents, 0.0))
    two = total(jnp.where(lanes == one, parents, 0.0))
    start = jnp.where(first[:, :1], 2 * step * count, (2 * step + 1) * count).astype(f32)
    place = total(jnp.where(hit, lanes, 0.0)) + start
    for j in range(blocks):
        keys = marks_ref[j, 8:9, :count].astype(f32)
        seen = ((keys == own) | (keys == one) | (keys == two)) & (lanes + float(j * count) <= place)
        bias_ref[:, j * count : (j + 1) * count] = jnp.where(seen, 0.0, negative).astype(bf16)

    both = jnp.concatenate([(hit & first).astype(bf16), (hit & ~first).astype(bf16)], axis=1)
    picked = product(both, rows).astype(bf16)
    picked_ref[...] = picked
    logits = product(picked, router_ref[...])
    gate_ref[...] = jax.nn.sigmoid(total(logits * difference))

    @pl.when(step == 0)
    def _():
        for h in range(heads):
            here = pl.ds(2 * h * HEAD, 2 * HEAD)
            pltpu.make_async_copy(weight.at[:, here], weight.at[:, here], sems.at[h]).wait()
            shared_ref[:, here] = product(rows, weight[:, here]).astype(bf16)

    @pl.when(step > 0)
    def _():
        shared_ref[...] = product(rows, weight[...]).astype(bf16)


def front(tree, held, scalars, blocks_of, router, key_weight, value_weight, got_key, got_value, capacity):
    blocks, count, columns = blocks_of.shape
    width, piece = got_key.shape
    experts = router.shape[1]
    length = blocks * count
    rows = blocks * capacity
    steps = blocks // 2
    pinned = pl.BlockSpec(memory_space=pltpu.HBM)

    def out_spec(height, columns):
        return pl.BlockSpec((height, columns), lambda i, s: (tree * steps + i, 0))

    pair = 2 * capacity
    return pl.pallas_call(
        functools.partial(front_body, capacity),
        grid_spec=pltpu.PrefetchScalarGridSpec(
            num_scalar_prefetch=1,
            grid=(steps,),
            in_specs=[
                pl.BlockSpec((2, count, columns), lambda i, s: (i, 0, 0)),
                pl.BlockSpec((blocks, 16, 128), lambda i, s: (0, 0, width // 128)),
                pl.BlockSpec(router.shape, lambda i, s: (0, 0)),
            ]
            + [pinned] * 4
            + [pl.BlockSpec(memory_space=pl.ANY)] * len(held),
            out_specs=[
                out_spec(2 * count, 2 * piece),
                out_spec(pair, width),
                out_spec(pair, 1),
                out_spec(pair, length),
                out_spec(pair, experts),
                out_spec(pair, experts),
            ],
            scratch_shapes=[
                pltpu.VMEM((width, 2 * piece), bf16),
                pltpu.SemaphoreType.DMA((piece // HEAD,)),
            ],
        ),
        out_shape=[
            jax.ShapeDtypeStruct((2 * length, 2 * piece), bf16),
            jax.ShapeDtypeStruct((2 * rows, width), bf16),
            jax.ShapeDtypeStruct((2 * rows, 1), f32),
            jax.ShapeDtypeStruct((2 * rows, length), bf16),
            jax.ShapeDtypeStruct((2 * rows, experts), f32),
            jax.ShapeDtypeStruct((2 * rows, experts), f32),
        ],
        input_output_aliases={8 + i: i for i in range(len(held))},
        compiler_params=pltpu.CompilerParams(vmem_limit_bytes=limit_of(2 * rows)),
        cost_estimate=pl.CostEstimate(
            flops=4 * length * width * piece,
            bytes_accessed=2 * length * width + 4 * width * piece,
            transcendentals=0,
        ),
        name="front",
    )(scalars, blocks_of, blocks_of, router, key_weight, value_weight, got_key, got_value, *held)


def shared_out_body(steps, scalars, sums_ref, key_ref, value_ref, got_key_ref, got_value_ref, *outs):
    step = pl.program_id(0)
    sums = sums_ref[...]
    heads = sums.shape[2] // (2 * HEAD)

    def part(t, i):
        return jnp.concatenate(
            [sums[t, :, (2 * h + i) * HEAD : (2 * h + i + 1) * HEAD] for h in range(heads)], axis=1
        )

    def fill(pair, keys, values):
        for t in range(2):
            value = product_last(part(t, 0), keys[...]) + product_last(part(t, 1), values[...])
            pair[t][...] = value.astype(bf16)

    for side in range(2):
        for local in range(2):
            first = step < steps // 2 if side == 0 else step >= steps // 2

            @pl.when(first & (scalars[1] == local))
            def _():
                pair = (outs[side], outs[2 + side])
                if local:
                    fill(pair, key_ref, value_ref)
                else:
                    fill(pair, got_key_ref, got_value_ref)


def shared_out(scalars, sums, key_weight, value_weight, got_key, got_value, tile=512):
    _, rows, _ = sums.shape
    width, piece = got_key.shape
    half, steps = width // 2, width // tile

    def at(j, s):
        return lax.rem(j + steps // 2 * (1 - s[0]), steps)

    local = pl.BlockSpec((tile, piece), lambda j, s: (at(j, s), s[2]))
    sent = pl.BlockSpec((tile, piece), lambda j, s: (at(j, s), 0))
    theirs = pl.BlockSpec((rows, tile), lambda j, s: (0, jnp.minimum(j, steps // 2 - 1)))
    mine = pl.BlockSpec((rows, tile), lambda j, s: (0, jnp.maximum(j - steps // 2, 0)))
    return pl.pallas_call(
        functools.partial(shared_out_body, steps),
        grid_spec=pltpu.PrefetchScalarGridSpec(
            num_scalar_prefetch=1,
            grid=(steps,),
            in_specs=[pl.BlockSpec(sums.shape, lambda j, s: (0, 0, 0)), local, local, sent, sent],
            out_specs=[theirs, mine, theirs, mine],
        ),
        out_shape=[jax.ShapeDtypeStruct((rows, half), bf16)] * 4,
        compiler_params=pltpu.CompilerParams(vmem_limit_bytes=limit_of(2 * rows)),
        cost_estimate=pl.CostEstimate(
            flops=8 * rows * width * piece,
            bytes_accessed=8 * width * piece + 8 * rows * width,
            transcendentals=0,
        ),
        name="shared_out",
    )(scalars, sums, key_weight, value_weight, got_key, got_value)


def per_device(
    tokens,
    cotangent,
    attn_gain,
    mlp_gain,
    key_weight,
    value_weight,
    query_weight,
    output_weight,
    attn_router,
    gate_weight,
    up_weight,
    down_weight,
    mlp_router,
    segment_ids,
    parent_ids,
    attn_routes,
    mlp_routes,
    slot_order,
):
    count, width = tokens.shape[1:]
    half = width // 2
    piece = query_weight.shape[1]
    experts = attn_router.shape[1]
    blocks = lax.axis_size("dp")
    members = blocks // experts
    capacity = min(count, 5 * count * attn_routes.shape[2] // (4 * experts))
    length, parents = segment_ids.shape[1], parent_ids.shape[1]
    tiles = max(2, length // 512)
    dp, core, shard = lax.axis_index("dp"), lax.axis_index("expert"), lax.axis_index("shard")
    expert, member = dp // members, dp % members

    def my_half(values):
        return lax.dynamic_slice_in_dim(values, shard * half, half, values.ndim - 1)

    def whole(mine):
        got = swap(mine, "shard")
        first = shard == 0
        return jnp.concatenate(
            [jnp.where(first, mine, got), jnp.where(first, got, mine)], axis=mine.ndim - 1
        )

    block, attn_pack, mlp_pack = prepare(
        jnp.reshape(dp, (1,)).astype(jnp.int32),
        tokens,
        attn_gain[None],
        slot_order,
        attn_routes,
        mlp_routes,
        segment_ids,
        parent_ids,
        experts,
        capacity,
    )
    own_blocks, arrivals = ring_gather(block, "dp", blocks, 1)

    heads_at = (member * 2 + core) * 2 + shard
    holder = (member * 2 + core) // members
    offset = holder * 2 * members
    names = ("dp", "expert", "shard")
    sends = []
    for d in range(blocks):
        for c in range(2):
            at = (d * 2 + c) * 2
            source = ((d % members) * 2 + c) // members
            sends.append((at + source, at + 1 - source))
    partner_at = (member * 2 + core) * 2 + 1 - shard

    def partner_columns(weight):
        columns = lax.dynamic_slice_in_dim(weight, (partner_at - offset) * piece, piece, 1)
        return lax.ppermute(after(columns, block), names, sends)

    local = (shard == holder).astype(jnp.int32)
    local_at = local * (heads_at - offset)
    got_key, got_value = partner_columns(key_weight), partner_columns(value_weight)
    own_blocks, got_key, got_value = lax.optimization_barrier((own_blocks, got_key, got_value))
    tree_blocks = [own_blocks, swap(own_blocks, "expert")]

    shard_index = jnp.reshape(shard, (1,)).astype(jnp.int32)

    def pack_rows(values, pack):
        packed = product(pack, values).astype(bf16).reshape(experts, 1, capacity, half)
        packed = jnp.broadcast_to(packed, (experts, members, capacity, half))
        return packed.reshape(blocks, capacity, half)

    def dispatch(packed, work=None, begin=None):
        arrived = lax.all_to_all(packed, "dp", 0, 0, tiled=True)
        done = []
        if work:
            arrived, *done = lax.optimization_barrier((arrived, *work(packed)))
        arrived = arrived.reshape(blocks * capacity, half)
        other = swap(arrived, "expert")
        got = swap(arrived, "shard")
        begun = []
        if begin:
            got, *begun = lax.optimization_barrier((got, *begin(arrived, other)))
        return [arrived, got, other, swap(got, "expert")], done, begun

    def join_ends(sides, work=None):
        own, other, *_ = sides(False, None)
        theirs = (own.astype(f32) + swap(other, "expert").astype(f32)).astype(bf16)
        back = swap(theirs, "shard")
        own, other, *rest = sides(True, theirs)
        done = []
        if work:
            back, *done = lax.optimization_barrier((back, *work(theirs)))
        total = own.astype(f32) + swap(other, "expert").astype(f32) + back.astype(f32)
        return total, rest, done, theirs, own

    def sum_tokens(back, pack):
        if members > 1:
            back = back.reshape(experts, members, capacity, half).astype(f32)
            back = jnp.sum(back, axis=1).astype(bf16)
        return product_first(pack, back.reshape(experts * capacity, half))

    def send_back(joined, work=None):
        back = lax.all_to_all(joined, "dp", 0, 0, tiled=True)
        done = []
        if work:
            back, *done = lax.optimization_barrier((back, *work(joined)))
        return back, done

    def for_tokens(joined):
        return joined.astype(bf16).reshape(blocks, capacity, half)

    grad_half = my_half(cotangent[0])
    grad_packed = after(pack_rows(grad_half, mlp_pack), arrivals[2])
    grad_arrived = lax.all_to_all(grad_packed, "dp", 0, 0, tiled=True)
    grad_arrived = grad_arrived.reshape(blocks * capacity, half)
    scalars = jnp.stack([local, local_at, expert]).astype(jnp.int32)
    held = ()
    for t in range(2):
        held = front(
            t, held, scalars, tree_blocks[t], attn_router, key_weight, value_weight, got_key, got_value, capacity
        )
        if t == 0:
            grad_got = swap(after(grad_arrived, held[2]), "shard")
    shared, rows, attn_gate, bias, attn_difference, mlp_difference = held
    queries = product(rows, query_weight).astype(bf16)
    mixed, log_total = attend(queries, shared, bias, attn_gate, tiles)
    mixed, grad_got = lax.optimization_barrier((mixed, grad_got))
    grad_pieces = (grad_arrived, grad_got, swap(grad_arrived, "expert"), swap(grad_got, "expert"))

    def attn_sides(mine, event):
        return rows_half(shard_index, mine, [after(mixed, event)], [output_weight])

    def plain_work(event):
        return plain_in(shard_index, after(grad_pieces, event), down_weight)

    attn_joined, _, (grad_rows, plain_grad), *_ = join_ends(attn_sides, plain_work)
    back = send_back(for_tokens(attn_joined))[0]
    inputs = tokens[0].astype(f32)
    attn_scale = lax.rsqrt(jnp.mean(inputs * inputs, axis=1, keepdims=True) + epsilon)
    middle = my_half(inputs) + sum_tokens(back, attn_pack)

    def feature_mean(values):
        part = jnp.sum(values, axis=1, keepdims=True)
        return (part + swap(part, "shard")) / width

    mlp_scale = lax.rsqrt(feature_mean(middle * middle) + epsilon)
    half_gain = my_half(mlp_gain)
    mlp_normed = (middle * mlp_scale * half_gain).astype(bf16)

    def begin(own, other):
        return expert_begin(shard_index, own, other, gate_weight, up_weight)

    mlp_pieces, _, begun = dispatch(pack_rows(mlp_normed, mlp_pack), None, begin)
    mlp_rows, mlp_gate, mlp_total, gated_hidden, gate_pre_grad, up_pre_grad = expert_in(
        shard_index, mlp_pieces, mlp_router, mlp_difference, plain_grad, begun, gate_weight, up_weight
    )

    def mlp_sides(mine, event):
        return rows_half(
            shard_index,
            mine,
            after([gate_pre_grad, up_pre_grad], event),
            [gate_weight, up_weight],
            (mlp_total, mlp_gate, mlp_difference, mlp_router),
        )

    def down_work(event):
        return [product_first(after(grad_rows, event), gated_hidden)]

    row_joined, (mlp_coefs,), (down_grad,), *_ = join_ends(mlp_sides, down_work)
    row_joined = for_tokens(row_joined)

    def term_half(mine, event):
        return rows_half(shard_index, mine, [after(gated_hidden, event)], [down_weight])

    def gate_work(event):
        gate_grad = product_first(after(mlp_rows, event), gate_pre_grad)
        own, other = term_half(False, gate_grad)
        theirs = own.astype(f32) + swap(other, "expert").astype(f32)
        return [gate_grad, theirs.astype(bf16)]

    back, (gate_grad, term_theirs) = send_back(row_joined, gate_work)
    mlp_normed_grad = sum_tokens(back, mlp_pack)

    mlp_n = middle * mlp_scale
    weighted = mlp_normed_grad * half_gain
    mlp_gain_part = jnp.sum(mlp_normed_grad * mlp_n, axis=0)
    middle_grad = grad_half.astype(f32) + mlp_scale * (
        weighted - mlp_n * feature_mean(weighted * mlp_n)
    )
    low_grad = middle_grad.astype(bf16)

    def up_work(event):
        up_grad = product_first(after(mlp_rows, event), up_pre_grad)
        router_part = product_first(mlp_coefs, after(mlp_rows, event).astype(f32))
        term_back = swap(after(term_theirs, event), "shard")
        own, other = term_half(True, event)
        total = own.astype(f32) + swap(other, "expert").astype(f32) + term_back.astype(f32)
        return [up_grad, router_part, for_tokens(total)]

    term_pieces, (up_grad, mlp_router_part, term_joined), _ = dispatch(
        pack_rows(low_grad, attn_pack), up_work
    )
    term_back = lax.all_to_all(after(term_joined, term_pieces[0]), "dp", 0, 0, tiled=True)
    term_rows, attn_total, attended_grad = attended_in(
        shard_index, term_pieces, attn_gate, mixed, output_weight
    )
    query_rows_grad, held = attend_back(queries, shared, bias, log_total, attended_grad, tiles)
    held, term_back = lax.optimization_barrier((held, term_back))
    part = length // experts
    held = held.reshape(2, experts, part, 2 * piece)
    key_sums, first_key_sums = ring_scatter(held, experts, members)
    key_sums = key_sums.astype(bf16)

    def input_sides(mine, event):
        return rows_half(
            shard_index,
            mine,
            [after(query_rows_grad, first_key_sums if event is None else event)],
            [query_weight],
            (attn_total, attn_gate, attn_difference, attn_router),
        )

    def query_work(event):
        query_grad = product_first(after(rows, event), query_rows_grad)
        return [query_grad, product_first(after(term_rows, event), mixed)]

    input_joined, (attn_coefs,), (query_grad, output_grad), *_ = join_ends(input_sides, query_work)
    input_joined = for_tokens(input_joined)

    all_sums, arrivals = ring_gather(key_sums.reshape(2 * part, 2 * piece), "dp", experts, members)
    all_sums = all_sums.reshape(2 * length, 2 * piece)
    back = send_back(after(input_joined, key_sums))[0]
    normed_grad = sum_tokens(after(back, arrivals[2]), attn_pack)
    layer_out = whole((middle + sum_tokens(term_back, mlp_pack)).astype(bf16))[None]
    attn_router_part = product_first(attn_coefs, after(rows, arrivals[0]).astype(f32))
    slots = width // experts
    normed_part = jnp.stack(
        [
            lax.dynamic_slice_in_dim(own, expert * slots, slots, 2).reshape(experts, part, slots)
            for own in tree_blocks
        ],
        axis=1,
    ).reshape(2 * length, slots)
    weight_sums = product_first(normed_part, all_sums)

    scalars = jnp.stack([shard, local, local_at]).astype(jnp.int32)
    parts = shared_out(
        scalars,
        after(key_sums, arrivals[0]),
        key_weight,
        value_weight,
        got_key,
        got_value,
    )
    theirs = parts[0].astype(f32) + swap(parts[2], "expert").astype(f32)
    back = swap(theirs.astype(bf16), "shard")
    shared = parts[1].astype(f32) + swap(parts[3], "expert").astype(f32) + back.astype(f32)
    if members > 1:
        groups = [[e * members + m for m in range(members)] for e in range(experts)]
        shared = lax.psum_scatter(
            shared, "dp", scatter_dimension=0, axis_index_groups=groups, tiled=True
        )
    normed_grad = normed_grad + shared

    attn_n = my_half(inputs) * attn_scale
    weighted = normed_grad * my_half(attn_gain)
    attn_gain_part = jnp.sum(normed_grad * attn_n, axis=0)
    tokens_grad = middle_grad + attn_scale * (weighted - attn_n * feature_mean(weighted * attn_n))
    got = swap(tokens_grad.astype(bf16), "shard").astype(f32)
    tokens_grad = jnp.concatenate(
        [jnp.where(shard == 0, tokens_grad, got), jnp.where(shard == 0, got, tokens_grad)], axis=1
    )[None]

    features = width // (2 * blocks)
    heads = piece // HEAD
    pieces = weight_sums.astype(bf16).reshape(members, 2, features, 2 * piece)
    if members > 1:
        groups = [[e * members + m for m in range(members)] for e in range(experts)]
        pieces = lax.all_to_all(pieces, "dp", 0, 0, axis_index_groups=groups, tiled=True)
    pieces = pair_all_to_all(pieces.transpose(1, 0, 2, 3), "expert")
    pieces = pieces.transpose(1, 0, 2, 3).reshape(2, members, features, 2 * piece)
    pieces = pair_all_to_all(pieces, "shard").reshape(2, members, features, heads, 2, HEAD)
    pieces = pieces.transpose(4, 2, 1, 0, 3, 5).reshape(2, features, -1).astype(f32)

    def spread(values):
        return lax.dynamic_update_slice(jnp.zeros((1, width), f32), values[None], (0, shard * half))

    small = [attn_router_part, mlp_router_part, spread(attn_gain_part), spread(mlp_gain_part)]
    small = jnp.pad(jnp.concatenate(small), ((0, 6), (0, 0)))
    small = small + swap(after(small, weight_sums), "shard")
    small = small.reshape(-1, blocks, 2, features).transpose(2, 1, 0, 3)
    mine = lax.dynamic_index_in_dim(small, core, 0, keepdims=False)
    theirs = lax.dynamic_index_in_dim(small, 1 - core, 0, keepdims=False)
    mine = mine + swap(theirs, "expert")
    small = jnp.sum(lax.all_to_all(mine, "dp", 0, 0, tiled=True), axis=0)
    return (
        layer_out,
        tokens_grad,
        small[2 * experts],
        small[2 * experts + 1],
        pieces[0],
        pieces[1],
        query_grad,
        output_grad,
        small[:experts].T,
        gate_grad,
        up_grad,
        down_grad,
        small[experts : 2 * experts].T,
    )


def solution(mesh):
    tree = P("expert", "dp", None)
    columns = P(None, ("dp", "expert", "shard"))
    spread = P(("dp", "expert"), None)
    in_specs = (
        tree,
        tree,
        P(),
        P(),
        P(None, "shard"),
        P(None, "shard"),
        columns,
        columns,
        P(),
        columns,
        columns,
        columns,
        P(),
        P("expert", None),
        P("expert", None),
        tree,
        tree,
        tree,
    )
    out_specs = (
        tree,
        tree,
        P(("dp", "expert")),
        P(("dp", "expert")),
        P(("dp", "expert"), "shard"),
        P(("dp", "expert"), "shard"),
        columns,
        columns,
        spread,
        columns,
        columns,
        columns,
        spread,
    )
    return jax.shard_map(
        per_device, mesh=mesh, in_specs=in_specs, out_specs=out_specs, check_vma=False
    )
```

```python
import functools

import jax
import jax.numpy as jnp
from jax import lax
from jax.experimental import pallas as pl
from jax.experimental.pallas import tpu as pltpu
from jax.sharding import PartitionSpec as P

HEAD = 128

epsilon = 1e-06
negative = -1e30
ATTN, MLP, GATE = 0, 32, 64
scale = HEAD ** (-0.5)
bf16 = jnp.bfloat16
f32 = jnp.float32


def product(former, latter):
    return jnp.dot(former, latter, preferred_element_type=f32)


def product_last(former, latter):
    return lax.dot_general(
        former, latter, (((1,), (1,)), ((), ())), preferred_element_type=f32
    )


def product_first(former, latter):
    return lax.dot_general(
        former, latter, (((0,), (0,)), ((), ())), preferred_element_type=f32
    )


def limit_of(rows):
    return min(56, max(40, rows * 24 // 640)) * 2**20


def swap(values, axis):
    return lax.ppermute(values, axis, [(0, 1), (1, 0)])


def pair_all_to_all(parts, axis):
    me = lax.axis_index(axis)
    mine = lax.dynamic_index_in_dim(parts, me, 0, keepdims=False)
    theirs = lax.dynamic_index_in_dim(parts, 1 - me, 0, keepdims=False)
    got = swap(theirs, axis)
    first = me == 0
    return jnp.stack([jnp.where(first, mine, got), jnp.where(first, got, mine)])


def ring_order(count):
    return list(range(0, count, 2)) + list(range(1, count, 2))[::-1]


def ring_member(place, count):
    place = lax.rem(place + 2 * count, count)
    return jnp.where(place < count // 2, 2 * place, 2 * (count - place) - 1)


def ring_place(member, count):
    return jnp.where(member % 2 == 0, member // 2, count - (member + 1) // 2)


def empty(shape, dtype):
    return pl.pallas_call(
        lambda ref: None,
        out_shape=jax.ShapeDtypeStruct(shape, dtype),
        out_specs=pl.BlockSpec(memory_space=pl.ANY),
        name="empty",
    )()


def pinned(values, work, event):
    *values, made = lax.optimization_barrier((*values, work(event) if work else []))
    return values, made


def ring_gather(block, axis, count, stride, works=()):
    works = list(works) + [None] * (count // 2)
    order = ring_order(count)
    member = lax.axis_index(axis) // stride
    place = ring_place(member, count)
    right, left = ring_moves(order, 1, stride), ring_moves(order, -1, stride)
    rows, columns = block.shape
    half = rows // 2
    out = empty((count, rows, columns), block.dtype)

    def put(out, piece, source, row):
        return lax.dynamic_update_slice(out, piece[None], (source, row, 0))

    out = put(out, block, member, 0)
    forward, backward = block, block
    results = []
    for step in range(1, count // 2 + 1):
        last = step == count // 2
        if last:
            forward, backward = forward[:half], backward[half:]
        event = forward
        forward = lax.ppermute(forward, axis, right)
        backward = lax.ppermute(backward, axis, left)
        (forward, backward), made = pinned((forward, backward), works[step - 1], event)
        results.append(made)
        out = put(out, forward, ring_member(place - step, count), 0)
        out = put(out, backward, ring_member(place + step, count), half if last else 0)
    return out, results


def ring_moves(order, by, stride):
    count = len(order)
    return [
        (order[i] * stride + j, order[(i + by) % count] * stride + j)
        for i in range(count)
        for j in range(stride)
    ]


def after(values, *events):
    if events[0] is None:
        return values
    return lax.optimization_barrier((values,) + events)[0]


def ring_scatter(parts, count, stride, works=()):
    works = list(works) + [None] * (count // 2)
    order = ring_order(count)
    place = ring_place(lax.axis_index("dp") // stride, count)
    right, left = ring_moves(order, 1, stride), ring_moves(order, -1, stride)
    far = count // 2

    def part(offset):
        return lax.dynamic_index_in_dim(parts, ring_member(place + offset, count), 0, keepdims=False)

    def added(sent, offset, first):
        own = part(offset).astype(f32)
        if first is not None:
            sent = jnp.pad(sent, ((first, 1 - first), (0, 0), (0, 0)))
        return (own + sent.astype(f32)).astype(bf16)

    forward, backward = part(far)[:1], part(-far)[1:]
    results = []
    for step in range(far):
        event = forward
        forward = lax.ppermute(forward, "dp", right)
        backward = lax.ppermute(backward, "dp", left)
        (forward, backward), made = pinned((forward, backward), works[step], event)
        results.append(made)
        offset = far - 1 - step
        if offset:
            forward = added(forward, offset, 0 if step == 0 else None)
            backward = added(backward, -offset, 1 if step == 0 else None)
    return part(0).astype(f32) + forward.astype(f32) + backward.astype(f32), results


def attend_body(tiles, keys_per_tile, q_ref, k_ref, v_ref, bias_ref, info_ref, out_ref, total_ref):
    rows = q_ref.shape[0] // tiles
    lanes = lax.broadcasted_iota(jnp.int32, (rows, 128), 1)
    for tile in range(tiles):
        here = pl.ds(tile * rows, rows)
        keys = (tile + 1) * keys_per_tile
        scores = product_last(q_ref[here, :], k_ref[:keys, :]) * scale
        scores = scores + bias_ref[here, :keys].astype(f32)
        highest = jnp.max(scores, axis=1, keepdims=True)
        expo = jnp.exp(scores - highest)
        summed = jnp.sum(expo, axis=1, keepdims=True)
        mixed = product(expo.astype(bf16), v_ref[:keys, :]) * (1.0 / summed)
        mixed = mixed.astype(bf16).astype(f32)
        out_ref[here, :] = (mixed * info_ref[here, GATE : GATE + 1]).astype(bf16)
        total = highest + jnp.log(summed)
        total_ref[here, :] = jnp.where(lanes == pl.program_id(1), total, total_ref[here, :])


def attend(queries, shared, bias, info, tiles):
    rows, columns = queries.shape[0] // 2, queries.shape[1]
    length = shared.shape[0] // 2
    heads = columns // HEAD
    return pl.pallas_call(
        functools.partial(attend_body, tiles, length // tiles),
        grid=(2, heads),
        in_specs=[
            pl.BlockSpec((rows, HEAD), lambda t, h: (t, h)),
            pl.BlockSpec((length, HEAD), lambda t, h: (t, 2 * h)),
            pl.BlockSpec((length, HEAD), lambda t, h: (t, 2 * h + 1)),
            pl.BlockSpec((rows, length), lambda t, h: (t, 0)),
            pl.BlockSpec((rows, 128), lambda t, h: (t, 0)),
        ],
        out_specs=[
            pl.BlockSpec((rows, HEAD), lambda t, h: (t, h)),
            pl.BlockSpec((rows, 128), lambda t, h: (t, 0)),
        ],
        out_shape=[
            jax.ShapeDtypeStruct((2 * rows, columns), bf16),
            jax.ShapeDtypeStruct((2 * rows, 128), f32),
        ],
        compiler_params=pltpu.CompilerParams(vmem_limit_bytes=limit_of(2 * rows)),
        cost_estimate=pl.CostEstimate(
            flops=8 * rows * length * columns,
            bytes_accessed=4 * (rows * length + 2 * length * columns),
            transcendentals=2 * rows * length * heads,
        ),
        name="attend",
    )(queries, shared, shared, bias, info)


def attend_back_body(
    tiles, keys_per_tile, q_ref, k_ref, v_ref, bias_ref, total_ref, grad_ref, dq_ref, both_ref, dk_sum, dv_sum
):
    rows = q_ref.shape[0] // tiles
    lanes = lax.broadcasted_iota(jnp.int32, (rows, 128), 1)
    dk_sum[...] = jnp.zeros_like(dk_sum)
    dv_sum[...] = jnp.zeros_like(dv_sum)
    for tile in range(tiles):
        here = pl.ds(tile * rows, rows)
        keys = (tile + 1) * keys_per_tile
        query, grad = q_ref[here, :], grad_ref[here, :]
        scores = product_last(query, k_ref[:keys, :]) * scale
        scores = scores + bias_ref[here, :keys].astype(f32)
        total = jnp.where(lanes == pl.program_id(1), total_ref[here, :], 0.0)
        probs = jnp.exp(scores - jnp.sum(total, axis=1, keepdims=True))
        prob_grad = product_last(grad, v_ref[:keys, :])
        inner = jnp.sum(probs * prob_grad, axis=1, keepdims=True)
        score_grad = (probs * (prob_grad - inner) * scale).astype(bf16)
        dq_ref[here, :] = product(score_grad, k_ref[:keys, :]).astype(bf16)
        dk_sum[:keys, :] += product_first(score_grad, query)
        dv_sum[:keys, :] += product_first(probs.astype(bf16), grad)
    both_ref[0, 0] = dk_sum[...].astype(bf16)
    both_ref[1, 0] = dv_sum[...].astype(bf16)


def attend_back(queries, shared, bias, total, grads, tiles):
    rows, columns = queries.shape[0] // 2, queries.shape[1]
    length = shared.shape[0] // 2
    heads = columns // HEAD
    row_spec = pl.BlockSpec((rows, HEAD), lambda t, h: (t, h))
    return pl.pallas_call(
        functools.partial(attend_back_body, tiles, length // tiles),
        grid=(2, heads),
        in_specs=[
            row_spec,
            pl.BlockSpec((length, HEAD), lambda t, h: (t, 2 * h)),
            pl.BlockSpec((length, HEAD), lambda t, h: (t, 2 * h + 1)),
            pl.BlockSpec((rows, length), lambda t, h: (t, 0)),
            pl.BlockSpec((rows, 128), lambda t, h: (t, 0)),
            row_spec,
        ],
        out_specs=[row_spec, pl.BlockSpec((2, 1, length, HEAD), lambda t, h: (h, t, 0, 0))],
        out_shape=[
            jax.ShapeDtypeStruct((2 * rows, columns), bf16),
            jax.ShapeDtypeStruct((2 * heads, 2, length, HEAD), bf16),
        ],
        scratch_shapes=[pltpu.VMEM((length, HEAD), f32), pltpu.VMEM((length, HEAD), f32)],
        compiler_params=pltpu.CompilerParams(vmem_limit_bytes=60 * 2**20),
        cost_estimate=pl.CostEstimate(
            flops=20 * rows * length * columns,
            bytes_accessed=4 * (rows * length + 4 * length * columns),
            transcendentals=2 * rows * length * heads,
        ),
        name="attend_back",
    )(queries, shared, shared, bias, total, grads)


def chunk_of(rows):
    return 640 if rows % 640 == 0 else rows


def assemble(shard, pieces, out_ref, sems):
    rows, half = pieces[0].shape
    copies = []
    for i, piece in enumerate(pieces):
        at = pl.multiple_of((shard if i % 2 == 0 else 1 - shard) * half, 128)
        place = out_ref.at[pl.ds(i // 2 * rows, rows), pl.ds(at, half)]
        copies.append(pltpu.make_async_copy(piece, place, sems.at[i]))
    for copy in copies:
        copy.start()
    for copy in copies:
        copy.wait()


def plain_in_body(shard_ref, p0, p1, p2, p3, w_ref, x_ref, y_ref, sems):
    @pl.when(pl.program_id(0) == 0)
    def _():
        assemble(shard_ref[0], (p0, p1, p2, p3), x_ref, sems)

    chunk = chunk_of(x_ref.shape[0])

    @pl.loop(0, x_ref.shape[0] // chunk)
    def _(i):
        here = pl.ds(pl.multiple_of(i * chunk, 16), chunk)
        y_ref[here, :] = product(x_ref[here, :], w_ref[...]).astype(bf16)


def plain_in(shard, pieces, weight, tile=512):
    rows, half = pieces[0].shape
    columns = weight.shape[1]
    return pl.pallas_call(
        plain_in_body,
        grid_spec=pltpu.PrefetchScalarGridSpec(
            num_scalar_prefetch=1,
            grid=(pl.cdiv(columns, tile),),
            in_specs=[pl.BlockSpec(memory_space=pl.ANY)] * 4
            + [pl.BlockSpec((2 * half, tile), lambda j, s: (0, j))],
            out_specs=[
                pl.BlockSpec((2 * rows, 2 * half), lambda j, s: (0, 0)),
                pl.BlockSpec((2 * rows, tile), lambda j, s: (0, j)),
            ],
            scratch_shapes=[pltpu.SemaphoreType.DMA((4,))],
        ),
        out_shape=[
            jax.ShapeDtypeStruct((2 * rows, 2 * half), bf16),
            jax.ShapeDtypeStruct((2 * rows, columns), bf16),
        ],
        compiler_params=pltpu.CompilerParams(vmem_limit_bytes=limit_of(2 * rows)),
        cost_estimate=pl.CostEstimate(
            flops=8 * rows * half * columns,
            bytes_accessed=16 * rows * half + 4 * half * columns + 8 * rows * columns,
            transcendentals=0,
        ),
        name="plain_in",
    )(shard, *pieces, weight)


def expert_begin_body(shard_ref, p0, p2, gw_ref, uw_ref, gate_ref, up_ref, x_ref, sems):
    rows = p0.shape[0]

    @pl.when(pl.program_id(0) == 0)
    def _():
        copies = [
            pltpu.make_async_copy(p, x_ref.at[pl.ds(i * rows, rows), :], sems.at[i])
            for i, p in enumerate((p0, p2))
        ]
        for copy in copies:
            copy.start()
        for copy in copies:
            copy.wait()

    chunk = chunk_of(x_ref.shape[0])

    @pl.loop(0, x_ref.shape[0] // chunk)
    def _(i):
        here = pl.ds(pl.multiple_of(i * chunk, 16), chunk)
        gate_ref[here, :] = product(x_ref[here, :], gw_ref[...]).astype(bf16)
        up_ref[here, :] = product(x_ref[here, :], uw_ref[...]).astype(bf16)


def expert_begin(shard, own, other, gate_weight, up_weight, tile=512):
    rows, half = own.shape
    columns = gate_weight.shape[1]
    weight_spec = pl.BlockSpec((half, tile), lambda j, s: (s[0], j))
    tile_spec = pl.BlockSpec((2 * rows, tile), lambda j, s: (0, j))
    return pl.pallas_call(
        expert_begin_body,
        grid_spec=pltpu.PrefetchScalarGridSpec(
            num_scalar_prefetch=1,
            grid=(pl.cdiv(columns, tile),),
            in_specs=[pl.BlockSpec(memory_space=pl.ANY)] * 2 + [weight_spec, weight_spec],
            out_specs=[tile_spec, tile_spec],
            scratch_shapes=[
                pltpu.VMEM((2 * rows, half), bf16),
                pltpu.SemaphoreType.DMA((2,)),
            ],
        ),
        out_shape=[jax.ShapeDtypeStruct((2 * rows, columns), bf16)] * 2,
        compiler_params=pltpu.CompilerParams(vmem_limit_bytes=60 * 2**20),
        cost_estimate=pl.CostEstimate(
            flops=8 * rows * half * columns,
            bytes_accessed=8 * rows * half + 4 * half * columns + 16 * rows * columns,
            transcendentals=0,
        ),
        name="expert_begin",
    )(shard, own, other, gate_weight, up_weight)


def expert_in_body(
    columns, shard_ref, p0, p1, p2, p3, router_ref, info_ref, plain_ref, gp_ref, up_ref, gw_ref, uw_ref,
    x_ref, gate_ref, total_ref, hidden_ref, dgate_ref, dup_ref, their_ref, sems,
):
    tile = gw_ref.shape[1]
    rows = p0.shape[0]
    step = pl.program_id(0)

    @pl.when(step == 0)
    def _():
        copies = [
            pltpu.make_async_copy(p, their_ref.at[pl.ds(i * rows, rows), :], sems.at[4 + i])
            for i, p in enumerate((p1, p3))
        ]
        for copy in copies:
            copy.start()
        assemble(shard_ref[0], (p0, p1, p2, p3), x_ref, sems)
        for copy in copies:
            copy.wait()
        logits = product(x_ref[...], router_ref[...])
        difference = info_ref[:, MLP : MLP + router_ref.shape[1]]
        gate = jax.nn.sigmoid(jnp.sum(logits * difference, axis=1, keepdims=True))
        gate_ref[...] = jnp.broadcast_to(gate, gate_ref.shape)
        total_ref[...] = jnp.zeros_like(total_ref)

    chunk = chunk_of(x_ref.shape[0])

    @pl.loop(0, x_ref.shape[0] // chunk)
    def _(i):
        here = pl.ds(pl.multiple_of(i * chunk, 16), chunk)
        their = their_ref[here, :]
        gate_pre = gp_ref[here, :].astype(f32) + product(their, gw_ref[...])
        up_pre = up_ref[here, :].astype(f32) + product(their, uw_ref[...])
        plain, gate = plain_ref[here, :].astype(f32), gate_ref[here, :1]
        inside = lax.broadcasted_iota(jnp.int32, (1, tile), 1) + step * tile < columns
        sigmoid = jax.nn.sigmoid(gate_pre)
        silu = gate_pre * sigmoid
        hidden = (silu * up_pre).astype(bf16).astype(f32)
        gated = (gate * hidden).astype(bf16)
        hidden_ref[here, :] = gated
        total_ref[here, :] += jnp.sum(
            jnp.where(inside, gated.astype(f32) * plain, 0.0), axis=1, keepdims=True
        )
        hidden_grad = gate * plain
        up_grad = hidden_grad * silu
        dup_ref[here, :] = up_grad.astype(bf16)
        gate_grad = hidden_grad * up_pre * (sigmoid + silu * (1.0 - sigmoid))
        dgate_ref[here, :] = gate_grad.astype(bf16)


def expert_in(shard, pieces, router, info, plain, begun, gate_weight, up_weight, tile=256):
    rows, half = pieces[0].shape
    columns = gate_weight.shape[1]
    weight_spec = pl.BlockSpec((half, tile), lambda j, s: (1 - s[0], j))
    tile_spec = pl.BlockSpec((2 * rows, tile), lambda j, s: (0, j))
    held_spec = pl.BlockSpec((2 * rows, 128), lambda j, s: (0, 0))
    hidden_shape = jax.ShapeDtypeStruct((2 * rows, columns), bf16)
    return pl.pallas_call(
        functools.partial(expert_in_body, columns),
        grid_spec=pltpu.PrefetchScalarGridSpec(
            num_scalar_prefetch=1,
            grid=(pl.cdiv(columns, tile),),
            in_specs=[pl.BlockSpec(memory_space=pl.ANY)] * 4
            + [
                pl.BlockSpec(router.shape, lambda j, s: (0, 0)),
                pl.BlockSpec(info.shape, lambda j, s: (0, 0)),
                tile_spec,
                tile_spec,
                tile_spec,
                weight_spec,
                weight_spec,
            ],
            out_specs=[
                pl.BlockSpec((2 * rows, 2 * half), lambda j, s: (0, 0)),
                held_spec,
                held_spec,
                tile_spec,
                tile_spec,
                tile_spec,
            ],
            scratch_shapes=[
                pltpu.VMEM((2 * rows, half), bf16),
                pltpu.SemaphoreType.DMA((6,)),
            ],
        ),
        out_shape=[
            jax.ShapeDtypeStruct((2 * rows, 2 * half), bf16),
            jax.ShapeDtypeStruct((2 * rows, 128), f32),
            jax.ShapeDtypeStruct((2 * rows, 128), f32),
            hidden_shape,
            hidden_shape,
            hidden_shape,
        ],
        compiler_params=pltpu.CompilerParams(vmem_limit_bytes=60 * 2**20),
        cost_estimate=pl.CostEstimate(
            flops=8 * rows * half * columns,
            bytes_accessed=16 * rows * half + 4 * half * columns + 36 * rows * columns,
            transcendentals=2 * rows * columns,
        ),
        name="expert_in",
    )(shard, *pieces, router, info, plain, *begun, gate_weight, up_weight)


def attended_in_body(
    shard_ref, p0, p1, p2, p3, info_ref, mixed_ref, w_ref, x_ref, total_ref, y_ref, sems
):
    @pl.when(pl.program_id(0) == 0)
    def _():
        assemble(shard_ref[0], (p0, p1, p2, p3), x_ref, sems)
        total_ref[...] = jnp.zeros_like(total_ref)

    chunk = chunk_of(x_ref.shape[0])

    @pl.loop(0, x_ref.shape[0] // chunk)
    def _(i):
        here = pl.ds(pl.multiple_of(i * chunk, 16), chunk)
        plain = product(x_ref[here, :], w_ref[...])
        total_ref[here, :] += jnp.sum(mixed_ref[here, :].astype(f32) * plain, axis=1, keepdims=True)
        y_ref[here, :] = (info_ref[here, GATE : GATE + 1] * plain).astype(bf16)


def attended_in(shard, pieces, info, mixed, weight):
    rows, half = pieces[0].shape
    columns = weight.shape[1]
    tile = min(256, columns)
    return pl.pallas_call(
        attended_in_body,
        grid_spec=pltpu.PrefetchScalarGridSpec(
            num_scalar_prefetch=1,
            grid=(columns // tile,),
            in_specs=[pl.BlockSpec(memory_space=pl.ANY)] * 4
            + [
                pl.BlockSpec((2 * rows, 128), lambda j, s: (0, 0)),
                pl.BlockSpec((2 * rows, tile), lambda j, s: (0, j)),
                pl.BlockSpec((2 * half, tile), lambda j, s: (0, j)),
            ],
            out_specs=[
                pl.BlockSpec((2 * rows, 2 * half), lambda j, s: (0, 0)),
                pl.BlockSpec((2 * rows, 128), lambda j, s: (0, 0)),
                pl.BlockSpec((2 * rows, tile), lambda j, s: (0, j)),
            ],
            scratch_shapes=[pltpu.SemaphoreType.DMA((4,))],
        ),
        out_shape=[
            jax.ShapeDtypeStruct((2 * rows, 2 * half), bf16),
            jax.ShapeDtypeStruct((2 * rows, 128), f32),
            jax.ShapeDtypeStruct((2 * rows, columns), bf16),
        ],
        compiler_params=pltpu.CompilerParams(vmem_limit_bytes=limit_of(2 * rows)),
        cost_estimate=pl.CostEstimate(
            flops=8 * rows * half * columns,
            bytes_accessed=16 * rows * half + 4 * half * columns + 8 * rows * columns,
            transcendentals=0,
        ),
        name="attended_in",
    )(shard, *pieces, info, mixed, weight)


def rows_half_body(count, extra, gate_at, diff_at, shard_ref, *refs):
    lefts, weights = refs[:count], refs[count : 2 * count]
    rest = refs[2 * count :]
    if extra:
        total_ref, gate_ref, diff_ref, router_ref = rest[:4]
        rest = rest[4:]
        coef_ref = rest[2]

        @pl.when(pl.program_id(0) == 0)
        def _():
            gate = gate_ref[:, gate_at : gate_at + 1]
            difference = diff_ref[:, diff_at : diff_at + router_ref.shape[1]]
            coef_ref[...] = (1.0 - gate) * total_ref[:, :1] * difference

    rows = rest[0].shape[0]
    chunk = chunk_of(rows)
    for t in range(2):

        @pl.loop(0, rows // chunk)
        def _(i):
            here = pl.ds(pl.multiple_of(t * rows + i * chunk, 16), chunk)
            there = pl.ds(pl.multiple_of(i * chunk, 16), chunk)
            value = sum(product_last(a[here, :], w[...]) for a, w in zip(lefts, weights))
            if extra:
                value = value + product_last(coef_ref[here, :].astype(bf16), router_ref[...])
            rest[t][there, :] = value.astype(bf16)


def rows_half(shard, mine, lefts, weights, extra=None, tile=512):
    rows, width = lefts[0].shape[0] // 2, weights[0].shape[0]
    half = width // 2
    steps = half // tile

    def at(j, s):
        return j + steps * (s[0] if mine else 1 - s[0])

    def whole_spec(array):
        return pl.BlockSpec(array.shape, lambda j, s: (0, 0))

    in_specs = [whole_spec(a) for a in lefts]
    in_specs += [pl.BlockSpec((tile, w.shape[1]), lambda j, s: (at(j, s), 0)) for w in weights]
    operands = list(lefts) + list(weights)
    out_specs = [pl.BlockSpec((rows, tile), lambda j, s: (0, j))] * 2
    out_shape = [jax.ShapeDtypeStruct((rows, half), bf16)] * 2
    gate_at = diff_at = 0
    if extra:
        total, gate, gate_at, difference, diff_at, router = extra
        in_specs += [whole_spec(total), whole_spec(gate), whole_spec(difference)]
        in_specs += [pl.BlockSpec((tile, router.shape[1]), lambda j, s: (at(j, s), 0))]
        operands += [total, gate, difference, router]
        coefs = jax.ShapeDtypeStruct((2 * rows, router.shape[1]), f32)
        out_specs.append(whole_spec(coefs))
        out_shape.append(coefs)
    depth = sum(w.shape[1] for w in weights)
    return pl.pallas_call(
        functools.partial(rows_half_body, len(lefts), extra is not None, gate_at, diff_at),
        grid_spec=pltpu.PrefetchScalarGridSpec(
            num_scalar_prefetch=1, grid=(steps,), in_specs=in_specs, out_specs=out_specs
        ),
        out_shape=out_shape,
        compiler_params=pltpu.CompilerParams(vmem_limit_bytes=limit_of(2 * rows) if len(lefts) == 1 else 60 * 2**20),
        cost_estimate=pl.CostEstimate(
            flops=4 * rows * half * depth,
            bytes_accessed=4 * rows * depth + 2 * half * depth + 4 * rows * half,
            transcendentals=0,
        ),
        name="rows_mine" if mine else "rows_theirs",
    )(shard, *operands)


def prepare_body(
    capacity, scalars, tokens_ref, gain_ref, order_ref, attn_ref, mlp_ref, segment_ref, parent_ref,
    block_ref, attn_pack_ref, mlp_pack_ref, tile_ref,
):
    width = tokens_ref.shape[2]
    count = tokens_ref.shape[1]
    values = tokens_ref[0].astype(f32)
    scales = lax.rsqrt(jnp.mean(values * values, axis=1, keepdims=True) + epsilon)
    block_ref[:, :width] = (values * scales * gain_ref[...]).astype(bf16)

    ranks = order_ref[0].astype(f32)
    pairs = lax.broadcasted_iota(jnp.int32, (2 * count, count), 0)
    owners = lax.broadcasted_iota(jnp.int32, (2 * count, count), 1)
    turns = [(pairs == 2 * owners + k).astype(f32) for k in range(2)]
    rank_rows = [product(ranks, turn) for turn in turns]
    rank_columns = [
        lax.dot_general(turn, ranks, (((0,), (1,)), ((), ())), preferred_element_type=f32)
        for turn in turns
    ]
    same = (
        lax.broadcasted_iota(jnp.int32, (count, count), 0)
        == lax.broadcasted_iota(jnp.int32, (count, count), 1)
    ).astype(f32)
    places = lax.broadcasted_iota(jnp.int32, attn_pack_ref.shape, 0).astype(f32)
    tile_ref[...] = jnp.zeros_like(tile_ref)
    for at, (route_ref, pack_ref) in enumerate(((attn_ref, attn_pack_ref), (mlp_ref, mlp_pack_ref))):
        routes = route_ref[0].astype(f32)
        rows = product_first(routes, same)
        hit = None
        for k in range(2):
            route = rows[k : k + 1]
            slot = jnp.zeros((1, count), f32)
            for other in range(2):
                earlier = (routes[:, other : other + 1] == route) & (
                    rank_columns[other] < rank_rows[k]
                )
                slot = slot + jnp.sum(earlier.astype(f32), axis=0, keepdims=True)
            slot = jnp.minimum(slot, float(capacity))
            tile_ref[4 * at + 2 * k : 4 * at + 2 * k + 1, :] = route
            tile_ref[4 * at + 2 * k + 1 : 4 * at + 2 * k + 2, :] = slot
            code = jnp.where(slot < capacity, route * capacity + slot, -1.0)
            here = places == code
            hit = here if hit is None else hit | here
        pack_ref[...] = hit.astype(bf16)
    tile_ref[8:9, :] = segment_ref[...].astype(f32)
    tile_ref[9:10, : parent_ref.shape[1]] = parent_ref[...].astype(f32)
    block_ref[:, width:] = jnp.zeros((count, block_ref.shape[1] - width), bf16)
    block_ref[:16, width : width + count] = tile_ref[...].astype(bf16)


def prepare(place, tokens, gain, order, attn_routes, mlp_routes, segments, parents, experts, capacity):
    _, count, width = tokens.shape

    def whole_spec(array):
        return pl.BlockSpec(array.shape, lambda i, s: (0,) * array.ndim)

    pack = jax.ShapeDtypeStruct((experts * capacity, count), bf16)
    return pl.pallas_call(
        functools.partial(prepare_body, capacity),
        grid_spec=pltpu.PrefetchScalarGridSpec(
            num_scalar_prefetch=1,
            grid=(1,),
            in_specs=[whole_spec(a) for a in (tokens, gain, order, attn_routes, mlp_routes)]
            + [pl.BlockSpec((1, count), lambda i, s: (0, s[0])), whole_spec(parents)],
            out_specs=[
                pl.BlockSpec((count, width + 128), lambda i, s: (0, 0)),
                pl.BlockSpec(pack.shape, lambda i, s: (0, 0)),
                pl.BlockSpec(pack.shape, lambda i, s: (0, 0)),
            ],
            scratch_shapes=[pltpu.VMEM((16, count), f32)],
        ),
        out_shape=[jax.ShapeDtypeStruct((count, width + 128), bf16), pack, pack],
        compiler_params=pltpu.CompilerParams(vmem_limit_bytes=24 * 2**20),
        name="prepare",
    )(place, tokens, gain, order, attn_routes, mlp_routes, segments, parents)


def difference_of(expert, other, experts):
    range_of = lax.broadcasted_iota(jnp.int32, (other.shape[0], experts), 1).astype(f32)
    return (range_of == expert).astype(f32) - (range_of == other).astype(f32)


def front_body(
    capacity, steps, scalars, own_ref, other_ref, own_marks_ref, other_marks_ref, router_ref,
    key_hbm, value_hbm, got_key_hbm, got_value_hbm, shared_ref, picked_ref, bias_ref, info_ref, weight, sems,
):
    piece = weight.shape[1] // 2
    heads = piece // HEAD

    turn = pl.program_id(0)

    def fetch(sources, at):
        for h in range(heads):
            for i, source in enumerate(sources):
                from_here = source.at[:, pl.ds(pl.multiple_of(at + h * HEAD, HEAD), HEAD)]
                place = weight.at[:, pl.ds((2 * h + i) * HEAD, HEAD)]
                pltpu.make_async_copy(from_here, place, sems.at[h]).start()

    @pl.when((turn == 0) & (scalars[0] == 1))
    def _():
        fetch((key_hbm, value_hbm), scalars[1] * piece)

    @pl.when((turn == 0) & (scalars[0] == 0))
    def _():
        fetch((got_key_hbm, got_value_hbm), 0)

    def one_step(step, rows_ref, marks_ref):
        front_step(
            capacity, heads, turn, step, scalars, rows_ref, marks_ref, router_ref,
            shared_ref, picked_ref, bias_ref, info_ref, weight, sems,
        )

    @pl.when(turn < steps)
    def _():
        one_step(turn, own_ref, own_marks_ref)

    @pl.when(turn >= steps)
    def _():
        one_step(turn - steps, other_ref, other_marks_ref)


def front_step(
    capacity, heads, turn, step, scalars, rows_ref, marks_ref, router_ref,
    shared_ref, picked_ref, bias_ref, info_ref, weight, sems,
):
    count = rows_ref.shape[1]
    width = weight.shape[0]
    blocks = marks_ref.shape[0]
    rows = jnp.concatenate([rows_ref[0, :, :width], rows_ref[1, :, :width]])
    expert = scalars[2].astype(f32)
    index = lax.broadcasted_iota(jnp.int32, (2 * capacity, count), 0)
    lanes = lax.broadcasted_iota(jnp.int32, (2 * capacity, count), 1).astype(f32)
    first = index < capacity
    slots = jnp.where(first, index, index - capacity).astype(f32)
    upper = marks_ref[2 * step].astype(f32)
    lower = marks_ref[2 * step + 1].astype(f32)

    def mark(i):
        return jnp.where(first, upper[i : i + 1, :count], lower[i : i + 1, :count])

    def total(values):
        return jnp.sum(values, axis=1, keepdims=True)

    def hits_of(at):
        hits = [(mark(at + 2 * k) == expert) & (mark(at + 2 * k + 1) == slots) for k in range(2)]
        other = total(jnp.where(hits[0], mark(at + 2), 0.0) + jnp.where(hits[1], mark(at), 0.0))
        return hits[0] | hits[1], other

    experts = router_ref.shape[1]
    info_ref[:, MLP : MLP + experts] = difference_of(expert, hits_of(4)[1], experts)
    hit, other = hits_of(0)
    difference = difference_of(expert, other, experts)
    info_ref[:, ATTN : ATTN + experts] = difference

    own = total(jnp.where(hit, mark(8), 0.0))
    parents = mark(9)
    one = total(jnp.where(lanes == own, parents, 0.0))
    two = total(jnp.where(lanes == one, parents, 0.0))
    start = jnp.where(first[:, :1], 2 * step * count, (2 * step + 1) * count).astype(f32)
    place = total(jnp.where(hit, lanes, 0.0)) + start
    for j in range(blocks):
        keys = marks_ref[j, 8:9, :count].astype(f32)
        seen = ((keys == own) | (keys == one) | (keys == two)) & (lanes + float(j * count) <= place)
        bias_ref[:, j * count : (j + 1) * count] = jnp.where(seen, 0.0, negative).astype(bf16)

    both = jnp.concatenate([(hit & first).astype(bf16), (hit & ~first).astype(bf16)], axis=1)
    picked = product(both, rows).astype(bf16)
    picked_ref[...] = picked
    logits = product(picked, router_ref[...])
    info_ref[:, GATE : GATE + 1] = jax.nn.sigmoid(total(logits * difference))

    @pl.when(turn == 0)
    def _():
        for h in range(heads):
            here = pl.ds(2 * h * HEAD, 2 * HEAD)
            pltpu.make_async_copy(weight.at[:, here], weight.at[:, here], sems.at[h]).wait()
            shared_ref[:, here] = product(rows, weight[:, here]).astype(bf16)

    @pl.when(turn > 0)
    def _():
        shared_ref[...] = product(rows, weight[...]).astype(bf16)


def front(scalars, own, other, router, key_weight, value_weight, got_key, got_value, capacity):
    blocks, count, columns = own.shape
    width, piece = got_key.shape
    length = blocks * count
    rows = blocks * capacity
    steps = blocks // 2
    pinned_spec = pl.BlockSpec(memory_space=pltpu.HBM)
    marks_spec = pl.BlockSpec((blocks, 16, 128), lambda i, s: (0, 0, width // 128))

    def out_spec(height, columns):
        return pl.BlockSpec((height, columns), lambda i, s: (i, 0))

    pair = 2 * capacity
    return pl.pallas_call(
        functools.partial(front_body, capacity, steps),
        grid_spec=pltpu.PrefetchScalarGridSpec(
            num_scalar_prefetch=1,
            grid=(2 * steps,),
            in_specs=[
                pl.BlockSpec((2, count, columns), lambda i, s: (jnp.minimum(i, steps - 1), 0, 0)),
                pl.BlockSpec((2, count, columns), lambda i, s: (jnp.maximum(i - steps, 0), 0, 0)),
                marks_spec,
                marks_spec,
                pl.BlockSpec(router.shape, lambda i, s: (0, 0)),
            ]
            + [pinned_spec] * 4,
            out_specs=[
                out_spec(2 * count, 2 * piece),
                out_spec(pair, width),
                out_spec(pair, length),
                out_spec(pair, 128),
            ],
            scratch_shapes=[
                pltpu.VMEM((width, 2 * piece), bf16),
                pltpu.SemaphoreType.DMA((piece // HEAD,)),
            ],
        ),
        out_shape=[
            jax.ShapeDtypeStruct((2 * length, 2 * piece), bf16),
            jax.ShapeDtypeStruct((2 * rows, width), bf16),
            jax.ShapeDtypeStruct((2 * rows, length), bf16),
            jax.ShapeDtypeStruct((2 * rows, 128), f32),
        ],
        compiler_params=pltpu.CompilerParams(vmem_limit_bytes=60 * 2**20),
        cost_estimate=pl.CostEstimate(
            flops=8 * length * width * piece,
            bytes_accessed=4 * length * width + 4 * width * piece,
            transcendentals=0,
        ),
        name="front",
    )(scalars, own, other, own, other, router, key_weight, value_weight, got_key, got_value)


def shared_out_body(steps, scalars, sums_ref, key_ref, value_ref, got_key_ref, got_value_ref, *outs):
    step = pl.program_id(0)
    sums = sums_ref[...]
    heads = sums.shape[0] // 2

    def part(t, i):
        return jnp.concatenate([sums[2 * h + i, t] for h in range(heads)], axis=1)

    def fill(pair, keys, values):
        for t in range(2):
            value = product_last(part(t, 0), keys[...]) + product_last(part(t, 1), values[...])
            pair[t][...] = value.astype(bf16)

    for side in range(2):
        for local in range(2):
            first = step < steps // 2 if side == 0 else step >= steps // 2

            @pl.when(first & (scalars[1] == local))
            def _():
                pair = (outs[side], outs[2 + side])
                if local:
                    fill(pair, key_ref, value_ref)
                else:
                    fill(pair, got_key_ref, got_value_ref)


def shared_out(scalars, sums, key_weight, value_weight, got_key, got_value, tile=512):
    rows = sums.shape[2]
    width, piece = got_key.shape
    half, steps = width // 2, width // tile

    def at(j, s):
        return lax.rem(j + steps // 2 * (1 - s[0]), steps)

    local = pl.BlockSpec((tile, piece), lambda j, s: (at(j, s), s[2]))
    sent = pl.BlockSpec((tile, piece), lambda j, s: (at(j, s), 0))
    theirs = pl.BlockSpec((rows, tile), lambda j, s: (0, jnp.minimum(j, steps // 2 - 1)))
    mine = pl.BlockSpec((rows, tile), lambda j, s: (0, jnp.maximum(j - steps // 2, 0)))
    return pl.pallas_call(
        functools.partial(shared_out_body, steps),
        grid_spec=pltpu.PrefetchScalarGridSpec(
            num_scalar_prefetch=1,
            grid=(steps,),
            in_specs=[pl.BlockSpec(sums.shape, lambda j, s: (0, 0, 0, 0)), local, local, sent, sent],
            out_specs=[theirs, mine, theirs, mine],
        ),
        out_shape=[jax.ShapeDtypeStruct((rows, half), bf16)] * 4,
        compiler_params=pltpu.CompilerParams(vmem_limit_bytes=60 * 2**20),
        cost_estimate=pl.CostEstimate(
            flops=8 * rows * width * piece,
            bytes_accessed=8 * width * piece + 8 * rows * width,
            transcendentals=0,
        ),
        name="shared_out",
    )(scalars, sums, key_weight, value_weight, got_key, got_value)


def per_device(
    tokens,
    cotangent,
    attn_gain,
    mlp_gain,
    key_weight,
    value_weight,
    query_weight,
    output_weight,
    attn_router,
    gate_weight,
    up_weight,
    down_weight,
    mlp_router,
    segment_ids,
    parent_ids,
    attn_routes,
    mlp_routes,
    slot_order,
):
    count, width = tokens.shape[1:]
    half = width // 2
    piece = query_weight.shape[1]
    experts = attn_router.shape[1]
    blocks = lax.axis_size("dp")
    members = blocks // experts
    capacity = min(count, 5 * count * attn_routes.shape[2] // (4 * experts))
    length, parents = segment_ids.shape[1], parent_ids.shape[1]
    tiles = max(2, length // 512)
    dp, core, shard = lax.axis_index("dp"), lax.axis_index("expert"), lax.axis_index("shard")
    expert, member = dp // members, dp % members

    def my_half(values):
        return lax.dynamic_slice_in_dim(values, shard * half, half, values.ndim - 1)

    def whole(mine):
        got = swap(mine, "shard")
        first = shard == 0
        return jnp.concatenate(
            [jnp.where(first, mine, got), jnp.where(first, got, mine)], axis=mine.ndim - 1
        )

    block, attn_pack, mlp_pack = prepare(
        jnp.reshape(dp, (1,)).astype(jnp.int32),
        tokens,
        attn_gain[None],
        slot_order,
        attn_routes,
        mlp_routes,
        segment_ids,
        parent_ids,
        experts,
        capacity,
    )
    heads_at = (member * 2 + core) * 2 + shard
    holder = (member * 2 + core) // members
    offset = holder * 2 * members
    names = ("dp", "expert", "shard")
    sends = []
    for d in range(blocks):
        for c in range(2):
            at = (d * 2 + c) * 2
            source = ((d % members) * 2 + c) // members
            sends.append((at + source, at + 1 - source))
    partner_at = (member * 2 + core) * 2 + 1 - shard

    def partner_columns(weight):
        columns = lax.dynamic_slice_in_dim(weight, (partner_at - offset) * piece, piece, 1)
        return lax.ppermute(after(columns, block), names, sends)

    grad_half = lax.dynamic_slice_in_dim(cotangent[0], shard * half, half, 1)

    def pack_rows(values, pack):
        packed = product(pack, values).astype(bf16).reshape(experts, 1, capacity, half)
        packed = jnp.broadcast_to(packed, (experts, members, capacity, half))
        return packed.reshape(blocks, capacity, half)

    works = [None] * (blocks // 2)
    works[-1] = lambda event: [pack_rows(after(grad_half, event), mlp_pack)]
    own_blocks, made = ring_gather(block, "dp", blocks, 1, works)
    grad_packed = made[-1][0]
    got_key, got_value = partner_columns(key_weight), partner_columns(value_weight)
    own_blocks, got_key, got_value = lax.optimization_barrier((own_blocks, got_key, got_value))
    tree_blocks = [own_blocks, swap(own_blocks, "expert")]

    local = (shard == holder).astype(jnp.int32)
    local_at = local * (heads_at - offset)
    shard_index = jnp.reshape(shard, (1,)).astype(jnp.int32)

    def dispatch(packed, work=None, begin=None):
        arrived = lax.all_to_all(packed, "dp", 0, 0, tiled=True)
        done = []
        if work:
            arrived, *done = lax.optimization_barrier((arrived, *work(packed)))
        arrived = arrived.reshape(blocks * capacity, half)
        other = swap(arrived, "expert")
        got = swap(arrived, "shard")
        begun = []
        if begin:
            got, *begun = lax.optimization_barrier((got, *begin(arrived, other)))
        return [arrived, got, other, swap(got, "expert")], done, begun

    def join_ends(sides, work=None):
        own, other, *_ = sides(False, None)
        theirs = (own.astype(f32) + swap(other, "expert").astype(f32)).astype(bf16)
        back, own, other, *rest = lax.optimization_barrier(
            (swap(theirs, "shard"), *sides(True, theirs), *(work(theirs) if work else []))
        )
        total = own.astype(f32) + swap(other, "expert").astype(f32) + back.astype(f32)
        return total, rest

    def sum_tokens(back, pack):
        if members > 1:
            back = back.reshape(experts, members, capacity, half).astype(f32)
            back = jnp.sum(back, axis=1).astype(bf16)
        return product_first(pack, back.reshape(experts * capacity, half))

    def send_back(joined, work=None):
        back = lax.all_to_all(joined, "dp", 0, 0, tiled=True)
        done = []
        if work:
            back, *done = lax.optimization_barrier((back, *work(joined)))
        return back, done

    def for_tokens(joined):
        return joined.astype(bf16).reshape(blocks, capacity, half)

    grad_arrived = lax.all_to_all(grad_packed, "dp", 0, 0, tiled=True)
    grad_arrived = grad_arrived.reshape(blocks * capacity, half)
    scalars = jnp.stack([local, local_at, expert]).astype(jnp.int32)
    shared, rows, bias, info = front(
        scalars, *tree_blocks, attn_router, key_weight, value_weight, got_key, got_value, capacity
    )
    grad_got = swap(after(grad_arrived, rows), "shard")
    queries = product(rows, query_weight).astype(bf16)
    mixed, log_total = attend(queries, shared, bias, info, tiles)
    mixed, grad_got = lax.optimization_barrier((mixed, grad_got))
    grad_pieces = (grad_arrived, grad_got, swap(grad_arrived, "expert"), swap(grad_got, "expert"))

    def attn_sides(mine, event):
        return rows_half(shard_index, mine, [after(mixed, event)], [output_weight])

    def plain_work(event):
        return plain_in(shard_index, after(grad_pieces, event), down_weight)

    attn_joined, (grad_rows, plain_grad) = join_ends(attn_sides, plain_work)
    back = send_back(for_tokens(attn_joined))[0]
    inputs = tokens[0].astype(f32)
    attn_scale = lax.rsqrt(jnp.mean(inputs * inputs, axis=1, keepdims=True) + epsilon)
    middle = my_half(inputs) + sum_tokens(back, attn_pack)

    def feature_mean(values):
        part = jnp.sum(values, axis=1, keepdims=True)
        return (part + swap(part, "shard")) / width

    mlp_scale = lax.rsqrt(feature_mean(middle * middle) + epsilon)
    half_gain = my_half(mlp_gain)
    mlp_normed = (middle * mlp_scale * half_gain).astype(bf16)

    def begin(own, other):
        return expert_begin(shard_index, own, other, gate_weight, up_weight)

    mlp_pieces, _, begun = dispatch(pack_rows(mlp_normed, mlp_pack), None, begin)
    mlp_rows, mlp_gate, mlp_total, gated_hidden, gate_pre_grad, up_pre_grad = expert_in(
        shard_index, mlp_pieces, mlp_router, info, plain_grad, begun, gate_weight, up_weight
    )

    def mlp_sides(mine, event):
        return rows_half(
            shard_index,
            mine,
            after([gate_pre_grad, up_pre_grad], event),
            [gate_weight, up_weight],
            (mlp_total, mlp_gate, 0, info, MLP, mlp_router),
        )

    def term_half(mine, event):
        return rows_half(shard_index, mine, [after(gated_hidden, event)], [down_weight])

    row_joined, (mlp_coefs,) = join_ends(mlp_sides)
    row_joined = for_tokens(row_joined)

    def gate_work(event):
        own, other = term_half(False, event)
        theirs = own.astype(f32) + swap(other, "expert").astype(f32)
        return [theirs.astype(bf16), product_first(after(mlp_rows, own), gate_pre_grad)]

    back, (term_theirs, gate_grad) = send_back(row_joined, gate_work)
    mlp_normed_grad = sum_tokens(back, mlp_pack)

    mlp_n = middle * mlp_scale
    weighted = mlp_normed_grad * half_gain
    mlp_gain_part = jnp.sum(mlp_normed_grad * mlp_n, axis=0)
    middle_grad = grad_half.astype(f32) + mlp_scale * (
        weighted - mlp_n * feature_mean(weighted * mlp_n)
    )
    low_grad = middle_grad.astype(bf16)

    def up_work(event):
        up_grad = product_first(after(mlp_rows, event), up_pre_grad)
        router_part = product_first(mlp_coefs, after(mlp_rows, event).astype(f32))
        return [up_grad, router_part]

    def down_work(own, other):
        return [product_first(after(grad_rows, own), gated_hidden)]

    packed = pack_rows(low_grad, attn_pack)
    term_pieces, (up_grad, mlp_router_part), (down_grad,) = dispatch(packed, up_work, down_work)
    term_back = swap(after(term_theirs, packed), "shard")
    own, other = term_half(True, packed)
    total = own.astype(f32) + swap(other, "expert").astype(f32) + term_back.astype(f32)
    term_joined = after(for_tokens(total), term_pieces[0])
    term_back = lax.all_to_all(term_joined, "dp", 0, 0, tiled=True)
    term_rows, attn_total, attended_grad = attended_in(
        shard_index, term_pieces, info, mixed, output_weight
    )
    query_rows_grad, held = attend_back(queries, shared, bias, log_total, attended_grad, tiles)
    held, term_back = lax.optimization_barrier((held, term_back))
    part = length // experts
    cut = experts * HEAD // (2 * piece)

    def cut_parts(values):
        shape = values.shape
        values = values.reshape(shape[:-1] + (cut, shape[-1] // cut))
        return jnp.moveaxis(values, -2, 1).reshape((experts,) + shape[1:-1] + (-1,))

    def join_parts(values):
        shape = values.shape
        values = jnp.moveaxis(values.reshape((experts // cut, cut) + shape[1:]), 1, -2)
        return values.reshape(values.shape[:-2] + (-1,))

    rings = None
    if members > 1:
        rings = [[e * members + m for e in range(experts)] for m in range(members)]

    def to_experts(values):
        return lax.all_to_all(values, "dp", 0, 0, axis_index_groups=rings, tiled=True)

    held = cut_parts(held)
    def input_rows(mine, event):
        return rows_half(
            shard_index,
            mine,
            [after(query_rows_grad, event)],
            [query_weight],
            (attn_total, info, GATE, info, ATTN, attn_router),
        )

    kept = []

    def theirs_work(event):
        own, other, _ = input_rows(False, event)
        theirs = own.astype(f32) + swap(other, "expert").astype(f32)
        kept.append(theirs.astype(bf16))
        return kept[:]

    def mine_work(event):
        kept.append(swap(after(kept[0], event), "shard"))
        kept.extend(input_rows(True, event))
        return kept[2:] + [product_first(after(rows, event), query_rows_grad)]

    def output_work(event):
        return [kept[1], product_first(after(term_rows, event), mixed)]

    works = [None, theirs_work, mine_work, output_work]
    key_sums, made = ring_scatter(held, experts, members, works)
    key_sums = key_sums.astype(bf16)
    _, _, (own, other, attn_coefs, query_grad), (back, output_grad) = made
    total = own.astype(f32) + swap(other, "expert").astype(f32) + back.astype(f32)
    input_joined = for_tokens(total)
    scalars = jnp.stack([shard, local, local_at]).astype(jnp.int32)

    def weight_work(event):
        sums = after(key_sums, event)
        sums = sum(product_first(tree_blocks[t].reshape(length, -1), sums[t]) for t in range(2))
        return [sums[:width].astype(bf16).reshape(experts, width // experts, -1)]

    def shared_work(event):
        parts = shared_out(
            scalars, after(token_sums, event), key_weight, value_weight, got_key, got_value
        )
        theirs = parts[0].astype(f32) + swap(parts[2], "expert").astype(f32)
        shared = parts[1].astype(f32) + swap(parts[3], "expert").astype(f32)
        return [shared, swap(theirs.astype(bf16), "shard")]

    token_sums = key_sums.reshape(2, experts, part, -1).transpose(1, 0, 2, 3)
    (token_sums,), (weight_sums,) = pinned((to_experts(token_sums),), weight_work, token_sums)
    token_sums = join_parts(token_sums)
    input_joined = after(input_joined, token_sums)
    back = lax.all_to_all(input_joined, "dp", 0, 0, tiled=True)
    (back,), (shared, theirs) = pinned((back,), shared_work, input_joined)
    shared = shared + theirs.astype(f32)
    if members > 1:
        groups = [[e * members + m for m in range(members)] for e in range(experts)]
        shared = lax.psum_scatter(
            shared, "dp", scatter_dimension=0, axis_index_groups=groups, tiled=True
        )
    attn_n = my_half(inputs) * attn_scale
    features = width // (2 * blocks)

    def spread(values):
        return lax.dynamic_update_slice(jnp.zeros((1, width), f32), values[None], (0, shard * half))

    def last_work(event):
        normed_grad = sum_tokens(after(back, event), attn_pack) + shared
        weighted = normed_grad * my_half(attn_gain)
        gain_part = jnp.sum(normed_grad * attn_n, axis=0)
        grad = middle_grad + attn_scale * (weighted - attn_n * feature_mean(weighted * attn_n))
        small = [attn_router_part, mlp_router_part, spread(gain_part), spread(mlp_gain_part)]
        small = jnp.pad(jnp.concatenate(small), ((0, 6), (0, 0)))
        small = small + swap(small, "shard")
        small = small.reshape(-1, blocks, 2, features).transpose(2, 1, 0, 3)
        mine = lax.dynamic_index_in_dim(small, core, 0, keepdims=False)
        theirs = lax.dynamic_index_in_dim(small, 1 - core, 0, keepdims=False)
        return [grad, swap(grad.astype(bf16), "shard"), mine + swap(theirs, "expert")]

    attn_router_part = product_first(attn_coefs, after(rows, key_sums).astype(f32))
    weight_sums = after(weight_sums, back)
    (weight_sums,), (tokens_grad, got, small) = pinned(
        (to_experts(weight_sums),), last_work, weight_sums
    )
    weight_sums = join_parts(weight_sums)
    layer_out = whole((middle + sum_tokens(term_back, mlp_pack)).astype(bf16))[None]
    got = got.astype(f32)
    tokens_grad = jnp.concatenate(
        [jnp.where(shard == 0, tokens_grad, got), jnp.where(shard == 0, got, tokens_grad)], axis=1
    )[None]
    small = jnp.sum(lax.all_to_all(small, "dp", 0, 0, tiled=True), axis=0)

    heads = piece // HEAD
    pieces = weight_sums.reshape(2 * heads, members, 2, features, HEAD).transpose(1, 2, 0, 3, 4)
    if members > 1:
        pieces = lax.all_to_all(pieces, "dp", 0, 0, axis_index_groups=groups, tiled=True)
    pieces = pair_all_to_all(pieces.transpose(1, 0, 2, 3, 4), "expert")
    pieces = pieces.transpose(1, 0, 2, 3, 4).reshape(2, members, 2 * heads, features, HEAD)
    pieces = pair_all_to_all(pieces, "shard").reshape(2, members, heads, 2, features, HEAD)
    pieces = pieces.transpose(3, 4, 1, 0, 2, 5).reshape(2, features, -1).astype(f32)

    return (
        layer_out,
        tokens_grad,
        small[2 * experts],
        small[2 * experts + 1],
        pieces[0],
        pieces[1],
        query_grad,
        output_grad,
        small[:experts].T,
        gate_grad,
        up_grad,
        down_grad,
        small[experts : 2 * experts].T,
    )


def solution(mesh):
    tree = P("expert", "dp", None)
    columns = P(None, ("dp", "expert", "shard"))
    spread = P(("dp", "expert"), None)
    in_specs = (
        tree,
        tree,
        P(),
        P(),
        P(None, "shard"),
        P(None, "shard"),
        columns,
        columns,
        P(),
        columns,
        columns,
        columns,
        P(),
        P("expert", None),
        P("expert", None),
        tree,
        tree,
        tree,
    )
    out_specs = (
        tree,
        tree,
        P(("dp", "expert")),
        P(("dp", "expert")),
        P(("dp", "expert"), "shard"),
        P(("dp", "expert"), "shard"),
        columns,
        columns,
        spread,
        columns,
        columns,
        columns,
        spread,
    )
    return jax.shard_map(
        per_device, mesh=mesh, in_specs=in_specs, out_specs=out_specs, check_vma=False
    )
```

```python
import functools

import jax
import jax.numpy as jnp
from jax import lax
from jax.experimental import pallas as pl
from jax.experimental.pallas import tpu as pltpu
from jax.sharding import PartitionSpec as P

HEAD = 128

epsilon = 1e-06
negative = -1e30
ATTN, MLP, GATE = 0, 32, 64
scale = HEAD ** (-0.5)
bf16 = jnp.bfloat16
f32 = jnp.float32


def product(former, latter):
    return jnp.dot(former, latter, preferred_element_type=f32)


def product_last(former, latter):
    return lax.dot_general(
        former, latter, (((1,), (1,)), ((), ())), preferred_element_type=f32
    )


def product_first(former, latter):
    return lax.dot_general(
        former, latter, (((0,), (0,)), ((), ())), preferred_element_type=f32
    )


def limit_of(rows):
    return min(56, max(40, rows * 24 // 640)) * 2**20


def swap(values, axis):
    return lax.ppermute(values, axis, [(0, 1), (1, 0)])


def pair_all_to_all(parts, axis):
    me = lax.axis_index(axis)
    mine = lax.dynamic_index_in_dim(parts, me, 0, keepdims=False)
    theirs = lax.dynamic_index_in_dim(parts, 1 - me, 0, keepdims=False)
    got = swap(theirs, axis)
    first = me == 0
    return jnp.stack([jnp.where(first, mine, got), jnp.where(first, got, mine)])


def ring_order(count):
    return list(range(0, count, 2)) + list(range(1, count, 2))[::-1]


def ring_member(place, count):
    place = lax.rem(place + 2 * count, count)
    return jnp.where(place < count // 2, 2 * place, 2 * (count - place) - 1)


def ring_place(member, count):
    return jnp.where(member % 2 == 0, member // 2, count - (member + 1) // 2)


def empty(shape, dtype):
    return pl.pallas_call(
        lambda ref: None,
        out_shape=jax.ShapeDtypeStruct(shape, dtype),
        out_specs=pl.BlockSpec(memory_space=pl.ANY),
        name="empty",
    )()


def pinned(values, work, event):
    *values, made = lax.optimization_barrier((*values, work(event) if work else []))
    return values, made


def ring_gather(block, axis, count, stride, works=()):
    works = list(works) + [None] * (count // 2)
    order = ring_order(count)
    member = lax.axis_index(axis) // stride
    place = ring_place(member, count)
    right, left = ring_moves(order, 1, stride), ring_moves(order, -1, stride)
    rows, columns = block.shape
    half = rows // 2
    out = empty((count, rows, columns), block.dtype)

    def put(out, piece, source, row):
        return lax.dynamic_update_slice(out, piece[None], (source, row, 0))

    out = put(out, block, member, 0)
    forward, backward = block, block
    results = []
    for step in range(1, count // 2 + 1):
        last = step == count // 2
        if last:
            forward, backward = forward[:half], backward[half:]
        event = forward
        forward = lax.ppermute(forward, axis, right)
        backward = lax.ppermute(backward, axis, left)
        (forward, backward), made = pinned((forward, backward), works[step - 1], event)
        results.append(made)
        out = put(out, forward, ring_member(place - step, count), 0)
        out = put(out, backward, ring_member(place + step, count), half if last else 0)
    return out, results


def ring_moves(order, by, stride):
    count = len(order)
    return [
        (order[i] * stride + j, order[(i + by) % count] * stride + j)
        for i in range(count)
        for j in range(stride)
    ]


def after(values, *events):
    if events[0] is None:
        return values
    return lax.optimization_barrier((values,) + events)[0]


def ring_scatter(parts, count, stride, works=()):
    works = list(works) + [None] * (count // 2)
    order = ring_order(count)
    place = ring_place(lax.axis_index("dp") // stride, count)
    right, left = ring_moves(order, 1, stride), ring_moves(order, -1, stride)
    far = count // 2

    def part(offset):
        return lax.dynamic_index_in_dim(parts, ring_member(place + offset, count), 0, keepdims=False)

    def added(sent, offset, first):
        own = part(offset).astype(f32)
        if first is not None:
            sent = jnp.pad(sent, ((first, 1 - first), (0, 0), (0, 0)))
        return (own + sent.astype(f32)).astype(bf16)

    forward, backward = part(far)[:1], part(-far)[1:]
    results = []
    for step in range(far):
        event = forward
        forward = lax.ppermute(forward, "dp", right)
        backward = lax.ppermute(backward, "dp", left)
        (forward, backward), made = pinned((forward, backward), works[step], event)
        results.append(made)
        offset = far - 1 - step
        if offset:
            forward = added(forward, offset, 0 if step == 0 else None)
            backward = added(backward, -offset, 1 if step == 0 else None)
    return part(0).astype(f32) + forward.astype(f32) + backward.astype(f32), results


def attend_body(tiles, keys_per_tile, q_ref, k_ref, v_ref, bias_ref, info_ref, out_ref, total_ref):
    rows = q_ref.shape[0] // tiles
    lanes = lax.broadcasted_iota(jnp.int32, (rows, 128), 1)
    for tile in range(tiles):
        here = pl.ds(tile * rows, rows)
        keys = (tile + 1) * keys_per_tile
        scores = product_last(q_ref[here, :], k_ref[:keys, :]) * scale
        scores = scores + bias_ref[here, :keys].astype(f32)
        highest = jnp.max(scores, axis=1, keepdims=True)
        expo = jnp.exp(scores - highest)
        summed = jnp.sum(expo, axis=1, keepdims=True)
        mixed = product(expo.astype(bf16), v_ref[:keys, :]) * (1.0 / summed)
        mixed = mixed.astype(bf16).astype(f32)
        out_ref[here, :] = (mixed * info_ref[here, GATE : GATE + 1]).astype(bf16)
        total = highest + jnp.log(summed)
        total_ref[here, :] = jnp.where(lanes == pl.program_id(1), total, total_ref[here, :])


def attend(queries, shared, bias, info, tiles):
    rows, columns = queries.shape[0] // 2, queries.shape[1]
    length = shared.shape[0] // 2
    heads = columns // HEAD
    return pl.pallas_call(
        functools.partial(attend_body, tiles, length // tiles),
        grid=(2, heads),
        in_specs=[
            pl.BlockSpec((rows, HEAD), lambda t, h: (t, h)),
            pl.BlockSpec((length, HEAD), lambda t, h: (t, 2 * h)),
            pl.BlockSpec((length, HEAD), lambda t, h: (t, 2 * h + 1)),
            pl.BlockSpec((rows, length), lambda t, h: (t, 0)),
            pl.BlockSpec((rows, 128), lambda t, h: (t, 0)),
        ],
        out_specs=[
            pl.BlockSpec((rows, HEAD), lambda t, h: (t, h)),
            pl.BlockSpec((rows, 128), lambda t, h: (t, 0)),
        ],
        out_shape=[
            jax.ShapeDtypeStruct((2 * rows, columns), bf16),
            jax.ShapeDtypeStruct((2 * rows, 128), f32),
        ],
        compiler_params=pltpu.CompilerParams(vmem_limit_bytes=limit_of(2 * rows)),
        cost_estimate=pl.CostEstimate(
            flops=8 * rows * length * columns,
            bytes_accessed=4 * (rows * length + 2 * length * columns),
            transcendentals=2 * rows * length * heads,
        ),
        name="attend",
    )(queries, shared, shared, bias, info)


def attend_back_body(
    tiles, keys_per_tile, q_ref, k_ref, v_ref, bias_ref, total_ref, grad_ref, dq_ref, both_ref, dk_sum, dv_sum
):
    rows = q_ref.shape[0] // tiles
    lanes = lax.broadcasted_iota(jnp.int32, (rows, 128), 1)
    dk_sum[...] = jnp.zeros_like(dk_sum)
    dv_sum[...] = jnp.zeros_like(dv_sum)
    for tile in range(tiles):
        here = pl.ds(tile * rows, rows)
        keys = (tile + 1) * keys_per_tile
        query, grad = q_ref[here, :], grad_ref[here, :]
        scores = product_last(query, k_ref[:keys, :]) * scale
        scores = scores + bias_ref[here, :keys].astype(f32)
        total = jnp.where(lanes == pl.program_id(1), total_ref[here, :], 0.0)
        probs = jnp.exp(scores - jnp.sum(total, axis=1, keepdims=True))
        prob_grad = product_last(grad, v_ref[:keys, :])
        inner = jnp.sum(probs * prob_grad, axis=1, keepdims=True)
        score_grad = (probs * (prob_grad - inner) * scale).astype(bf16)
        dq_ref[here, :] = product(score_grad, k_ref[:keys, :]).astype(bf16)
        dk_sum[:keys, :] += product_first(score_grad, query)
        dv_sum[:keys, :] += product_first(probs.astype(bf16), grad)
    both_ref[0, 0] = dk_sum[...].astype(bf16)
    both_ref[1, 0] = dv_sum[...].astype(bf16)


def attend_back(queries, shared, bias, total, grads, tiles):
    rows, columns = queries.shape[0] // 2, queries.shape[1]
    length = shared.shape[0] // 2
    heads = columns // HEAD
    row_spec = pl.BlockSpec((rows, HEAD), lambda t, h: (t, h))
    return pl.pallas_call(
        functools.partial(attend_back_body, tiles, length // tiles),
        grid=(2, heads),
        in_specs=[
            row_spec,
            pl.BlockSpec((length, HEAD), lambda t, h: (t, 2 * h)),
            pl.BlockSpec((length, HEAD), lambda t, h: (t, 2 * h + 1)),
            pl.BlockSpec((rows, length), lambda t, h: (t, 0)),
            pl.BlockSpec((rows, 128), lambda t, h: (t, 0)),
            row_spec,
        ],
        out_specs=[row_spec, pl.BlockSpec((2, 1, length, HEAD), lambda t, h: (h, t, 0, 0))],
        out_shape=[
            jax.ShapeDtypeStruct((2 * rows, columns), bf16),
            jax.ShapeDtypeStruct((2 * heads, 2, length, HEAD), bf16),
        ],
        scratch_shapes=[pltpu.VMEM((length, HEAD), f32), pltpu.VMEM((length, HEAD), f32)],
        compiler_params=pltpu.CompilerParams(vmem_limit_bytes=60 * 2**20),
        cost_estimate=pl.CostEstimate(
            flops=20 * rows * length * columns,
            bytes_accessed=4 * (rows * length + 4 * length * columns),
            transcendentals=2 * rows * length * heads,
        ),
        name="attend_back",
    )(queries, shared, shared, bias, total, grads)


def chunk_of(rows):
    return 640 if rows % 640 == 0 else rows


def assemble(shard, pieces, out_ref, sems):
    rows, half = pieces[0].shape
    copies = []
    for i, piece in enumerate(pieces):
        at = pl.multiple_of((shard if i % 2 == 0 else 1 - shard) * half, 128)
        place = out_ref.at[pl.ds(i // 2 * rows, rows), pl.ds(at, half)]
        copies.append(pltpu.make_async_copy(piece, place, sems.at[i]))
    for copy in copies:
        copy.start()
    for copy in copies:
        copy.wait()


def plain_in_body(shard_ref, p0, p1, p2, p3, w_ref, x_ref, y_ref, sems):
    @pl.when(pl.program_id(0) == 0)
    def _():
        assemble(shard_ref[0], (p0, p1, p2, p3), x_ref, sems)

    chunk = chunk_of(x_ref.shape[0])

    @pl.loop(0, x_ref.shape[0] // chunk)
    def _(i):
        here = pl.ds(pl.multiple_of(i * chunk, 16), chunk)
        y_ref[here, :] = product(x_ref[here, :], w_ref[...]).astype(bf16)


def plain_in(shard, pieces, weight, tile=512):
    rows, half = pieces[0].shape
    columns = weight.shape[1]
    return pl.pallas_call(
        plain_in_body,
        grid_spec=pltpu.PrefetchScalarGridSpec(
            num_scalar_prefetch=1,
            grid=(pl.cdiv(columns, tile),),
            in_specs=[pl.BlockSpec(memory_space=pl.ANY)] * 4
            + [pl.BlockSpec((2 * half, tile), lambda j, s: (0, j))],
            out_specs=[
                pl.BlockSpec((2 * rows, 2 * half), lambda j, s: (0, 0)),
                pl.BlockSpec((2 * rows, tile), lambda j, s: (0, j)),
            ],
            scratch_shapes=[pltpu.SemaphoreType.DMA((4,))],
        ),
        out_shape=[
            jax.ShapeDtypeStruct((2 * rows, 2 * half), bf16),
            jax.ShapeDtypeStruct((2 * rows, columns), bf16),
        ],
        compiler_params=pltpu.CompilerParams(vmem_limit_bytes=limit_of(2 * rows)),
        cost_estimate=pl.CostEstimate(
            flops=8 * rows * half * columns,
            bytes_accessed=16 * rows * half + 4 * half * columns + 8 * rows * columns,
            transcendentals=0,
        ),
        name="plain_in",
    )(shard, *pieces, weight)


def expert_begin_body(shard_ref, p0, p2, gw_ref, uw_ref, gate_ref, up_ref, x_ref, sems):
    rows = p0.shape[0]

    @pl.when(pl.program_id(0) == 0)
    def _():
        copies = [
            pltpu.make_async_copy(p, x_ref.at[pl.ds(i * rows, rows), :], sems.at[i])
            for i, p in enumerate((p0, p2))
        ]
        for copy in copies:
            copy.start()
        for copy in copies:
            copy.wait()

    chunk = chunk_of(x_ref.shape[0])

    @pl.loop(0, x_ref.shape[0] // chunk)
    def _(i):
        here = pl.ds(pl.multiple_of(i * chunk, 16), chunk)
        gate_ref[here, :] = product(x_ref[here, :], gw_ref[...]).astype(bf16)
        up_ref[here, :] = product(x_ref[here, :], uw_ref[...]).astype(bf16)


def expert_begin(shard, own, other, gate_weight, up_weight, tile=512):
    rows, half = own.shape
    columns = gate_weight.shape[1]
    weight_spec = pl.BlockSpec((half, tile), lambda j, s: (s[0], j))
    tile_spec = pl.BlockSpec((2 * rows, tile), lambda j, s: (0, j))
    return pl.pallas_call(
        expert_begin_body,
        grid_spec=pltpu.PrefetchScalarGridSpec(
            num_scalar_prefetch=1,
            grid=(pl.cdiv(columns, tile),),
            in_specs=[pl.BlockSpec(memory_space=pl.ANY)] * 2 + [weight_spec, weight_spec],
            out_specs=[tile_spec, tile_spec],
            scratch_shapes=[
                pltpu.VMEM((2 * rows, half), bf16),
                pltpu.SemaphoreType.DMA((2,)),
            ],
        ),
        out_shape=[jax.ShapeDtypeStruct((2 * rows, columns), bf16)] * 2,
        compiler_params=pltpu.CompilerParams(vmem_limit_bytes=60 * 2**20),
        cost_estimate=pl.CostEstimate(
            flops=8 * rows * half * columns,
            bytes_accessed=8 * rows * half + 4 * half * columns + 16 * rows * columns,
            transcendentals=0,
        ),
        name="expert_begin",
    )(shard, own, other, gate_weight, up_weight)


def expert_in_body(
    columns, tiles, shard_ref, p0, p1, p2, p3, router_ref, info_ref, plain_ref, gp_ref, up_ref, gw_ref, uw_ref,
    g_ref, u_ref, r_ref, x_ref, gate_ref, total_ref, hidden_ref, dgate_ref, dup_ref, own_ref, other_ref,
    their_ref, dgate_all, dup_all, coef_ref, sems,
):
    tile = gw_ref.shape[1]
    rows = p0.shape[0]
    step = pl.program_id(0)
    difference = info_ref[:, MLP : MLP + router_ref.shape[1]]

    @pl.when(step == 0)
    def _():
        copies = [
            pltpu.make_async_copy(p, their_ref.at[pl.ds(i * rows, rows), :], sems.at[4 + i])
            for i, p in enumerate((p1, p3))
        ]
        for copy in copies:
            copy.start()
        assemble(shard_ref[0], (p0, p1, p2, p3), x_ref, sems)
        for copy in copies:
            copy.wait()
        logits = product(x_ref[...], router_ref[...])
        gate = jax.nn.sigmoid(jnp.sum(logits * difference, axis=1, keepdims=True))
        gate_ref[...] = jnp.broadcast_to(gate, gate_ref.shape)
        total_ref[...] = jnp.zeros_like(total_ref)

    chunk = chunk_of(x_ref.shape[0])
    at = pl.ds(pl.multiple_of(jnp.minimum(step, tiles - 1) * tile, 128), tile)

    def first_part(i):
        here = pl.ds(pl.multiple_of(i * chunk, 16), chunk)
        their = their_ref[here, :]
        gate_pre = gp_ref[here, :].astype(f32) + product(their, gw_ref[...])
        up_pre = up_ref[here, :].astype(f32) + product(their, uw_ref[...])
        plain, gate = plain_ref[here, :].astype(f32), gate_ref[here, :1]
        inside = lax.broadcasted_iota(jnp.int32, (1, tile), 1) + step * tile < columns
        sigmoid = jax.nn.sigmoid(gate_pre)
        silu = gate_pre * sigmoid
        hidden = (silu * up_pre).astype(bf16).astype(f32)
        gated = (gate * hidden).astype(bf16)
        hidden_ref[here, :] = gated
        total_ref[here, :] += jnp.sum(
            jnp.where(inside, gated.astype(f32) * plain, 0.0), axis=1, keepdims=True
        )
        hidden_grad = gate * plain
        up_grad = hidden_grad * silu
        dup_ref[here, :] = up_grad.astype(bf16)
        dup_all[here, at] = up_grad.astype(bf16)
        gate_grad = hidden_grad * up_pre * (sigmoid + silu * (1.0 - sigmoid))
        dgate_ref[here, :] = gate_grad.astype(bf16)
        dgate_all[here, at] = gate_grad.astype(bf16)

    @pl.when(step < tiles)
    def _():
        pl.loop(0, x_ref.shape[0] // chunk)(first_part)

    @pl.when(step == tiles)
    def _():
        coef_ref[...] = (1.0 - gate_ref[:, :1]) * total_ref[:, :1] * difference

    @pl.when(step >= tiles)
    def _():
        for t, out_ref in enumerate((own_ref, other_ref)):
            here = pl.ds(t * rows, rows)
            value = product_last(dgate_all[here, :columns], g_ref[...])
            value = value + product_last(dup_all[here, :columns], u_ref[...])
            value = value + product_last(coef_ref[here, :].astype(bf16), r_ref[...])
            out_ref[...] = value.astype(bf16)


def expert_in(shard, pieces, router, info, plain, begun, gate_weight, up_weight, tile=512, row_tile=256):
    rows, half = pieces[0].shape
    columns = gate_weight.shape[1]
    tile = min(tile, columns)
    tiles, steps = pl.cdiv(columns, tile), half // row_tile
    weight_spec = pl.BlockSpec((half, tile), lambda j, s: (1 - s[0], jnp.minimum(j, tiles - 1)))
    tile_spec = pl.BlockSpec((2 * rows, tile), lambda j, s: (0, jnp.minimum(j, tiles - 1)))
    out_spec = pl.BlockSpec((rows, row_tile), lambda j, s: (0, jnp.maximum(j - tiles, 0)))

    def row_spec(columns):
        return pl.BlockSpec(
            (row_tile, columns), lambda j, s: (steps * (1 - s[0]) + jnp.maximum(j - tiles, 0), 0)
        )

    held_spec = pl.BlockSpec((2 * rows, 128), lambda j, s: (0, 0))
    hidden_shape = jax.ShapeDtypeStruct((2 * rows, columns), bf16)
    return pl.pallas_call(
        functools.partial(expert_in_body, columns, tiles),
        grid_spec=pltpu.PrefetchScalarGridSpec(
            num_scalar_prefetch=1,
            grid=(tiles + steps,),
            in_specs=[pl.BlockSpec(memory_space=pl.ANY)] * 4
            + [
                pl.BlockSpec(router.shape, lambda j, s: (0, 0)),
                pl.BlockSpec(info.shape, lambda j, s: (0, 0)),
                tile_spec,
                tile_spec,
                tile_spec,
                weight_spec,
                weight_spec,
                row_spec(columns),
                row_spec(columns),
                row_spec(router.shape[1]),
            ],
            out_specs=[
                pl.BlockSpec((2 * rows, 2 * half), lambda j, s: (0, 0)),
                held_spec,
                held_spec,
                tile_spec,
                tile_spec,
                tile_spec,
                out_spec,
                out_spec,
            ],
            scratch_shapes=[
                pltpu.VMEM((2 * rows, half), bf16),
                pltpu.VMEM((2 * rows, tiles * tile), bf16),
                pltpu.VMEM((2 * rows, tiles * tile), bf16),
                pltpu.VMEM((2 * rows, router.shape[1]), f32),
                pltpu.SemaphoreType.DMA((6,)),
            ],
        ),
        out_shape=[
            jax.ShapeDtypeStruct((2 * rows, 2 * half), bf16),
            jax.ShapeDtypeStruct((2 * rows, 128), f32),
            jax.ShapeDtypeStruct((2 * rows, 128), f32),
            hidden_shape,
            hidden_shape,
            hidden_shape,
            jax.ShapeDtypeStruct((rows, half), bf16),
            jax.ShapeDtypeStruct((rows, half), bf16),
        ],
        compiler_params=pltpu.CompilerParams(vmem_limit_bytes=60 * 2**20),
        cost_estimate=pl.CostEstimate(
            flops=16 * rows * half * columns,
            bytes_accessed=16 * rows * half + 4 * half * columns + 36 * rows * columns,
            transcendentals=2 * rows * columns,
        ),
        name="expert_in",
    )(shard, *pieces, router, info, plain, *begun, gate_weight, up_weight, gate_weight, up_weight, router)


def attended_in_body(
    shard_ref, p0, p1, p2, p3, info_ref, mixed_ref, w_ref, x_ref, total_ref, y_ref, sems
):
    @pl.when(pl.program_id(0) == 0)
    def _():
        assemble(shard_ref[0], (p0, p1, p2, p3), x_ref, sems)
        total_ref[...] = jnp.zeros_like(total_ref)

    chunk = chunk_of(x_ref.shape[0])

    @pl.loop(0, x_ref.shape[0] // chunk)
    def _(i):
        here = pl.ds(pl.multiple_of(i * chunk, 16), chunk)
        plain = product(x_ref[here, :], w_ref[...])
        total_ref[here, :] += jnp.sum(mixed_ref[here, :].astype(f32) * plain, axis=1, keepdims=True)
        y_ref[here, :] = (info_ref[here, GATE : GATE + 1] * plain).astype(bf16)


def attended_in(shard, pieces, info, mixed, weight):
    rows, half = pieces[0].shape
    columns = weight.shape[1]
    tile = min(256, columns)
    return pl.pallas_call(
        attended_in_body,
        grid_spec=pltpu.PrefetchScalarGridSpec(
            num_scalar_prefetch=1,
            grid=(columns // tile,),
            in_specs=[pl.BlockSpec(memory_space=pl.ANY)] * 4
            + [
                pl.BlockSpec((2 * rows, 128), lambda j, s: (0, 0)),
                pl.BlockSpec((2 * rows, tile), lambda j, s: (0, j)),
                pl.BlockSpec((2 * half, tile), lambda j, s: (0, j)),
            ],
            out_specs=[
                pl.BlockSpec((2 * rows, 2 * half), lambda j, s: (0, 0)),
                pl.BlockSpec((2 * rows, 128), lambda j, s: (0, 0)),
                pl.BlockSpec((2 * rows, tile), lambda j, s: (0, j)),
            ],
            scratch_shapes=[pltpu.SemaphoreType.DMA((4,))],
        ),
        out_shape=[
            jax.ShapeDtypeStruct((2 * rows, 2 * half), bf16),
            jax.ShapeDtypeStruct((2 * rows, 128), f32),
            jax.ShapeDtypeStruct((2 * rows, columns), bf16),
        ],
        compiler_params=pltpu.CompilerParams(vmem_limit_bytes=limit_of(2 * rows)),
        cost_estimate=pl.CostEstimate(
            flops=8 * rows * half * columns,
            bytes_accessed=16 * rows * half + 4 * half * columns + 8 * rows * columns,
            transcendentals=0,
        ),
        name="attended_in",
    )(shard, *pieces, info, mixed, weight)


def rows_half_body(count, extra, gate_at, diff_at, shard_ref, *refs):
    lefts, weights = refs[:count], refs[count : 2 * count]
    rest = refs[2 * count :]
    if extra:
        total_ref, gate_ref, diff_ref, router_ref = rest[:4]
        rest = rest[4:]
        coef_ref = rest[2]

        @pl.when(pl.program_id(0) == 0)
        def _():
            gate = gate_ref[:, gate_at : gate_at + 1]
            difference = diff_ref[:, diff_at : diff_at + router_ref.shape[1]]
            coef_ref[...] = (1.0 - gate) * total_ref[:, :1] * difference

    rows = rest[0].shape[0]
    chunk = chunk_of(rows)
    for t in range(2):

        @pl.loop(0, rows // chunk)
        def _(i):
            here = pl.ds(pl.multiple_of(t * rows + i * chunk, 16), chunk)
            there = pl.ds(pl.multiple_of(i * chunk, 16), chunk)
            value = sum(product_last(a[here, :], w[...]) for a, w in zip(lefts, weights))
            if extra:
                value = value + product_last(coef_ref[here, :].astype(bf16), router_ref[...])
            rest[t][there, :] = value.astype(bf16)


def rows_half(shard, mine, lefts, weights, extra=None, tile=512):
    rows, width = lefts[0].shape[0] // 2, weights[0].shape[0]
    half = width // 2
    steps = half // tile

    def at(j, s):
        return j + steps * (s[0] if mine else 1 - s[0])

    def whole_spec(array):
        return pl.BlockSpec(array.shape, lambda j, s: (0, 0))

    in_specs = [whole_spec(a) for a in lefts]
    in_specs += [pl.BlockSpec((tile, w.shape[1]), lambda j, s: (at(j, s), 0)) for w in weights]
    operands = list(lefts) + list(weights)
    out_specs = [pl.BlockSpec((rows, tile), lambda j, s: (0, j))] * 2
    out_shape = [jax.ShapeDtypeStruct((rows, half), bf16)] * 2
    gate_at = diff_at = 0
    if extra:
        total, gate, gate_at, difference, diff_at, router = extra
        in_specs += [whole_spec(total), whole_spec(gate), whole_spec(difference)]
        in_specs += [pl.BlockSpec((tile, router.shape[1]), lambda j, s: (at(j, s), 0))]
        operands += [total, gate, difference, router]
        coefs = jax.ShapeDtypeStruct((2 * rows, router.shape[1]), f32)
        out_specs.append(whole_spec(coefs))
        out_shape.append(coefs)
    depth = sum(w.shape[1] for w in weights)
    return pl.pallas_call(
        functools.partial(rows_half_body, len(lefts), extra is not None, gate_at, diff_at),
        grid_spec=pltpu.PrefetchScalarGridSpec(
            num_scalar_prefetch=1, grid=(steps,), in_specs=in_specs, out_specs=out_specs
        ),
        out_shape=out_shape,
        compiler_params=pltpu.CompilerParams(vmem_limit_bytes=limit_of(2 * rows) if len(lefts) == 1 else 60 * 2**20),
        cost_estimate=pl.CostEstimate(
            flops=4 * rows * half * depth,
            bytes_accessed=4 * rows * depth + 2 * half * depth + 4 * rows * half,
            transcendentals=0,
        ),
        name="rows_mine" if mine else "rows_theirs",
    )(shard, *operands)


def prepare_body(
    capacity, scalars, tokens_ref, gain_ref, order_ref, attn_ref, mlp_ref, segment_ref, parent_ref,
    block_ref, attn_pack_ref, mlp_pack_ref, tile_ref,
):
    width = tokens_ref.shape[2]
    count = tokens_ref.shape[1]
    values = tokens_ref[0].astype(f32)
    scales = lax.rsqrt(jnp.mean(values * values, axis=1, keepdims=True) + epsilon)
    block_ref[:, :width] = (values * scales * gain_ref[...]).astype(bf16)

    ranks = order_ref[0].astype(f32)
    pairs = lax.broadcasted_iota(jnp.int32, (2 * count, count), 0)
    owners = lax.broadcasted_iota(jnp.int32, (2 * count, count), 1)
    turns = [(pairs == 2 * owners + k).astype(f32) for k in range(2)]
    rank_rows = [product(ranks, turn) for turn in turns]
    rank_columns = [
        lax.dot_general(turn, ranks, (((0,), (1,)), ((), ())), preferred_element_type=f32)
        for turn in turns
    ]
    same = (
        lax.broadcasted_iota(jnp.int32, (count, count), 0)
        == lax.broadcasted_iota(jnp.int32, (count, count), 1)
    ).astype(f32)
    places = lax.broadcasted_iota(jnp.int32, attn_pack_ref.shape, 0).astype(f32)
    tile_ref[...] = jnp.zeros_like(tile_ref)
    for at, (route_ref, pack_ref) in enumerate(((attn_ref, attn_pack_ref), (mlp_ref, mlp_pack_ref))):
        rows = route_ref[...].astype(f32)
        routes = product_last(same, rows)
        hit = None
        for k in range(2):
            route = rows[k : k + 1]
            slot = jnp.zeros((1, count), f32)
            for other in range(2):
                earlier = (routes[:, other : other + 1] == route) & (
                    rank_columns[other] < rank_rows[k]
                )
                slot = slot + jnp.sum(earlier.astype(f32), axis=0, keepdims=True)
            slot = jnp.minimum(slot, float(capacity))
            tile_ref[4 * at + 2 * k : 4 * at + 2 * k + 1, :] = route
            tile_ref[4 * at + 2 * k + 1 : 4 * at + 2 * k + 2, :] = slot
            code = jnp.where(slot < capacity, route * capacity + slot, -1.0)
            here = places == code
            hit = here if hit is None else hit | here
        pack_ref[...] = hit.astype(bf16)
    tile_ref[8:9, :] = segment_ref[...].astype(f32)
    tile_ref[9:10, : parent_ref.shape[1]] = parent_ref[...].astype(f32)
    block_ref[:, width:] = jnp.zeros((count, block_ref.shape[1] - width), bf16)
    block_ref[:16, width : width + count] = tile_ref[...].astype(bf16)


def prepare(place, tokens, gain, order, attn_routes, mlp_routes, segments, parents, experts, capacity):
    _, count, width = tokens.shape

    def whole_spec(array):
        return pl.BlockSpec(array.shape, lambda i, s: (0,) * array.ndim)

    pack = jax.ShapeDtypeStruct((experts * capacity, count), bf16)
    return pl.pallas_call(
        functools.partial(prepare_body, capacity),
        grid_spec=pltpu.PrefetchScalarGridSpec(
            num_scalar_prefetch=1,
            grid=(1,),
            in_specs=[whole_spec(a) for a in (tokens, gain, order, attn_routes, mlp_routes)]
            + [pl.BlockSpec((1, count), lambda i, s: (0, s[0])), whole_spec(parents)],
            out_specs=[
                pl.BlockSpec((count, width + 128), lambda i, s: (0, 0)),
                pl.BlockSpec(pack.shape, lambda i, s: (0, 0)),
                pl.BlockSpec(pack.shape, lambda i, s: (0, 0)),
            ],
            scratch_shapes=[pltpu.VMEM((16, count), f32)],
        ),
        out_shape=[jax.ShapeDtypeStruct((count, width + 128), bf16), pack, pack],
        compiler_params=pltpu.CompilerParams(vmem_limit_bytes=24 * 2**20),
        name="prepare",
    )(place, tokens, gain, order, attn_routes, mlp_routes, segments, parents)


def difference_of(expert, other, experts):
    range_of = lax.broadcasted_iota(jnp.int32, (other.shape[0], experts), 1).astype(f32)
    return (range_of == expert).astype(f32) - (range_of == other).astype(f32)


def front_body(
    capacity, steps, scalars, own_ref, other_ref, own_marks_ref, other_marks_ref, router_ref,
    key_hbm, value_hbm, got_key_hbm, got_value_hbm, shared_ref, picked_ref, bias_ref, info_ref, weight, sems,
):
    piece = weight.shape[1] // 2
    heads = piece // HEAD

    turn = pl.program_id(0)

    def fetch(sources, at):
        for h in range(heads):
            for i, source in enumerate(sources):
                from_here = source.at[:, pl.ds(pl.multiple_of(at + h * HEAD, HEAD), HEAD)]
                place = weight.at[:, pl.ds((2 * h + i) * HEAD, HEAD)]
                pltpu.make_async_copy(from_here, place, sems.at[h]).start()

    @pl.when((turn == 0) & (scalars[0] == 1))
    def _():
        fetch((key_hbm, value_hbm), scalars[1] * piece)

    @pl.when((turn == 0) & (scalars[0] == 0))
    def _():
        fetch((got_key_hbm, got_value_hbm), 0)

    def one_step(step, rows_ref, marks_ref):
        front_step(
            capacity, heads, turn, step, scalars, rows_ref, marks_ref, router_ref,
            shared_ref, picked_ref, bias_ref, info_ref, weight, sems,
        )

    @pl.when(turn < steps)
    def _():
        one_step(turn, own_ref, own_marks_ref)

    @pl.when(turn >= steps)
    def _():
        one_step(turn - steps, other_ref, other_marks_ref)


def front_step(
    capacity, heads, turn, step, scalars, rows_ref, marks_ref, router_ref,
    shared_ref, picked_ref, bias_ref, info_ref, weight, sems,
):
    count = rows_ref.shape[1]
    width = weight.shape[0]
    blocks = marks_ref.shape[0]
    rows = jnp.concatenate([rows_ref[0, :, :width], rows_ref[1, :, :width]])
    expert = scalars[2].astype(f32)
    index = lax.broadcasted_iota(jnp.int32, (2 * capacity, count), 0)
    lanes = lax.broadcasted_iota(jnp.int32, (2 * capacity, count), 1).astype(f32)
    first = index < capacity
    slots = jnp.where(first, index, index - capacity).astype(f32)
    upper = marks_ref[2 * step].astype(f32)
    lower = marks_ref[2 * step + 1].astype(f32)

    def mark(i):
        return jnp.where(first, upper[i : i + 1, :count], lower[i : i + 1, :count])

    def total(values):
        return jnp.sum(values, axis=1, keepdims=True)

    def hits_of(at):
        hits = [(mark(at + 2 * k) == expert) & (mark(at + 2 * k + 1) == slots) for k in range(2)]
        other = total(jnp.where(hits[0], mark(at + 2), 0.0) + jnp.where(hits[1], mark(at), 0.0))
        return hits[0] | hits[1], other

    experts = router_ref.shape[1]
    info_ref[:, MLP : MLP + experts] = difference_of(expert, hits_of(4)[1], experts)
    hit, other = hits_of(0)
    difference = difference_of(expert, other, experts)
    info_ref[:, ATTN : ATTN + experts] = difference

    own = total(jnp.where(hit, mark(8), 0.0))
    parents = mark(9)
    one = total(jnp.where(lanes == own, parents, 0.0))
    two = total(jnp.where(lanes == one, parents, 0.0))
    start = jnp.where(first[:, :1], 2 * step * count, (2 * step + 1) * count).astype(f32)
    place = total(jnp.where(hit, lanes, 0.0)) + start
    for j in range(blocks):
        keys = marks_ref[j, 8:9, :count].astype(f32)
        seen = ((keys == own) | (keys == one) | (keys == two)) & (lanes + float(j * count) <= place)
        bias_ref[:, j * count : (j + 1) * count] = jnp.where(seen, 0.0, negative).astype(bf16)

    both = jnp.concatenate([(hit & first).astype(bf16), (hit & ~first).astype(bf16)], axis=1)
    picked = product(both, rows).astype(bf16)
    picked_ref[...] = picked
    logits = product(picked, router_ref[...])
    info_ref[:, GATE : GATE + 1] = jax.nn.sigmoid(total(logits * difference))

    @pl.when(turn == 0)
    def _():
        for h in range(heads):
            here = pl.ds(2 * h * HEAD, 2 * HEAD)
            pltpu.make_async_copy(weight.at[:, here], weight.at[:, here], sems.at[h]).wait()
            shared_ref[:, here] = product(rows, weight[:, here]).astype(bf16)

    @pl.when(turn > 0)
    def _():
        shared_ref[...] = product(rows, weight[...]).astype(bf16)


def front(scalars, own, other, router, key_weight, value_weight, got_key, got_value, capacity):
    blocks, count, columns = own.shape
    width, piece = got_key.shape
    length = blocks * count
    rows = blocks * capacity
    steps = blocks // 2
    pinned_spec = pl.BlockSpec(memory_space=pltpu.HBM)
    marks_spec = pl.BlockSpec((blocks, 16, 128), lambda i, s: (0, 0, width // 128))

    def out_spec(height, columns):
        return pl.BlockSpec((height, columns), lambda i, s: (i, 0))

    pair = 2 * capacity
    return pl.pallas_call(
        functools.partial(front_body, capacity, steps),
        grid_spec=pltpu.PrefetchScalarGridSpec(
            num_scalar_prefetch=1,
            grid=(2 * steps,),
            in_specs=[
                pl.BlockSpec((2, count, columns), lambda i, s: (jnp.minimum(i, steps - 1), 0, 0)),
                pl.BlockSpec((2, count, columns), lambda i, s: (jnp.maximum(i - steps, 0), 0, 0)),
                marks_spec,
                marks_spec,
                pl.BlockSpec(router.shape, lambda i, s: (0, 0)),
            ]
            + [pinned_spec] * 4,
            out_specs=[
                out_spec(2 * count, 2 * piece),
                out_spec(pair, width),
                out_spec(pair, length),
                out_spec(pair, 128),
            ],
            scratch_shapes=[
                pltpu.VMEM((width, 2 * piece), bf16),
                pltpu.SemaphoreType.DMA((piece // HEAD,)),
            ],
        ),
        out_shape=[
            jax.ShapeDtypeStruct((2 * length, 2 * piece), bf16),
            jax.ShapeDtypeStruct((2 * rows, width), bf16),
            jax.ShapeDtypeStruct((2 * rows, length), bf16),
            jax.ShapeDtypeStruct((2 * rows, 128), f32),
        ],
        compiler_params=pltpu.CompilerParams(vmem_limit_bytes=60 * 2**20),
        cost_estimate=pl.CostEstimate(
            flops=8 * length * width * piece,
            bytes_accessed=4 * length * width + 4 * width * piece,
            transcendentals=0,
        ),
        name="front",
    )(scalars, own, other, own, other, router, key_weight, value_weight, got_key, got_value)


def shared_out_body(steps, scalars, sums_ref, key_ref, value_ref, got_key_ref, got_value_ref, *outs):
    step = pl.program_id(0)
    sums = sums_ref[...]
    heads = sums.shape[0] // 2

    def part(t, i):
        return jnp.concatenate([sums[2 * h + i, t] for h in range(heads)], axis=1)

    def fill(pair, keys, values):
        for t in range(2):
            value = product_last(part(t, 0), keys[...]) + product_last(part(t, 1), values[...])
            pair[t][...] = value.astype(bf16)

    for side in range(2):
        for local in range(2):
            first = step < steps // 2 if side == 0 else step >= steps // 2

            @pl.when(first & (scalars[1] == local))
            def _():
                pair = (outs[side], outs[2 + side])
                if local:
                    fill(pair, key_ref, value_ref)
                else:
                    fill(pair, got_key_ref, got_value_ref)


def shared_out(scalars, sums, key_weight, value_weight, got_key, got_value, tile=512):
    rows = sums.shape[2]
    width, piece = got_key.shape
    half, steps = width // 2, width // tile

    def at(j, s):
        return lax.rem(j + steps // 2 * (1 - s[0]), steps)

    local = pl.BlockSpec((tile, piece), lambda j, s: (at(j, s), s[2]))
    sent = pl.BlockSpec((tile, piece), lambda j, s: (at(j, s), 0))
    theirs = pl.BlockSpec((rows, tile), lambda j, s: (0, jnp.minimum(j, steps // 2 - 1)))
    mine = pl.BlockSpec((rows, tile), lambda j, s: (0, jnp.maximum(j - steps // 2, 0)))
    return pl.pallas_call(
        functools.partial(shared_out_body, steps),
        grid_spec=pltpu.PrefetchScalarGridSpec(
            num_scalar_prefetch=1,
            grid=(steps,),
            in_specs=[pl.BlockSpec(sums.shape, lambda j, s: (0, 0, 0, 0)), local, local, sent, sent],
            out_specs=[theirs, mine, theirs, mine],
        ),
        out_shape=[jax.ShapeDtypeStruct((rows, half), bf16)] * 4,
        compiler_params=pltpu.CompilerParams(vmem_limit_bytes=60 * 2**20),
        cost_estimate=pl.CostEstimate(
            flops=8 * rows * width * piece,
            bytes_accessed=8 * width * piece + 8 * rows * width,
            transcendentals=0,
        ),
        name="shared_out",
    )(scalars, sums, key_weight, value_weight, got_key, got_value)


def per_device(
    tokens,
    cotangent,
    attn_gain,
    mlp_gain,
    key_weight,
    value_weight,
    query_weight,
    output_weight,
    attn_router,
    gate_weight,
    up_weight,
    down_weight,
    mlp_router,
    segment_ids,
    parent_ids,
    attn_routes,
    mlp_routes,
    slot_order,
):
    count, width = tokens.shape[1:]
    half = width // 2
    piece = query_weight.shape[1]
    experts = attn_router.shape[1]
    blocks = lax.axis_size("dp")
    members = blocks // experts
    capacity = min(count, 5 * count * attn_routes.shape[2] // (4 * experts))
    length, parents = segment_ids.shape[1], parent_ids.shape[1]
    tiles = max(2, length // 512)
    dp, core, shard = lax.axis_index("dp"), lax.axis_index("expert"), lax.axis_index("shard")
    expert, member = dp // members, dp % members

    def my_half(values):
        return lax.dynamic_slice_in_dim(values, shard * half, half, values.ndim - 1)

    def whole(mine):
        got = swap(mine, "shard")
        first = shard == 0
        return jnp.concatenate(
            [jnp.where(first, mine, got), jnp.where(first, got, mine)], axis=mine.ndim - 1
        )

    block, attn_pack, mlp_pack = prepare(
        jnp.reshape(dp, (1,)).astype(jnp.int32),
        tokens,
        attn_gain[None],
        slot_order,
        attn_routes[0].T,
        mlp_routes[0].T,
        segment_ids,
        parent_ids,
        experts,
        capacity,
    )
    heads_at = (member * 2 + core) * 2 + shard
    holder = (member * 2 + core) // members
    offset = holder * 2 * members
    names = ("dp", "expert", "shard")
    sends = []
    for d in range(blocks):
        for c in range(2):
            at = (d * 2 + c) * 2
            source = ((d % members) * 2 + c) // members
            sends.append((at + source, at + 1 - source))
    partner_at = (member * 2 + core) * 2 + 1 - shard

    def partner_columns(weight):
        columns = lax.dynamic_slice_in_dim(weight, (partner_at - offset) * piece, piece, 1)
        return lax.ppermute(columns, names, sends)

    grad_half = lax.dynamic_slice_in_dim(cotangent[0], shard * half, half, 1)

    def pack_rows(values, pack):
        packed = product(pack, values).astype(bf16).reshape(experts, 1, capacity, half)
        packed = jnp.broadcast_to(packed, (experts, members, capacity, half))
        return packed.reshape(blocks, capacity, half)

    works = [None] * (blocks // 2)
    works[-1] = lambda event: [pack_rows(after(grad_half, event), mlp_pack)]
    own_blocks, made = ring_gather(block, "dp", blocks, 1, works)
    grad_packed = made[-1][0]
    got_key, got_value = partner_columns(key_weight), partner_columns(value_weight)
    own_blocks, got_key, got_value = lax.optimization_barrier((own_blocks, got_key, got_value))
    tree_blocks = [own_blocks, swap(own_blocks, "expert")]

    local = (shard == holder).astype(jnp.int32)
    local_at = local * (heads_at - offset)
    shard_index = jnp.reshape(shard, (1,)).astype(jnp.int32)

    def dispatch(packed, work=None, begin=None):
        arrived = lax.all_to_all(packed, "dp", 0, 0, tiled=True)
        done = []
        if work:
            arrived, *done = lax.optimization_barrier((arrived, *work(packed)))
        arrived = arrived.reshape(blocks * capacity, half)
        other = swap(arrived, "expert")
        got = swap(arrived, "shard")
        begun = []
        if begin:
            got, *begun = lax.optimization_barrier((got, *begin(arrived, other)))
        return [arrived, got, other, swap(got, "expert")], done, begun

    def join_ends(sides, work=None):
        own, other, *_ = sides(False, None)
        theirs = (own.astype(f32) + swap(other, "expert").astype(f32)).astype(bf16)
        back, own, other, *rest = lax.optimization_barrier(
            (swap(theirs, "shard"), *sides(True, theirs), *(work(theirs) if work else []))
        )
        total = own.astype(f32) + swap(other, "expert").astype(f32) + back.astype(f32)
        return total, rest

    def sum_tokens(back, pack):
        if members > 1:
            back = back.reshape(experts, members, capacity, half).astype(f32)
            back = jnp.sum(back, axis=1).astype(bf16)
        return product_first(pack, back.reshape(experts * capacity, half))

    def send_back(joined, work=None):
        back = lax.all_to_all(joined, "dp", 0, 0, tiled=True)
        done = []
        if work:
            back, *done = lax.optimization_barrier((back, *work(joined)))
        return back, done

    def for_tokens(joined):
        return joined.astype(bf16).reshape(blocks, capacity, half)

    grad_arrived = lax.all_to_all(grad_packed, "dp", 0, 0, tiled=True)
    grad_arrived = grad_arrived.reshape(blocks * capacity, half)
    scalars = jnp.stack([local, local_at, expert]).astype(jnp.int32)
    shared, rows, bias, info = front(
        scalars, *tree_blocks, attn_router, key_weight, value_weight, got_key, got_value, capacity
    )
    grad_got = swap(after(grad_arrived, rows), "shard")
    queries = product(rows, query_weight).astype(bf16)
    mixed, log_total = attend(queries, shared, bias, info, tiles)
    mixed, grad_got = lax.optimization_barrier((mixed, grad_got))
    grad_pieces = (grad_arrived, grad_got, swap(grad_arrived, "expert"), swap(grad_got, "expert"))

    def attn_sides(mine, event):
        return rows_half(shard_index, mine, [after(mixed, event)], [output_weight])

    def plain_work(event):
        return plain_in(shard_index, after(grad_pieces, event), down_weight)

    attn_joined, (grad_rows, plain_grad) = join_ends(attn_sides, plain_work)
    back = send_back(for_tokens(attn_joined))[0]
    inputs = tokens[0].astype(f32)
    attn_scale = lax.rsqrt(jnp.mean(inputs * inputs, axis=1, keepdims=True) + epsilon)
    middle = my_half(inputs) + sum_tokens(back, attn_pack)

    def feature_mean(values):
        part = jnp.sum(values, axis=1, keepdims=True)
        return (part + swap(part, "shard")) / width

    mlp_scale = lax.rsqrt(feature_mean(middle * middle) + epsilon)
    half_gain = my_half(mlp_gain)
    mlp_normed = (middle * mlp_scale * half_gain).astype(bf16)

    def begin(own, other):
        return expert_begin(shard_index, own, other, gate_weight, up_weight)

    mlp_pieces, _, begun = dispatch(pack_rows(mlp_normed, mlp_pack), None, begin)
    mlp_rows, mlp_gate, mlp_total, gated_hidden, gate_pre_grad, up_pre_grad, *theirs_rows = expert_in(
        shard_index, mlp_pieces, mlp_router, info, plain_grad, begun, gate_weight, up_weight
    )

    def mlp_sides(mine, event):
        if not mine:
            return theirs_rows
        return rows_half(
            shard_index,
            mine,
            after([gate_pre_grad, up_pre_grad], event),
            [gate_weight, up_weight],
            (mlp_total, mlp_gate, 0, info, MLP, mlp_router),
        )

    def term_half(mine, event):
        return rows_half(shard_index, mine, [after(gated_hidden, event)], [down_weight])

    row_joined, (mlp_coefs,) = join_ends(mlp_sides)
    row_joined = for_tokens(row_joined)

    def gate_work(event):
        own, other = term_half(False, event)
        theirs = own.astype(f32) + swap(other, "expert").astype(f32)
        return [theirs.astype(bf16), product_first(after(mlp_rows, own), gate_pre_grad)]

    back, (term_theirs, gate_grad) = send_back(row_joined, gate_work)
    mlp_normed_grad = sum_tokens(back, mlp_pack)

    mlp_n = middle * mlp_scale
    weighted = mlp_normed_grad * half_gain
    mlp_gain_part = jnp.sum(mlp_normed_grad * mlp_n, axis=0)
    middle_grad = grad_half.astype(f32) + mlp_scale * (
        weighted - mlp_n * feature_mean(weighted * mlp_n)
    )
    low_grad = middle_grad.astype(bf16)

    def up_work(event):
        up_grad = product_first(after(mlp_rows, event), up_pre_grad)
        router_part = product_first(mlp_coefs, after(mlp_rows, event).astype(f32))
        return [up_grad, router_part]

    def down_work(own, other):
        return [product_first(after(grad_rows, own), gated_hidden)]

    packed = pack_rows(low_grad, attn_pack)
    term_pieces, (up_grad, mlp_router_part), (down_grad,) = dispatch(packed, up_work, down_work)
    term_back = swap(after(term_theirs, packed), "shard")
    own, other = term_half(True, packed)
    total = own.astype(f32) + swap(other, "expert").astype(f32) + term_back.astype(f32)
    term_joined = after(for_tokens(total), term_pieces[0])
    term_back = lax.all_to_all(term_joined, "dp", 0, 0, tiled=True)
    term_rows, attn_total, attended_grad = attended_in(
        shard_index, term_pieces, info, mixed, output_weight
    )
    query_rows_grad, held = attend_back(queries, shared, bias, log_total, attended_grad, tiles)
    held, term_back = lax.optimization_barrier((held, term_back))
    part = length // experts
    cut = experts * HEAD // (2 * piece)

    def cut_parts(values):
        shape = values.shape
        values = values.reshape(shape[:-1] + (cut, shape[-1] // cut))
        return jnp.moveaxis(values, -2, 1).reshape((experts,) + shape[1:-1] + (-1,))

    def join_parts(values):
        shape = values.shape
        values = jnp.moveaxis(values.reshape((experts // cut, cut) + shape[1:]), 1, -2)
        return values.reshape(values.shape[:-2] + (-1,))

    rings = None
    if members > 1:
        rings = [[e * members + m for e in range(experts)] for m in range(members)]

    def to_experts(values):
        return lax.all_to_all(values, "dp", 0, 0, axis_index_groups=rings, tiled=True)

    held = cut_parts(held)
    def input_rows(mine, event):
        return rows_half(
            shard_index,
            mine,
            [after(query_rows_grad, event)],
            [query_weight],
            (attn_total, info, GATE, info, ATTN, attn_router),
        )

    kept = []

    def theirs_work(event):
        own, other, _ = input_rows(False, event)
        theirs = own.astype(f32) + swap(other, "expert").astype(f32)
        kept.append(theirs.astype(bf16))
        return kept[:]

    def mine_work(event):
        kept.append(swap(after(kept[0], event), "shard"))
        kept.extend(input_rows(True, event))
        return kept[2:] + [product_first(after(rows, event), query_rows_grad)]

    def output_work(event):
        return [kept[1], product_first(after(term_rows, event), mixed)]

    works = [theirs_work, mine_work, None, output_work]
    key_sums, made = ring_scatter(held, experts, members, works)
    key_sums = key_sums.astype(bf16)
    _, (own, other, attn_coefs, query_grad), _, (back, output_grad) = made
    total = own.astype(f32) + swap(other, "expert").astype(f32) + back.astype(f32)
    input_joined = for_tokens(total)
    scalars = jnp.stack([shard, local, local_at]).astype(jnp.int32)

    def weight_work(event):
        sums = after(key_sums, event)
        sums = sum(product_first(tree_blocks[t].reshape(length, -1), sums[t]) for t in range(2))
        return [sums[:width].astype(bf16).reshape(experts, width // experts, -1)]

    def shared_work(event):
        parts = shared_out(
            scalars, after(token_sums, event), key_weight, value_weight, got_key, got_value
        )
        theirs = parts[0].astype(f32) + swap(parts[2], "expert").astype(f32)
        shared = parts[1].astype(f32) + swap(parts[3], "expert").astype(f32)
        return [shared, swap(theirs.astype(bf16), "shard")]

    token_sums = key_sums.reshape(2, experts, part, -1).transpose(1, 0, 2, 3)
    (token_sums,), (weight_sums,) = pinned((to_experts(token_sums),), weight_work, token_sums)
    token_sums = join_parts(token_sums)
    input_joined = after(input_joined, token_sums)
    back = lax.all_to_all(input_joined, "dp", 0, 0, tiled=True)
    (back,), (shared, theirs) = pinned((back,), shared_work, input_joined)
    shared = shared + theirs.astype(f32)
    if members > 1:
        groups = [[e * members + m for m in range(members)] for e in range(experts)]
        shared = lax.psum_scatter(
            shared, "dp", scatter_dimension=0, axis_index_groups=groups, tiled=True
        )
    attn_n = my_half(inputs) * attn_scale
    features = width // (2 * blocks)

    def spread(values):
        return lax.dynamic_update_slice(jnp.zeros((1, width), f32), values[None], (0, shard * half))

    normed_grad = sum_tokens(back, attn_pack) + shared
    gain_part = jnp.sum(normed_grad * attn_n, axis=0)

    def last_work(event):
        grad = after(normed_grad, event)
        weighted = grad * my_half(attn_gain)
        grad = middle_grad + attn_scale * (weighted - attn_n * feature_mean(weighted * attn_n))
        return [grad, swap(grad.astype(bf16), "shard")]

    attn_router_part = product_first(attn_coefs, after(rows, key_sums).astype(f32))
    small = [attn_router_part, mlp_router_part, spread(gain_part), spread(mlp_gain_part)]
    small = jnp.pad(jnp.concatenate(small), ((0, 6), (0, 0)))
    small = small.reshape(-1, blocks, 2, features).transpose(1, 2, 0, 3)
    small = small.reshape(blocks, -1, features).astype(bf16)
    if members > 1:
        (weight_sums,), (tokens_grad, got) = pinned((to_experts(weight_sums),), last_work, small)
        small = lax.all_to_all(small, "dp", 0, 0, tiled=True)
    else:
        height = weight_sums.shape[1]
        both = jnp.concatenate([weight_sums, small], axis=1)
        (both,), (tokens_grad, got) = pinned((to_experts(both),), last_work, both)
        weight_sums, small = both[:, :height], both[:, height:]
    weight_sums = join_parts(weight_sums)
    small = jnp.sum(small.astype(f32), axis=0).reshape(2, -1, features)
    mine = lax.dynamic_index_in_dim(small, core, 0, keepdims=False)
    theirs = lax.dynamic_index_in_dim(small, 1 - core, 0, keepdims=False)
    small = mine + swap(theirs, "expert")
    small = small + swap(small, "shard")
    layer_out = whole((middle + sum_tokens(term_back, mlp_pack)).astype(bf16))[None]
    got = got.astype(f32)
    tokens_grad = jnp.concatenate(
        [jnp.where(shard == 0, tokens_grad, got), jnp.where(shard == 0, got, tokens_grad)], axis=1
    )[None]

    heads = piece // HEAD
    pieces = weight_sums.reshape(2 * heads, members, 2, features, HEAD).transpose(1, 2, 0, 3, 4)
    if members > 1:
        pieces = lax.all_to_all(pieces, "dp", 0, 0, axis_index_groups=groups, tiled=True)
    pieces = pair_all_to_all(pieces.transpose(1, 0, 2, 3, 4), "expert")
    pieces = pieces.transpose(1, 0, 2, 3, 4).reshape(2, members, 2 * heads, features, HEAD)
    pieces = pair_all_to_all(pieces, "shard").reshape(2, members, heads, 2, features, HEAD)
    pieces = pieces.transpose(3, 4, 1, 0, 2, 5).reshape(2, features, -1).astype(f32)

    return (
        layer_out,
        tokens_grad,
        small[2 * experts],
        small[2 * experts + 1],
        pieces[0],
        pieces[1],
        query_grad,
        output_grad,
        small[:experts].T,
        gate_grad,
        up_grad,
        down_grad,
        small[experts : 2 * experts].T,
    )


def solution(mesh):
    tree = P("expert", "dp", None)
    columns = P(None, ("dp", "expert", "shard"))
    spread = P(("dp", "expert"), None)
    in_specs = (
        tree,
        tree,
        P(),
        P(),
        P(None, "shard"),
        P(None, "shard"),
        columns,
        columns,
        P(),
        columns,
        columns,
        columns,
        P(),
        P("expert", None),
        P("expert", None),
        tree,
        tree,
        tree,
    )
    out_specs = (
        tree,
        tree,
        P(("dp", "expert")),
        P(("dp", "expert")),
        P(("dp", "expert"), "shard"),
        P(("dp", "expert"), "shard"),
        columns,
        columns,
        spread,
        columns,
        columns,
        columns,
        spread,
    )
    return jax.shard_map(
        per_device, mesh=mesh, in_specs=in_specs, out_specs=out_specs, check_vma=False
    )
```

```python
import functools

import jax
import jax.numpy as jnp
from jax import lax
from jax.experimental import pallas as pl
from jax.experimental.pallas import tpu as pltpu
from jax.sharding import PartitionSpec as P

HEAD = 128

epsilon = 1e-06
negative = -1e30
ATTN, MLP, GATE = 0, 32, 64
scale = HEAD ** (-0.5)
bf16 = jnp.bfloat16
f32 = jnp.float32


def product(former, latter):
    return jnp.dot(former, latter, preferred_element_type=f32)


def product_last(former, latter):
    return lax.dot_general(
        former, latter, (((1,), (1,)), ((), ())), preferred_element_type=f32
    )


def product_first(former, latter):
    return lax.dot_general(
        former, latter, (((0,), (0,)), ((), ())), preferred_element_type=f32
    )


def limit_of(rows):
    return min(56, max(40, rows * 24 // 640)) * 2**20


def grant(size, rows):
    return min(60, size * max(1, rows // 640)) * 2**20


def swap(values, axis):
    return lax.ppermute(values, axis, [(0, 1), (1, 0)])


def pair_all_to_all(parts, axis):
    me = lax.axis_index(axis)
    mine = lax.dynamic_index_in_dim(parts, me, 0, keepdims=False)
    theirs = lax.dynamic_index_in_dim(parts, 1 - me, 0, keepdims=False)
    got = swap(theirs, axis)
    first = me == 0
    return jnp.stack([jnp.where(first, mine, got), jnp.where(first, got, mine)])


def ring_order(count):
    return list(range(0, count, 2)) + list(range(1, count, 2))[::-1]


def ring_member(place, count):
    place = lax.rem(place + 2 * count, count)
    return jnp.where(place < count // 2, 2 * place, 2 * (count - place) - 1)


def ring_place(member, count):
    return jnp.where(member % 2 == 0, member // 2, count - (member + 1) // 2)


def empty(shape, dtype):
    return pl.pallas_call(
        lambda ref: None,
        out_shape=jax.ShapeDtypeStruct(shape, dtype),
        out_specs=pl.BlockSpec(memory_space=pl.ANY),
        name="empty",
    )()


def pinned(values, work, event):
    *values, made = lax.optimization_barrier((*values, work(event) if work else []))
    return values, made


def ring_gather(block, axis, count, stride, works=()):
    works = list(works) + [None] * (count // 2)
    order = ring_order(count)
    member = lax.axis_index(axis) // stride
    place = ring_place(member, count)
    right, left = ring_moves(order, 1, stride), ring_moves(order, -1, stride)
    rows, columns = block.shape
    half = rows // 2
    out = empty((count, rows, columns), block.dtype)

    def put(out, piece, source, row):
        return lax.dynamic_update_slice(out, piece[None], (source, row, 0))

    out = put(out, block, member, 0)
    forward, backward = block, block
    results = []
    for step in range(1, count // 2 + 1):
        last = step == count // 2
        if last:
            forward, backward = forward[:half], backward[half:]
        event = forward
        forward = lax.ppermute(forward, axis, right)
        backward = lax.ppermute(backward, axis, left)
        (forward, backward), made = pinned((forward, backward), works[step - 1], event)
        results.append(made)
        out = put(out, forward, ring_member(place - step, count), 0)
        out = put(out, backward, ring_member(place + step, count), half if last else 0)
    return out, results


def ring_moves(order, by, stride):
    count = len(order)
    return [
        (order[i] * stride + j, order[(i + by) % count] * stride + j)
        for i in range(count)
        for j in range(stride)
    ]


def after(values, *events):
    if events[0] is None:
        return values
    return lax.optimization_barrier((values,) + events)[0]


def ring_scatter(parts, count, stride, works=()):
    works = list(works) + [None] * (count // 2)
    order = ring_order(count)
    place = ring_place(lax.axis_index("dp") // stride, count)
    right, left = ring_moves(order, 1, stride), ring_moves(order, -1, stride)
    far = count // 2

    def part(offset):
        return lax.dynamic_index_in_dim(parts, ring_member(place + offset, count), 0, keepdims=False)

    def added(sent, offset, first):
        own = part(offset).astype(f32)
        if first is not None:
            sent = jnp.pad(sent, ((first, 1 - first), (0, 0), (0, 0)))
        return (own + sent.astype(f32)).astype(bf16)

    forward, backward = part(far)[:1], part(-far)[1:]
    results = []
    for step in range(far):
        event = forward
        forward = lax.ppermute(forward, "dp", right)
        backward = lax.ppermute(backward, "dp", left)
        (forward, backward), made = pinned((forward, backward), works[step], event)
        results.append(made)
        offset = far - 1 - step
        if offset:
            forward = added(forward, offset, 0 if step == 0 else None)
            backward = added(backward, -offset, 1 if step == 0 else None)
    return part(0).astype(f32) + forward.astype(f32) + backward.astype(f32), results


def attend_body(tiles, keys_per_tile, q_ref, k_ref, v_ref, bias_ref, info_ref, out_ref, total_ref):
    rows = q_ref.shape[0] // tiles
    lanes = lax.broadcasted_iota(jnp.int32, (rows, 128), 1)
    for tile in range(tiles):
        here = pl.ds(tile * rows, rows)
        keys = (tile + 1) * keys_per_tile
        scores = product_last(q_ref[here, :], k_ref[:keys, :]) * scale
        scores = scores + bias_ref[here, :keys].astype(f32)
        highest = jnp.max(scores, axis=1, keepdims=True)
        expo = jnp.exp(scores - highest)
        summed = jnp.sum(expo, axis=1, keepdims=True)
        mixed = product(expo.astype(bf16), v_ref[:keys, :]) * (1.0 / summed)
        mixed = mixed.astype(bf16).astype(f32)
        out_ref[here, :] = (mixed * info_ref[here, GATE : GATE + 1]).astype(bf16)
        total = highest + jnp.log(summed)
        total_ref[here, :] = jnp.where(lanes == pl.program_id(1), total, total_ref[here, :])


def attend(queries, shared, bias, info, tiles):
    rows, columns = queries.shape[0] // 2, queries.shape[1]
    length = shared.shape[0] // 2
    heads = columns // HEAD
    return pl.pallas_call(
        functools.partial(attend_body, tiles, length // tiles),
        grid=(2, heads),
        in_specs=[
            pl.BlockSpec((rows, HEAD), lambda t, h: (t, h)),
            pl.BlockSpec((length, HEAD), lambda t, h: (t, 2 * h)),
            pl.BlockSpec((length, HEAD), lambda t, h: (t, 2 * h + 1)),
            pl.BlockSpec((rows, length), lambda t, h: (t, 0)),
            pl.BlockSpec((rows, 128), lambda t, h: (t, 0)),
        ],
        out_specs=[
            pl.BlockSpec((rows, HEAD), lambda t, h: (t, h)),
            pl.BlockSpec((rows, 128), lambda t, h: (t, 0)),
        ],
        out_shape=[
            jax.ShapeDtypeStruct((2 * rows, columns), bf16),
            jax.ShapeDtypeStruct((2 * rows, 128), f32),
        ],
        compiler_params=pltpu.CompilerParams(vmem_limit_bytes=limit_of(2 * rows)),
        cost_estimate=pl.CostEstimate(
            flops=8 * rows * length * columns,
            bytes_accessed=4 * (rows * length + 2 * length * columns),
            transcendentals=2 * rows * length * heads,
        ),
        name="attend",
    )(queries, shared, shared, bias, info)


def attend_back_body(
    tiles, keys_per_tile, q_ref, k_ref, v_ref, bias_ref, total_ref, grad_ref, dq_ref, both_ref, dk_sum, dv_sum
):
    rows = q_ref.shape[0] // tiles
    lanes = lax.broadcasted_iota(jnp.int32, (rows, 128), 1)
    dk_sum[...] = jnp.zeros_like(dk_sum)
    dv_sum[...] = jnp.zeros_like(dv_sum)
    for tile in range(tiles):
        here = pl.ds(tile * rows, rows)
        keys = (tile + 1) * keys_per_tile
        query, grad = q_ref[here, :], grad_ref[here, :]
        scores = product_last(query, k_ref[:keys, :]) * scale
        scores = scores + bias_ref[here, :keys].astype(f32)
        total = jnp.where(lanes == pl.program_id(1), total_ref[here, :], 0.0)
        probs = jnp.exp(scores - jnp.sum(total, axis=1, keepdims=True))
        prob_grad = product_last(grad, v_ref[:keys, :])
        inner = jnp.sum(probs * prob_grad, axis=1, keepdims=True)
        score_grad = (probs * (prob_grad - inner) * scale).astype(bf16)
        dq_ref[here, :] = product(score_grad, k_ref[:keys, :]).astype(bf16)
        dk_sum[:keys, :] += product_first(score_grad, query)
        dv_sum[:keys, :] += product_first(probs.astype(bf16), grad)
    both_ref[0, 0] = dk_sum[...].astype(bf16)
    both_ref[1, 0] = dv_sum[...].astype(bf16)


def attend_back(queries, shared, bias, total, grads, tiles):
    rows, columns = queries.shape[0] // 2, queries.shape[1]
    length = shared.shape[0] // 2
    heads = columns // HEAD
    row_spec = pl.BlockSpec((rows, HEAD), lambda t, h: (t, h))
    return pl.pallas_call(
        functools.partial(attend_back_body, tiles, length // tiles),
        grid=(2, heads),
        in_specs=[
            row_spec,
            pl.BlockSpec((length, HEAD), lambda t, h: (t, 2 * h)),
            pl.BlockSpec((length, HEAD), lambda t, h: (t, 2 * h + 1)),
            pl.BlockSpec((rows, length), lambda t, h: (t, 0)),
            pl.BlockSpec((rows, 128), lambda t, h: (t, 0)),
            row_spec,
        ],
        out_specs=[row_spec, pl.BlockSpec((2, 1, length, HEAD), lambda t, h: (h, t, 0, 0))],
        out_shape=[
            jax.ShapeDtypeStruct((2 * rows, columns), bf16),
            jax.ShapeDtypeStruct((2 * heads, 2, length, HEAD), bf16),
        ],
        scratch_shapes=[pltpu.VMEM((length, HEAD), f32), pltpu.VMEM((length, HEAD), f32)],
        compiler_params=pltpu.CompilerParams(vmem_limit_bytes=60 * 2**20),
        cost_estimate=pl.CostEstimate(
            flops=20 * rows * length * columns,
            bytes_accessed=4 * (rows * length + 4 * length * columns),
            transcendentals=2 * rows * length * heads,
        ),
        name="attend_back",
    )(queries, shared, shared, bias, total, grads)


def chunk_of(rows):
    return 640 if rows % 640 == 0 else rows


def assemble(shard, pieces, out_ref, sems):
    rows, half = pieces[0].shape
    copies = []
    for i, piece in enumerate(pieces):
        at = pl.multiple_of((shard if i % 2 == 0 else 1 - shard) * half, 128)
        place = out_ref.at[pl.ds(i // 2 * rows, rows), pl.ds(at, half)]
        copies.append(pltpu.make_async_copy(piece, place, sems.at[i]))
    for copy in copies:
        copy.start()
    for copy in copies:
        copy.wait()


def plain_in_body(shard_ref, p0, p1, p2, p3, w_ref, x_ref, y_ref, sems):
    @pl.when(pl.program_id(0) == 0)
    def _():
        assemble(shard_ref[0], (p0, p1, p2, p3), x_ref, sems)

    chunk = chunk_of(x_ref.shape[0])

    @pl.loop(0, x_ref.shape[0] // chunk)
    def _(i):
        here = pl.ds(pl.multiple_of(i * chunk, 16), chunk)
        y_ref[here, :] = product(x_ref[here, :], w_ref[...]).astype(bf16)


def plain_in(shard, pieces, weight, tile=512):
    rows, half = pieces[0].shape
    columns = weight.shape[1]
    return pl.pallas_call(
        plain_in_body,
        grid_spec=pltpu.PrefetchScalarGridSpec(
            num_scalar_prefetch=1,
            grid=(pl.cdiv(columns, tile),),
            in_specs=[pl.BlockSpec(memory_space=pl.ANY)] * 4
            + [pl.BlockSpec((2 * half, tile), lambda j, s: (0, j))],
            out_specs=[
                pl.BlockSpec((2 * rows, 2 * half), lambda j, s: (0, 0)),
                pl.BlockSpec((2 * rows, tile), lambda j, s: (0, j)),
            ],
            scratch_shapes=[pltpu.SemaphoreType.DMA((4,))],
        ),
        out_shape=[
            jax.ShapeDtypeStruct((2 * rows, 2 * half), bf16),
            jax.ShapeDtypeStruct((2 * rows, columns), bf16),
        ],
        compiler_params=pltpu.CompilerParams(vmem_limit_bytes=limit_of(2 * rows)),
        cost_estimate=pl.CostEstimate(
            flops=8 * rows * half * columns,
            bytes_accessed=16 * rows * half + 4 * half * columns + 8 * rows * columns,
            transcendentals=0,
        ),
        name="plain_in",
    )(shard, *pieces, weight)


def expert_begin_body(shard_ref, p0, p2, gw_ref, uw_ref, gate_ref, up_ref, x_ref, sems):
    rows = p0.shape[0]

    @pl.when(pl.program_id(0) == 0)
    def _():
        copies = [
            pltpu.make_async_copy(p, x_ref.at[pl.ds(i * rows, rows), :], sems.at[i])
            for i, p in enumerate((p0, p2))
        ]
        for copy in copies:
            copy.start()
        for copy in copies:
            copy.wait()

    chunk = chunk_of(x_ref.shape[0])

    @pl.loop(0, x_ref.shape[0] // chunk)
    def _(i):
        here = pl.ds(pl.multiple_of(i * chunk, 16), chunk)
        gate_ref[here, :] = product(x_ref[here, :], gw_ref[...]).astype(bf16)
        up_ref[here, :] = product(x_ref[here, :], uw_ref[...]).astype(bf16)


def expert_begin(shard, own, other, gate_weight, up_weight, tile=512):
    rows, half = own.shape
    columns = gate_weight.shape[1]
    weight_spec = pl.BlockSpec((half, tile), lambda j, s: (s[0], j))
    tile_spec = pl.BlockSpec((2 * rows, tile), lambda j, s: (0, j))
    return pl.pallas_call(
        expert_begin_body,
        grid_spec=pltpu.PrefetchScalarGridSpec(
            num_scalar_prefetch=1,
            grid=(pl.cdiv(columns, tile),),
            in_specs=[pl.BlockSpec(memory_space=pl.ANY)] * 2 + [weight_spec, weight_spec],
            out_specs=[tile_spec, tile_spec],
            scratch_shapes=[
                pltpu.VMEM((2 * rows, half), bf16),
                pltpu.SemaphoreType.DMA((2,)),
            ],
        ),
        out_shape=[jax.ShapeDtypeStruct((2 * rows, columns), bf16)] * 2,
        compiler_params=pltpu.CompilerParams(vmem_limit_bytes=60 * 2**20),
        cost_estimate=pl.CostEstimate(
            flops=8 * rows * half * columns,
            bytes_accessed=8 * rows * half + 4 * half * columns + 16 * rows * columns,
            transcendentals=0,
        ),
        name="expert_begin",
    )(shard, own, other, gate_weight, up_weight)


def expert_in_body(
    columns, tiles, shard_ref, p0, p1, p2, p3, router_ref, info_ref, plain_ref, gp_ref, up_ref, gw_ref, uw_ref,
    g_ref, u_ref, r_ref, x_ref, gate_ref, total_ref, hidden_ref, dgate_ref, dup_ref, own_ref, other_ref,
    their_ref, dgate_all, dup_all, coef_ref, sems,
):
    tile = gw_ref.shape[1]
    rows = p0.shape[0]
    step = pl.program_id(0)
    difference = info_ref[:, MLP : MLP + router_ref.shape[1]]

    @pl.when(step == 0)
    def _():
        copies = [
            pltpu.make_async_copy(p, their_ref.at[pl.ds(i * rows, rows), :], sems.at[4 + i])
            for i, p in enumerate((p1, p3))
        ]
        for copy in copies:
            copy.start()
        assemble(shard_ref[0], (p0, p1, p2, p3), x_ref, sems)
        for copy in copies:
            copy.wait()
        logits = product(x_ref[...], router_ref[...])
        gate = jax.nn.sigmoid(jnp.sum(logits * difference, axis=1, keepdims=True))
        gate_ref[...] = jnp.broadcast_to(gate, gate_ref.shape)
        total_ref[...] = jnp.zeros_like(total_ref)

    chunk = chunk_of(x_ref.shape[0])
    at = pl.ds(pl.multiple_of(jnp.minimum(step, tiles - 1) * tile, 128), tile)

    def first_part(i):
        here = pl.ds(pl.multiple_of(i * chunk, 16), chunk)
        their = their_ref[here, :]
        gate_pre = gp_ref[here, :].astype(f32) + product(their, gw_ref[...])
        up_pre = up_ref[here, :].astype(f32) + product(their, uw_ref[...])
        plain, gate = plain_ref[here, :].astype(f32), gate_ref[here, :1]
        inside = lax.broadcasted_iota(jnp.int32, (1, tile), 1) + step * tile < columns
        sigmoid = jax.nn.sigmoid(gate_pre)
        silu = gate_pre * sigmoid
        hidden = (silu * up_pre).astype(bf16).astype(f32)
        gated = (gate * hidden).astype(bf16)
        hidden_ref[here, :] = gated
        total_ref[here, :] += jnp.sum(
            jnp.where(inside, gated.astype(f32) * plain, 0.0), axis=1, keepdims=True
        )
        hidden_grad = gate * plain
        up_grad = hidden_grad * silu
        dup_ref[here, :] = up_grad.astype(bf16)
        dup_all[here, at] = up_grad.astype(bf16)
        gate_grad = hidden_grad * up_pre * (sigmoid + silu * (1.0 - sigmoid))
        dgate_ref[here, :] = gate_grad.astype(bf16)
        dgate_all[here, at] = gate_grad.astype(bf16)

    @pl.when(step < tiles)
    def _():
        pl.loop(0, x_ref.shape[0] // chunk)(first_part)

    @pl.when(step == tiles)
    def _():
        coef_ref[...] = (1.0 - gate_ref[:, :1]) * total_ref[:, :1] * difference

    @pl.when(step >= tiles)
    def _():
        for t, out_ref in enumerate((own_ref, other_ref)):
            here = pl.ds(t * rows, rows)
            value = product_last(dgate_all[here, :columns], g_ref[...])
            value = value + product_last(dup_all[here, :columns], u_ref[...])
            value = value + product_last(coef_ref[here, :].astype(bf16), r_ref[...])
            out_ref[...] = value.astype(bf16)


def expert_in(shard, pieces, router, info, plain, begun, gate_weight, up_weight, tile=512, row_tile=256):
    rows, half = pieces[0].shape
    columns = gate_weight.shape[1]
    tile = min(tile, columns)
    tiles, steps = pl.cdiv(columns, tile), half // row_tile
    weight_spec = pl.BlockSpec((half, tile), lambda j, s: (1 - s[0], jnp.minimum(j, tiles - 1)))
    tile_spec = pl.BlockSpec((2 * rows, tile), lambda j, s: (0, jnp.minimum(j, tiles - 1)))
    out_spec = pl.BlockSpec((rows, row_tile), lambda j, s: (0, jnp.maximum(j - tiles, 0)))

    def row_spec(columns):
        return pl.BlockSpec(
            (row_tile, columns), lambda j, s: (steps * (1 - s[0]) + jnp.maximum(j - tiles, 0), 0)
        )

    held_spec = pl.BlockSpec((2 * rows, 128), lambda j, s: (0, 0))
    hidden_shape = jax.ShapeDtypeStruct((2 * rows, columns), bf16)
    return pl.pallas_call(
        functools.partial(expert_in_body, columns, tiles),
        grid_spec=pltpu.PrefetchScalarGridSpec(
            num_scalar_prefetch=1,
            grid=(tiles + steps,),
            in_specs=[pl.BlockSpec(memory_space=pl.ANY)] * 4
            + [
                pl.BlockSpec(router.shape, lambda j, s: (0, 0)),
                pl.BlockSpec(info.shape, lambda j, s: (0, 0)),
                tile_spec,
                tile_spec,
                tile_spec,
                weight_spec,
                weight_spec,
                row_spec(columns),
                row_spec(columns),
                row_spec(router.shape[1]),
            ],
            out_specs=[
                pl.BlockSpec((2 * rows, 2 * half), lambda j, s: (0, 0)),
                held_spec,
                held_spec,
                tile_spec,
                tile_spec,
                tile_spec,
                out_spec,
                out_spec,
            ],
            scratch_shapes=[
                pltpu.VMEM((2 * rows, half), bf16),
                pltpu.VMEM((2 * rows, tiles * tile), bf16),
                pltpu.VMEM((2 * rows, tiles * tile), bf16),
                pltpu.VMEM((2 * rows, router.shape[1]), f32),
                pltpu.SemaphoreType.DMA((6,)),
            ],
        ),
        out_shape=[
            jax.ShapeDtypeStruct((2 * rows, 2 * half), bf16),
            jax.ShapeDtypeStruct((2 * rows, 128), f32),
            jax.ShapeDtypeStruct((2 * rows, 128), f32),
            hidden_shape,
            hidden_shape,
            hidden_shape,
            jax.ShapeDtypeStruct((rows, half), bf16),
            jax.ShapeDtypeStruct((rows, half), bf16),
        ],
        compiler_params=pltpu.CompilerParams(vmem_limit_bytes=grant(50, 2 * rows)),
        cost_estimate=pl.CostEstimate(
            flops=16 * rows * half * columns,
            bytes_accessed=16 * rows * half + 4 * half * columns + 36 * rows * columns,
            transcendentals=2 * rows * columns,
        ),
        name="expert_in",
    )(shard, *pieces, router, info, plain, *begun, gate_weight, up_weight, gate_weight, up_weight, router)


def attended_in_body(
    shard_ref, p0, p1, p2, p3, info_ref, mixed_ref, w_ref, x_ref, total_ref, y_ref, sems
):
    @pl.when(pl.program_id(0) == 0)
    def _():
        assemble(shard_ref[0], (p0, p1, p2, p3), x_ref, sems)
        total_ref[...] = jnp.zeros_like(total_ref)

    chunk = chunk_of(x_ref.shape[0])

    @pl.loop(0, x_ref.shape[0] // chunk)
    def _(i):
        here = pl.ds(pl.multiple_of(i * chunk, 16), chunk)
        plain = product(x_ref[here, :], w_ref[...])
        total_ref[here, :] += jnp.sum(mixed_ref[here, :].astype(f32) * plain, axis=1, keepdims=True)
        y_ref[here, :] = (info_ref[here, GATE : GATE + 1] * plain).astype(bf16)


def attended_in(shard, pieces, info, mixed, weight):
    rows, half = pieces[0].shape
    columns = weight.shape[1]
    tile = min(256, columns)
    return pl.pallas_call(
        attended_in_body,
        grid_spec=pltpu.PrefetchScalarGridSpec(
            num_scalar_prefetch=1,
            grid=(columns // tile,),
            in_specs=[pl.BlockSpec(memory_space=pl.ANY)] * 4
            + [
                pl.BlockSpec((2 * rows, 128), lambda j, s: (0, 0)),
                pl.BlockSpec((2 * rows, tile), lambda j, s: (0, j)),
                pl.BlockSpec((2 * half, tile), lambda j, s: (0, j)),
            ],
            out_specs=[
                pl.BlockSpec((2 * rows, 2 * half), lambda j, s: (0, 0)),
                pl.BlockSpec((2 * rows, 128), lambda j, s: (0, 0)),
                pl.BlockSpec((2 * rows, tile), lambda j, s: (0, j)),
            ],
            scratch_shapes=[pltpu.SemaphoreType.DMA((4,))],
        ),
        out_shape=[
            jax.ShapeDtypeStruct((2 * rows, 2 * half), bf16),
            jax.ShapeDtypeStruct((2 * rows, 128), f32),
            jax.ShapeDtypeStruct((2 * rows, columns), bf16),
        ],
        compiler_params=pltpu.CompilerParams(vmem_limit_bytes=limit_of(2 * rows)),
        cost_estimate=pl.CostEstimate(
            flops=8 * rows * half * columns,
            bytes_accessed=16 * rows * half + 4 * half * columns + 8 * rows * columns,
            transcendentals=0,
        ),
        name="attended_in",
    )(shard, *pieces, info, mixed, weight)


def rows_half_body(count, extra, gate_at, diff_at, shard_ref, *refs):
    lefts, weights = refs[:count], refs[count : 2 * count]
    rest = refs[2 * count :]
    if extra:
        total_ref, gate_ref, diff_ref, router_ref = rest[:4]
        rest = rest[4:]
        coef_ref = rest[2]

        @pl.when(pl.program_id(0) == 0)
        def _():
            gate = gate_ref[:, gate_at : gate_at + 1]
            difference = diff_ref[:, diff_at : diff_at + router_ref.shape[1]]
            coef_ref[...] = (1.0 - gate) * total_ref[:, :1] * difference

    rows = rest[0].shape[0]
    chunk = chunk_of(rows)
    for t in range(2):

        @pl.loop(0, rows // chunk)
        def _(i):
            here = pl.ds(pl.multiple_of(t * rows + i * chunk, 16), chunk)
            there = pl.ds(pl.multiple_of(i * chunk, 16), chunk)
            value = sum(product_last(a[here, :], w[...]) for a, w in zip(lefts, weights))
            if extra:
                value = value + product_last(coef_ref[here, :].astype(bf16), router_ref[...])
            rest[t][there, :] = value.astype(bf16)


def rows_half(shard, mine, lefts, weights, extra=None, tile=512):
    rows, width = lefts[0].shape[0] // 2, weights[0].shape[0]
    half = width // 2
    steps = half // tile

    def at(j, s):
        return j + steps * (s[0] if mine else 1 - s[0])

    def whole_spec(array):
        return pl.BlockSpec(array.shape, lambda j, s: (0, 0))

    in_specs = [whole_spec(a) for a in lefts]
    in_specs += [pl.BlockSpec((tile, w.shape[1]), lambda j, s: (at(j, s), 0)) for w in weights]
    operands = list(lefts) + list(weights)
    out_specs = [pl.BlockSpec((rows, tile), lambda j, s: (0, j))] * 2
    out_shape = [jax.ShapeDtypeStruct((rows, half), bf16)] * 2
    gate_at = diff_at = 0
    if extra:
        total, gate, gate_at, difference, diff_at, router = extra
        in_specs += [whole_spec(total), whole_spec(gate), whole_spec(difference)]
        in_specs += [pl.BlockSpec((tile, router.shape[1]), lambda j, s: (at(j, s), 0))]
        operands += [total, gate, difference, router]
        coefs = jax.ShapeDtypeStruct((2 * rows, router.shape[1]), f32)
        out_specs.append(whole_spec(coefs))
        out_shape.append(coefs)
    depth = sum(w.shape[1] for w in weights)
    return pl.pallas_call(
        functools.partial(rows_half_body, len(lefts), extra is not None, gate_at, diff_at),
        grid_spec=pltpu.PrefetchScalarGridSpec(
            num_scalar_prefetch=1, grid=(steps,), in_specs=in_specs, out_specs=out_specs
        ),
        out_shape=out_shape,
        compiler_params=pltpu.CompilerParams(vmem_limit_bytes=grant(40, 2 * rows)),
        cost_estimate=pl.CostEstimate(
            flops=4 * rows * half * depth,
            bytes_accessed=4 * rows * depth + 2 * half * depth + 4 * rows * half,
            transcendentals=0,
        ),
        name="rows_mine" if mine else "rows_theirs",
    )(shard, *operands)


def prepare_body(
    capacity, scalars, tokens_ref, gain_ref, order_ref, attn_ref, mlp_ref, segment_ref, parent_ref,
    block_ref, attn_pack_ref, mlp_pack_ref, tile_ref,
):
    width = tokens_ref.shape[2]
    count = tokens_ref.shape[1]
    values = tokens_ref[0].astype(f32)
    scales = lax.rsqrt(jnp.mean(values * values, axis=1, keepdims=True) + epsilon)
    block_ref[:, :width] = (values * scales * gain_ref[...]).astype(bf16)

    ranks = order_ref[0].astype(f32)
    pairs = lax.broadcasted_iota(jnp.int32, (2 * count, count), 0)
    owners = lax.broadcasted_iota(jnp.int32, (2 * count, count), 1)
    turns = [(pairs == 2 * owners + k).astype(f32) for k in range(2)]
    rank_rows = [product(ranks, turn) for turn in turns]
    rank_columns = [
        lax.dot_general(turn, ranks, (((0,), (1,)), ((), ())), preferred_element_type=f32)
        for turn in turns
    ]
    same = (
        lax.broadcasted_iota(jnp.int32, (count, count), 0)
        == lax.broadcasted_iota(jnp.int32, (count, count), 1)
    ).astype(f32)
    places = lax.broadcasted_iota(jnp.int32, attn_pack_ref.shape, 0).astype(f32)
    tile_ref[...] = jnp.zeros_like(tile_ref)
    for at, (route_ref, pack_ref) in enumerate(((attn_ref, attn_pack_ref), (mlp_ref, mlp_pack_ref))):
        rows = route_ref[...].astype(f32)
        routes = product_last(same, rows)
        hit = None
        for k in range(2):
            route = rows[k : k + 1]
            slot = jnp.zeros((1, count), f32)
            for other in range(2):
                earlier = (routes[:, other : other + 1] == route) & (
                    rank_columns[other] < rank_rows[k]
                )
                slot = slot + jnp.sum(earlier.astype(f32), axis=0, keepdims=True)
            slot = jnp.minimum(slot, float(capacity))
            tile_ref[4 * at + 2 * k : 4 * at + 2 * k + 1, :] = route
            tile_ref[4 * at + 2 * k + 1 : 4 * at + 2 * k + 2, :] = slot
            code = jnp.where(slot < capacity, route * capacity + slot, -1.0)
            here = places == code
            hit = here if hit is None else hit | here
        pack_ref[...] = hit.astype(bf16)
    tile_ref[8:9, :] = segment_ref[...].astype(f32)
    tile_ref[9:10, : parent_ref.shape[1]] = parent_ref[...].astype(f32)
    block_ref[:, width:] = jnp.zeros((count, block_ref.shape[1] - width), bf16)
    block_ref[:16, width : width + count] = tile_ref[...].astype(bf16)


def prepare(place, tokens, gain, order, attn_routes, mlp_routes, segments, parents, experts, capacity):
    _, count, width = tokens.shape

    def whole_spec(array):
        return pl.BlockSpec(array.shape, lambda i, s: (0,) * array.ndim)

    pack = jax.ShapeDtypeStruct((experts * capacity, count), bf16)
    return pl.pallas_call(
        functools.partial(prepare_body, capacity),
        grid_spec=pltpu.PrefetchScalarGridSpec(
            num_scalar_prefetch=1,
            grid=(1,),
            in_specs=[whole_spec(a) for a in (tokens, gain, order, attn_routes, mlp_routes)]
            + [pl.BlockSpec((1, count), lambda i, s: (0, s[0])), whole_spec(parents)],
            out_specs=[
                pl.BlockSpec((count, width + 128), lambda i, s: (0, 0)),
                pl.BlockSpec(pack.shape, lambda i, s: (0, 0)),
                pl.BlockSpec(pack.shape, lambda i, s: (0, 0)),
            ],
            scratch_shapes=[pltpu.VMEM((16, count), f32)],
        ),
        out_shape=[jax.ShapeDtypeStruct((count, width + 128), bf16), pack, pack],
        compiler_params=pltpu.CompilerParams(vmem_limit_bytes=24 * 2**20),
        name="prepare",
    )(place, tokens, gain, order, attn_routes, mlp_routes, segments, parents)


def difference_of(expert, other, experts):
    range_of = lax.broadcasted_iota(jnp.int32, (other.shape[0], experts), 1).astype(f32)
    return (range_of == expert).astype(f32) - (range_of == other).astype(f32)


def front_body(
    capacity, steps, scalars, own_ref, other_ref, own_marks_ref, other_marks_ref, router_ref,
    key_hbm, value_hbm, got_key_hbm, got_value_hbm, shared_ref, picked_ref, bias_ref, info_ref, weight, sems,
):
    piece = weight.shape[1] // 2
    heads = piece // HEAD

    turn = pl.program_id(0)

    def fetch(sources, at):
        for h in range(heads):
            for i, source in enumerate(sources):
                from_here = source.at[:, pl.ds(pl.multiple_of(at + h * HEAD, HEAD), HEAD)]
                place = weight.at[:, pl.ds((2 * h + i) * HEAD, HEAD)]
                pltpu.make_async_copy(from_here, place, sems.at[h]).start()

    @pl.when((turn == 0) & (scalars[0] == 1))
    def _():
        fetch((key_hbm, value_hbm), scalars[1] * piece)

    @pl.when((turn == 0) & (scalars[0] == 0))
    def _():
        fetch((got_key_hbm, got_value_hbm), 0)

    def one_step(step, rows_ref, marks_ref):
        front_step(
            capacity, heads, turn, step, scalars, rows_ref, marks_ref, router_ref,
            shared_ref, picked_ref, bias_ref, info_ref, weight, sems,
        )

    @pl.when(turn < steps)
    def _():
        one_step(turn, own_ref, own_marks_ref)

    @pl.when(turn >= steps)
    def _():
        one_step(turn - steps, other_ref, other_marks_ref)


def front_step(
    capacity, heads, turn, step, scalars, rows_ref, marks_ref, router_ref,
    shared_ref, picked_ref, bias_ref, info_ref, weight, sems,
):
    count = rows_ref.shape[1]
    width = weight.shape[0]
    blocks = marks_ref.shape[0]
    rows = jnp.concatenate([rows_ref[0, :, :width], rows_ref[1, :, :width]])
    expert = scalars[2].astype(f32)
    index = lax.broadcasted_iota(jnp.int32, (2 * capacity, count), 0)
    lanes = lax.broadcasted_iota(jnp.int32, (2 * capacity, count), 1).astype(f32)
    first = index < capacity
    slots = jnp.where(first, index, index - capacity).astype(f32)
    upper = marks_ref[2 * step].astype(f32)
    lower = marks_ref[2 * step + 1].astype(f32)

    def mark(i):
        return jnp.where(first, upper[i : i + 1, :count], lower[i : i + 1, :count])

    def total(values):
        return jnp.sum(values, axis=1, keepdims=True)

    def hits_of(at):
        hits = [(mark(at + 2 * k) == expert) & (mark(at + 2 * k + 1) == slots) for k in range(2)]
        other = total(jnp.where(hits[0], mark(at + 2), 0.0) + jnp.where(hits[1], mark(at), 0.0))
        return hits[0] | hits[1], other

    experts = router_ref.shape[1]
    info_ref[:, MLP : MLP + experts] = difference_of(expert, hits_of(4)[1], experts)
    hit, other = hits_of(0)
    difference = difference_of(expert, other, experts)
    info_ref[:, ATTN : ATTN + experts] = difference

    own = total(jnp.where(hit, mark(8), 0.0))
    parents = mark(9)
    one = total(jnp.where(lanes == own, parents, 0.0))
    two = total(jnp.where(lanes == one, parents, 0.0))
    start = jnp.where(first[:, :1], 2 * step * count, (2 * step + 1) * count).astype(f32)
    place = total(jnp.where(hit, lanes, 0.0)) + start
    for j in range(blocks):
        keys = marks_ref[j, 8:9, :count].astype(f32)
        seen = ((keys == own) | (keys == one) | (keys == two)) & (lanes + float(j * count) <= place)
        bias_ref[:, j * count : (j + 1) * count] = jnp.where(seen, 0.0, negative).astype(bf16)

    both = jnp.concatenate([(hit & first).astype(bf16), (hit & ~first).astype(bf16)], axis=1)
    picked = product(both, rows).astype(bf16)
    picked_ref[...] = picked
    logits = product(picked, router_ref[...])
    info_ref[:, GATE : GATE + 1] = jax.nn.sigmoid(total(logits * difference))

    @pl.when(turn == 0)
    def _():
        for h in range(heads):
            here = pl.ds(2 * h * HEAD, 2 * HEAD)
            pltpu.make_async_copy(weight.at[:, here], weight.at[:, here], sems.at[h]).wait()
            shared_ref[:, here] = product(rows, weight[:, here]).astype(bf16)

    @pl.when(turn > 0)
    def _():
        shared_ref[...] = product(rows, weight[...]).astype(bf16)


def front(scalars, own, other, router, key_weight, value_weight, got_key, got_value, capacity):
    blocks, count, columns = own.shape
    width, piece = got_key.shape
    length = blocks * count
    rows = blocks * capacity
    steps = blocks // 2
    pinned_spec = pl.BlockSpec(memory_space=pltpu.HBM)
    marks_spec = pl.BlockSpec((blocks, 16, 128), lambda i, s: (0, 0, width // 128))

    def out_spec(height, columns):
        return pl.BlockSpec((height, columns), lambda i, s: (i, 0))

    pair = 2 * capacity
    return pl.pallas_call(
        functools.partial(front_body, capacity, steps),
        grid_spec=pltpu.PrefetchScalarGridSpec(
            num_scalar_prefetch=1,
            grid=(2 * steps,),
            in_specs=[
                pl.BlockSpec((2, count, columns), lambda i, s: (jnp.minimum(i, steps - 1), 0, 0)),
                pl.BlockSpec((2, count, columns), lambda i, s: (jnp.maximum(i - steps, 0), 0, 0)),
                marks_spec,
                marks_spec,
                pl.BlockSpec(router.shape, lambda i, s: (0, 0)),
            ]
            + [pinned_spec] * 4,
            out_specs=[
                out_spec(2 * count, 2 * piece),
                out_spec(pair, width),
                out_spec(pair, length),
                out_spec(pair, 128),
            ],
            scratch_shapes=[
                pltpu.VMEM((width, 2 * piece), bf16),
                pltpu.SemaphoreType.DMA((piece // HEAD,)),
            ],
        ),
        out_shape=[
            jax.ShapeDtypeStruct((2 * length, 2 * piece), bf16),
            jax.ShapeDtypeStruct((2 * rows, width), bf16),
            jax.ShapeDtypeStruct((2 * rows, length), bf16),
            jax.ShapeDtypeStruct((2 * rows, 128), f32),
        ],
        compiler_params=pltpu.CompilerParams(vmem_limit_bytes=grant(52, 2 * rows)),
        cost_estimate=pl.CostEstimate(
            flops=8 * length * width * piece,
            bytes_accessed=4 * length * width + 4 * width * piece,
            transcendentals=0,
        ),
        name="front",
    )(scalars, own, other, own, other, router, key_weight, value_weight, got_key, got_value)


def shared_out_body(steps, scalars, sums_ref, key_ref, value_ref, got_key_ref, got_value_ref, *outs):
    step = pl.program_id(0)
    sums = sums_ref[...]
    heads = sums.shape[0] // 2

    def part(t, i):
        return jnp.concatenate([sums[2 * h + i, t] for h in range(heads)], axis=1)

    def fill(pair, keys, values):
        for t in range(2):
            value = product_last(part(t, 0), keys[...]) + product_last(part(t, 1), values[...])
            pair[t][...] = value.astype(bf16)

    for side in range(2):
        for local in range(2):
            first = step < steps // 2 if side == 0 else step >= steps // 2

            @pl.when(first & (scalars[1] == local))
            def _():
                pair = (outs[side], outs[2 + side])
                if local:
                    fill(pair, key_ref, value_ref)
                else:
                    fill(pair, got_key_ref, got_value_ref)


def shared_out(scalars, sums, key_weight, value_weight, got_key, got_value, tile=512):
    rows = sums.shape[2]
    width, piece = got_key.shape
    half, steps = width // 2, width // tile

    def at(j, s):
        return lax.rem(j + steps // 2 * (1 - s[0]), steps)

    local = pl.BlockSpec((tile, piece), lambda j, s: (at(j, s), s[2]))
    sent = pl.BlockSpec((tile, piece), lambda j, s: (at(j, s), 0))
    theirs = pl.BlockSpec((rows, tile), lambda j, s: (0, jnp.minimum(j, steps // 2 - 1)))
    mine = pl.BlockSpec((rows, tile), lambda j, s: (0, jnp.maximum(j - steps // 2, 0)))
    return pl.pallas_call(
        functools.partial(shared_out_body, steps),
        grid_spec=pltpu.PrefetchScalarGridSpec(
            num_scalar_prefetch=1,
            grid=(steps,),
            in_specs=[pl.BlockSpec(sums.shape, lambda j, s: (0, 0, 0, 0)), local, local, sent, sent],
            out_specs=[theirs, mine, theirs, mine],
        ),
        out_shape=[jax.ShapeDtypeStruct((rows, half), bf16)] * 4,
        compiler_params=pltpu.CompilerParams(vmem_limit_bytes=60 * 2**20),
        cost_estimate=pl.CostEstimate(
            flops=8 * rows * width * piece,
            bytes_accessed=8 * width * piece + 8 * rows * width,
            transcendentals=0,
        ),
        name="shared_out",
    )(scalars, sums, key_weight, value_weight, got_key, got_value)


def per_device(
    tokens,
    cotangent,
    attn_gain,
    mlp_gain,
    key_weight,
    value_weight,
    query_weight,
    output_weight,
    attn_router,
    gate_weight,
    up_weight,
    down_weight,
    mlp_router,
    segment_ids,
    parent_ids,
    attn_routes,
    mlp_routes,
    slot_order,
):
    count, width = tokens.shape[1:]
    half = width // 2
    piece = query_weight.shape[1]
    experts = attn_router.shape[1]
    blocks = lax.axis_size("dp")
    members = blocks // experts
    capacity = min(count, 5 * count * attn_routes.shape[2] // (4 * experts))
    length, parents = segment_ids.shape[1], parent_ids.shape[1]
    tiles = max(2, length // 512)
    dp, core, shard = lax.axis_index("dp"), lax.axis_index("expert"), lax.axis_index("shard")
    expert, member = dp // members, dp % members

    def my_half(values):
        return lax.dynamic_slice_in_dim(values, shard * half, half, values.ndim - 1)

    def whole(mine):
        got = swap(mine, "shard")
        first = shard == 0
        return jnp.concatenate(
            [jnp.where(first, mine, got), jnp.where(first, got, mine)], axis=mine.ndim - 1
        )

    block, attn_pack, mlp_pack = prepare(
        jnp.reshape(dp, (1,)).astype(jnp.int32),
        tokens,
        attn_gain[None],
        slot_order,
        attn_routes[0].T,
        mlp_routes[0].T,
        segment_ids,
        parent_ids,
        experts,
        capacity,
    )
    heads_at = (member * 2 + core) * 2 + shard
    holder = (member * 2 + core) // members
    offset = holder * 2 * members
    names = ("dp", "expert", "shard")
    sends = []
    for d in range(blocks):
        for c in range(2):
            at = (d * 2 + c) * 2
            source = ((d % members) * 2 + c) // members
            sends.append((at + source, at + 1 - source))
    partner_at = (member * 2 + core) * 2 + 1 - shard

    def partner_columns(weight):
        columns = lax.dynamic_slice_in_dim(weight, (partner_at - offset) * piece, piece, 1)
        return lax.ppermute(columns, names, sends)

    grad_half = lax.dynamic_slice_in_dim(cotangent[0], shard * half, half, 1)

    def pack_rows(values, pack):
        packed = product(pack, values).astype(bf16).reshape(experts, 1, capacity, half)
        packed = jnp.broadcast_to(packed, (experts, members, capacity, half))
        return packed.reshape(blocks, capacity, half)

    works = [None] * (blocks // 2)
    works[-1] = lambda event: [pack_rows(after(grad_half, event), mlp_pack)]
    own_blocks, made = ring_gather(block, "dp", blocks, 1, works)
    grad_packed = made[-1][0]
    got_key, got_value = partner_columns(key_weight), partner_columns(value_weight)
    own_blocks, got_key, got_value = lax.optimization_barrier((own_blocks, got_key, got_value))
    tree_blocks = [own_blocks, swap(own_blocks, "expert")]

    local = (shard == holder).astype(jnp.int32)
    local_at = local * (heads_at - offset)
    shard_index = jnp.reshape(shard, (1,)).astype(jnp.int32)

    def dispatch(packed, work=None, begin=None):
        arrived = lax.all_to_all(packed, "dp", 0, 0, tiled=True)
        done = []
        if work:
            arrived, *done = lax.optimization_barrier((arrived, *work(packed)))
        arrived = arrived.reshape(blocks * capacity, half)
        other = swap(arrived, "expert")
        got = swap(arrived, "shard")
        begun = []
        if begin:
            got, *begun = lax.optimization_barrier((got, *begin(arrived, other)))
        return [arrived, got, other, swap(got, "expert")], done, begun

    def join_ends(sides, work=None):
        own, other, *_ = sides(False, None)
        theirs = (own.astype(f32) + swap(other, "expert").astype(f32)).astype(bf16)
        back, own, other, *rest = lax.optimization_barrier(
            (swap(theirs, "shard"), *sides(True, theirs), *(work(theirs) if work else []))
        )
        total = own.astype(f32) + swap(other, "expert").astype(f32) + back.astype(f32)
        return total, rest

    def sum_tokens(back, pack):
        if members > 1:
            back = back.reshape(experts, members, capacity, half).astype(f32)
            back = jnp.sum(back, axis=1).astype(bf16)
        return product_first(pack, back.reshape(experts * capacity, half))

    def send_back(joined, work=None):
        back = lax.all_to_all(joined, "dp", 0, 0, tiled=True)
        done = []
        if work:
            back, *done = lax.optimization_barrier((back, *work(joined)))
        return back, done

    def for_tokens(joined):
        return joined.astype(bf16).reshape(blocks, capacity, half)

    grad_arrived = lax.all_to_all(grad_packed, "dp", 0, 0, tiled=True)
    grad_arrived = grad_arrived.reshape(blocks * capacity, half)
    scalars = jnp.stack([local, local_at, expert]).astype(jnp.int32)
    shared, rows, bias, info = front(
        scalars, *tree_blocks, attn_router, key_weight, value_weight, got_key, got_value, capacity
    )
    grad_got = swap(after(grad_arrived, rows), "shard")
    queries = product(rows, query_weight).astype(bf16)
    mixed, log_total = attend(queries, shared, bias, info, tiles)
    mixed, grad_got = lax.optimization_barrier((mixed, grad_got))
    grad_pieces = (grad_arrived, grad_got, swap(grad_arrived, "expert"), swap(grad_got, "expert"))

    def attn_sides(mine, event):
        return rows_half(shard_index, mine, [after(mixed, event)], [output_weight])

    def plain_work(event):
        return plain_in(shard_index, after(grad_pieces, event), down_weight)

    attn_joined, (grad_rows, plain_grad) = join_ends(attn_sides, plain_work)
    back = send_back(for_tokens(attn_joined))[0]
    inputs = tokens[0].astype(f32)
    attn_scale = lax.rsqrt(jnp.mean(inputs * inputs, axis=1, keepdims=True) + epsilon)
    middle = my_half(inputs) + sum_tokens(back, attn_pack)

    def feature_mean(values):
        part = jnp.sum(values, axis=1, keepdims=True)
        return (part + swap(part, "shard")) / width

    mlp_scale = lax.rsqrt(feature_mean(middle * middle) + epsilon)
    half_gain = my_half(mlp_gain)
    mlp_normed = (middle * mlp_scale * half_gain).astype(bf16)

    def begin(own, other):
        return expert_begin(shard_index, own, other, gate_weight, up_weight)

    mlp_pieces, _, begun = dispatch(pack_rows(mlp_normed, mlp_pack), None, begin)
    mlp_rows, mlp_gate, mlp_total, gated_hidden, gate_pre_grad, up_pre_grad, *theirs_rows = expert_in(
        shard_index, mlp_pieces, mlp_router, info, plain_grad, begun, gate_weight, up_weight
    )

    def mlp_sides(mine, event):
        if not mine:
            return theirs_rows
        return rows_half(
            shard_index,
            mine,
            after([gate_pre_grad, up_pre_grad], event),
            [gate_weight, up_weight],
            (mlp_total, mlp_gate, 0, info, MLP, mlp_router),
        )

    def term_half(mine, event):
        return rows_half(shard_index, mine, [after(gated_hidden, event)], [down_weight])

    row_joined, (mlp_coefs,) = join_ends(mlp_sides)
    row_joined = for_tokens(row_joined)

    def gate_work(event):
        own, other = term_half(False, event)
        theirs = own.astype(f32) + swap(other, "expert").astype(f32)
        return [theirs.astype(bf16), product_first(after(mlp_rows, own), gate_pre_grad)]

    back, (term_theirs, gate_grad) = send_back(row_joined, gate_work)
    mlp_normed_grad = sum_tokens(back, mlp_pack)

    mlp_n = middle * mlp_scale
    weighted = mlp_normed_grad * half_gain
    mlp_gain_part = jnp.sum(mlp_normed_grad * mlp_n, axis=0)
    middle_grad = grad_half.astype(f32) + mlp_scale * (
        weighted - mlp_n * feature_mean(weighted * mlp_n)
    )
    low_grad = middle_grad.astype(bf16)

    def up_work(event):
        up_grad = product_first(after(mlp_rows, event), up_pre_grad)
        router_part = product_first(mlp_coefs, after(mlp_rows, event).astype(f32))
        return [up_grad, router_part]

    def down_work(own, other):
        return [product_first(after(grad_rows, own), gated_hidden)]

    packed = pack_rows(low_grad, attn_pack)
    term_pieces, (up_grad, mlp_router_part), (down_grad,) = dispatch(packed, up_work, down_work)
    term_back = swap(after(term_theirs, packed), "shard")
    own, other = term_half(True, packed)
    total = own.astype(f32) + swap(other, "expert").astype(f32) + term_back.astype(f32)
    term_joined = after(for_tokens(total), term_pieces[0])
    term_back = lax.all_to_all(term_joined, "dp", 0, 0, tiled=True)
    term_rows, attn_total, attended_grad = attended_in(
        shard_index, term_pieces, info, mixed, output_weight
    )
    query_rows_grad, held = attend_back(queries, shared, bias, log_total, attended_grad, tiles)
    held, term_back = lax.optimization_barrier((held, term_back))
    part = length // experts
    cut = experts * HEAD // (2 * piece)

    def cut_parts(values):
        shape = values.shape
        values = values.reshape(shape[:-1] + (cut, shape[-1] // cut))
        return jnp.moveaxis(values, -2, 1).reshape((experts,) + shape[1:-1] + (-1,))

    def join_parts(values):
        shape = values.shape
        values = jnp.moveaxis(values.reshape((experts // cut, cut) + shape[1:]), 1, -2)
        return values.reshape(values.shape[:-2] + (-1,))

    rings = None
    if members > 1:
        rings = [[e * members + m for e in range(experts)] for m in range(members)]

    def to_experts(values):
        return lax.all_to_all(values, "dp", 0, 0, axis_index_groups=rings, tiled=True)

    held = cut_parts(held)
    def input_rows(mine, event):
        return rows_half(
            shard_index,
            mine,
            [after(query_rows_grad, event)],
            [query_weight],
            (attn_total, info, GATE, info, ATTN, attn_router),
        )

    kept = []

    def theirs_work(event):
        own, other, _ = input_rows(False, event)
        theirs = own.astype(f32) + swap(other, "expert").astype(f32)
        kept.append(theirs.astype(bf16))
        return kept[:]

    def mine_work(event):
        kept.append(swap(after(kept[0], event), "shard"))
        kept.extend(input_rows(True, event))
        return kept[2:] + [product_first(after(rows, event), query_rows_grad)]

    def output_work(event):
        return [kept[1], product_first(after(term_rows, event), mixed)]

    works = [theirs_work, mine_work, None, output_work]
    key_sums, made = ring_scatter(held, experts, members, works)
    key_sums = key_sums.astype(bf16)
    _, (own, other, attn_coefs, query_grad), _, (back, output_grad) = made
    total = own.astype(f32) + swap(other, "expert").astype(f32) + back.astype(f32)
    input_joined = for_tokens(total)
    scalars = jnp.stack([shard, local, local_at]).astype(jnp.int32)

    def weight_work(event):
        sums = after(key_sums, event)
        sums = sum(product_first(tree_blocks[t].reshape(length, -1), sums[t]) for t in range(2))
        return [sums[:width].astype(bf16).reshape(experts, width // experts, -1)]

    def shared_work(event):
        parts = shared_out(
            scalars, after(token_sums, event), key_weight, value_weight, got_key, got_value
        )
        theirs = parts[0].astype(f32) + swap(parts[2], "expert").astype(f32)
        shared = parts[1].astype(f32) + swap(parts[3], "expert").astype(f32)
        return [shared, swap(theirs.astype(bf16), "shard")]

    token_sums = key_sums.reshape(2, experts, part, -1).transpose(1, 0, 2, 3)
    (token_sums,), (weight_sums,) = pinned((to_experts(token_sums),), weight_work, token_sums)
    token_sums = join_parts(token_sums)
    input_joined = after(input_joined, token_sums)
    back = lax.all_to_all(input_joined, "dp", 0, 0, tiled=True)
    (back,), (shared, theirs) = pinned((back,), shared_work, input_joined)
    shared = shared + theirs.astype(f32)
    if members > 1:
        groups = [[e * members + m for m in range(members)] for e in range(experts)]
        shared = lax.psum_scatter(
            shared, "dp", scatter_dimension=0, axis_index_groups=groups, tiled=True
        )
    attn_n = my_half(inputs) * attn_scale
    features = width // (2 * blocks)

    def spread(values):
        return lax.dynamic_update_slice(jnp.zeros((1, width), f32), values[None], (0, shard * half))

    normed_grad = sum_tokens(back, attn_pack) + shared
    gain_part = jnp.sum(normed_grad * attn_n, axis=0)

    def last_work(event):
        grad = after(normed_grad, event)
        weighted = grad * my_half(attn_gain)
        grad = middle_grad + attn_scale * (weighted - attn_n * feature_mean(weighted * attn_n))
        return [grad, swap(grad.astype(bf16), "shard")]

    attn_router_part = product_first(attn_coefs, after(rows, key_sums).astype(f32))
    small = [attn_router_part, mlp_router_part, spread(gain_part), spread(mlp_gain_part)]
    small = jnp.pad(jnp.concatenate(small), ((0, 6), (0, 0)))
    small = small.reshape(-1, blocks, 2, features).transpose(1, 2, 0, 3)
    small = small.reshape(blocks, -1, features).astype(bf16)
    if members > 1:
        (weight_sums,), (tokens_grad, got) = pinned((to_experts(weight_sums),), last_work, small)
        small = lax.all_to_all(small, "dp", 0, 0, tiled=True)
    else:
        height = weight_sums.shape[1]
        both = jnp.concatenate([weight_sums, small], axis=1)
        (both,), (tokens_grad, got) = pinned((to_experts(both),), last_work, both)
        weight_sums, small = both[:, :height], both[:, height:]
    weight_sums = join_parts(weight_sums)
    small = jnp.sum(small.astype(f32), axis=0).reshape(2, -1, features)
    mine = lax.dynamic_index_in_dim(small, core, 0, keepdims=False)
    theirs = lax.dynamic_index_in_dim(small, 1 - core, 0, keepdims=False)
    small = mine + swap(theirs, "expert")
    small = small + swap(small, "shard")
    layer_out = whole((middle + sum_tokens(term_back, mlp_pack)).astype(bf16))[None]
    got = got.astype(f32)
    tokens_grad = jnp.concatenate(
        [jnp.where(shard == 0, tokens_grad, got), jnp.where(shard == 0, got, tokens_grad)], axis=1
    )[None]

    heads = piece // HEAD
    pieces = weight_sums.reshape(2 * heads, members, 2, features, HEAD).transpose(1, 2, 0, 3, 4)
    if members > 1:
        pieces = lax.all_to_all(pieces, "dp", 0, 0, axis_index_groups=groups, tiled=True)
    pieces = pair_all_to_all(pieces.transpose(1, 0, 2, 3, 4), "expert")
    pieces = pieces.transpose(1, 0, 2, 3, 4).reshape(2, members, 2 * heads, features, HEAD)
    pieces = pair_all_to_all(pieces, "shard").reshape(2, members, heads, 2, features, HEAD)
    pieces = pieces.transpose(3, 4, 1, 0, 2, 5).reshape(2, features, -1).astype(f32)

    return (
        layer_out,
        tokens_grad,
        small[2 * experts],
        small[2 * experts + 1],
        pieces[0],
        pieces[1],
        query_grad,
        output_grad,
        small[:experts].T,
        gate_grad,
        up_grad,
        down_grad,
        small[experts : 2 * experts].T,
    )


def solution(mesh):
    tree = P("expert", "dp", None)
    columns = P(None, ("dp", "expert", "shard"))
    spread = P(("dp", "expert"), None)
    in_specs = (
        tree,
        tree,
        P(),
        P(),
        P(None, "shard"),
        P(None, "shard"),
        columns,
        columns,
        P(),
        columns,
        columns,
        columns,
        P(),
        P("expert", None),
        P("expert", None),
        tree,
        tree,
        tree,
    )
    out_specs = (
        tree,
        tree,
        P(("dp", "expert")),
        P(("dp", "expert")),
        P(("dp", "expert"), "shard"),
        P(("dp", "expert"), "shard"),
        columns,
        columns,
        spread,
        columns,
        columns,
        columns,
        spread,
    )
    return jax.shard_map(
        per_device, mesh=mesh, in_specs=in_specs, out_specs=out_specs, check_vma=False
    )
```
